128 devices in a mesh: dp: 8 (over z_lo, x), mp: 16 (over y, z_hi, core).
Axes of the slice: x: 4, y: 4, z: 4 (z_hi: 2, z_lo: 2; z = z_hi * 2 + z_lo), core: 2. Of those that a mesh axis runs over, the one named last changes fastest.
Arguments:
- hidden_rows: bfloat16 [512, 16384], P('dp', 'mp'), may hold values from -60 to 60
- head_weight: bfloat16 [16384, 16, 8, 128], P('mp', None, 'dp'), may hold values from -0.046875 to 0.046875
- norm_gain: float32 [16, 8, 128], P('mp', 'dp'), may hold values from 0.1 to 1.9
- vocab_embed: bfloat16 [65536, 16, 8, 128], P('mp', None, 'dp'), may hold values from -6 to 6
- targets: int32 [512], replicated, may hold values from 0 to 65535
Outputs:
- weight_grad: bfloat16 [16384, 16, 8, 128], P('mp', None, 'dp')
- loss: float32 [], replicated
The draws below stay inside these ranges and needn't reach their ends.
All inputs are finite; a program needn't handle non-finite values.
Results may differ from the reference program's by a relative error of at most 0.0046.
Values may be sent and summed in bfloat16 or wider, within the bound.
A program may use at most 128 MiB of HBM per device.

```python
import math
import jax
import jax.numpy as jnp
from jax import lax

D = 16384
TOKENS = 512
VOCAB = 65536
FB = 128
N_DP = 8
N_MP = 16


def shared_patterns(key):
    base = jax.random.fold_in(key, 101)
    first, second, third, fourth = jax.random.split(base, 4)
    patterns = jax.random.uniform(first, (2, D), jnp.float32, -1.732, 1.732)
    token_rows = jax.random.permutation(second, TOKENS)[:2]
    vocab_rows = jax.random.permutation(third, VOCAB)[:4]
    common = jax.random.uniform(fourth, (D,), jnp.float32, -1.732, 1.732)
    return (patterns, token_rows, vocab_rows, common)


def draw_hidden_rows(key, part):
    patterns, token_rows, vocab_rows, common = shared_patterns(key)
    key = jax.random.fold_in(key, 11)
    first, second, third = jax.random.split(key, 3)
    rising = jnp.exp(math.log(3.0) * jnp.arange(D, dtype=jnp.float32) / (D - 1))
    rough = jnp.exp(jax.random.uniform(second, (D,), jnp.float32, -0.69, 0.69))
    scales = jnp.exp(jax.random.uniform(third, (TOKENS, 1), jnp.float32, -0.69, 0.69))
    position = jnp.arange(TOKENS, dtype=jnp.float32) / (TOKENS - 1)
    base = jnp.clip(jax.random.normal(first, (TOKENS, D), jnp.float32), -4.0, 4.0)
    mixing = 0.9 * position
    rows = base * rising[None, :] * rough[None, :] * scales
    rows = rows * (1.0 - mixing)[:, None] + (2.0 * mixing)[:, None] * common[None, :]
    strength = jnp.array([1.5, 1.0], jnp.float32)[:, None]
    rows = rows.at[token_rows].set(strength * patterns)
    return rows.astype(jnp.bfloat16)


def draw_vocab_embed(key, part):
    patterns, token_rows, vocab_rows, common = shared_patterns(key)
    key = jax.random.fold_in(key, 23)
    first, second, third = jax.random.split(key, 3)
    scales = jnp.exp(jax.random.uniform(second, (VOCAB, 1), jnp.float32, 0.0, math.log(10.0))) * (0.2 / math.sqrt(D))
    base = jnp.clip(jax.random.normal(first, (VOCAB, D), jnp.float32), -4.0, 4.0) * scales
    coefficient = jnp.clip(jax.random.normal(third, (VOCAB, 1), jnp.float32), -3.0, 3.0)
    base = base + coefficient * (1.5 / D) * common[None, :]
    strength = jnp.array([150.0, 152.0, 340.0, 344.0], jnp.float32)[:, None] / D
    chosen = jnp.stack([patterns[0], patterns[0], patterns[1], patterns[1]], axis=0)
    base = base.at[vocab_rows].set(strength * chosen)
    return base.reshape(VOCAB, N_MP, N_DP, D // (N_MP * N_DP)).astype(jnp.bfloat16)


def with_ends(values, own_key, least, high):
    longest = values.shape.index(max(values.shape))
    spots = []
    for shift in (0, 1):
        where = [jax.random.randint(jax.random.fold_in(own_key, axis), (), 0, length) for axis, length in enumerate(values.shape)]
        where[longest] = (where[longest] + shift) % values.shape[longest]
        spots.append(tuple(where))
    return values.at[spots[0]].set(least).at[spots[1]].set(high)


def shard_levels(key, shape, shards, low, high):
    loudness = 1.0
    for dim, blocks in shards:
        heights = jax.random.uniform(jax.random.fold_in(jax.random.fold_in(key, 6), dim), (blocks,), jnp.float32, low / len(shards), high / len(shards))
        loudness = loudness * jnp.repeat(jnp.exp(heights), shape[dim] // blocks).reshape((-1,) + (1,) * (len(shape) - 1 - dim))
    return loudness


def centred(own_key, extent, deviation, reach, cuts=(), kind=jnp.bfloat16):
    loudness = shard_levels(own_key, extent, cuts, -0.22, 0.18) if cuts else 1.0
    values = jax.random.normal(own_key, extent, jnp.float32) * deviation * loudness
    return jnp.minimum(jnp.maximum(values, -reach), reach).astype(kind)


def setup_inputs(seed: int = 0) -> dict:
    key_list = jax.random.split(jax.random.key(seed), 6)
    hidden_rows = draw_hidden_rows(jax.random.fold_in(key_list[5], 71), 0)
    head_weight = centred(key_list[1], (D, N_MP, N_DP, FB), D ** -0.5, 0.046875, ((0, 16), (2, 8)))
    norm_gain = jnp.clip(1.0 + 0.18 * jax.random.normal(key_list[2], (N_MP, N_DP, FB), jnp.float32), 0.1, 1.9)
    vocab_embed = draw_vocab_embed(jax.random.fold_in(key_list[5], 71), 0)
    targets = with_ends(jax.random.randint(key_list[4], (TOKENS,), 0, VOCAB), jax.random.fold_in(key_list[4], 1), 0, VOCAB - 1).astype(jnp.int32)
    return {"hidden_rows": hidden_rows, "head_weight": head_weight, "norm_gain": norm_gain, "vocab_embed": vocab_embed, "targets": targets}


def reference(hidden_rows, head_weight, norm_gain, vocab_embed, targets):
    width = hidden_rows.shape[1]
    weight = head_weight.reshape(width, width)
    gain = norm_gain.reshape(width)
    embed = vocab_embed.reshape(vocab_embed.shape[0], width)
    count = hidden_rows.shape[0]
    pre = jnp.dot(hidden_rows, weight, preferred_element_type=jnp.float32)
    act = hidden_rows.astype(jnp.float32) + jax.nn.silu(pre)
    inv = lax.rsqrt(lax.optimization_barrier(jnp.mean(act * act, axis=1)) + 1e-05)
    normed = (act * inv[:, None] * gain[None, :]).astype(jnp.bfloat16)
    logits = jnp.dot(normed, embed.T, preferred_element_type=jnp.float32)
    top = lax.optimization_barrier(jnp.max(logits, axis=1))
    lse = top + jnp.log(lax.optimization_barrier(jnp.sum(jnp.exp(logits - top[:, None]), axis=1)))
    hit = lax.broadcasted_iota(jnp.int32, logits.shape, 1) == targets[:, None]
    picked = lax.optimization_barrier(jnp.sum(jnp.where(hit, logits, 0.0), axis=1))
    loss = jnp.sum(lse - picked) / count
    dlogits = ((jnp.exp(logits - lse[:, None]) - hit.astype(jnp.float32)) / count).astype(jnp.bfloat16)
    dnormed = jnp.dot(dlogits, embed, preferred_element_type=jnp.float32)
    scaled = gain[None, :] * dnormed
    inner = lax.optimization_barrier(jnp.mean(act * scaled, axis=1))
    dact = inv[:, None] * scaled - act * (inv * inv * inv * inner)[:, None]
    sig = jax.nn.sigmoid(pre)
    dpre = (dact * sig * (1.0 + pre * (1.0 - sig))).astype(jnp.bfloat16)
    grad = jnp.dot(hidden_rows.T, dpre, preferred_element_type=jnp.float32).astype(jnp.bfloat16)
    return (grad.reshape(head_weight.shape), loss)
```

```python
import jax
import jax.numpy as jnp
from jax import lax
from jax.experimental import pallas as pl
from jax.experimental.pallas import tpu as pltpu
from jax.sharding import PartitionSpec as P

MESH = pl.DeviceIdType.MESH
BF = jnp.bfloat16
F32 = jnp.float32
T, D, V, FB = 512, 16384, 4096, 128
CH = 1024
HALF = 512
NCH = V // CH
ROWS = 256
NT = (((1,), (1,)), ((), ()))
NN = (((1,), (0,)), ((), ()))


def dot(a, b, dims):
    return lax.dot_general(a, b, dims, preferred_element_type=F32)


def head_kernel(
    hid_ref, w_ref, gain_ref, e_ref, tgt_ref,
    dpf, hid_t, loss_ref,
    e_flat, w_flat, stage, hid_all, ps, core_in, ps2, mp_in, core_in2, mp_in2,
    pre_s, act_s, nb, nf, sq_own, sq_in, sq_sum, sq_in2, inv_s,
    lz, lx, rx, rz, sx2, rx2, sz2, rz2, lg, tsq, st_own, st_in, sc_all, dl,
    stage_sem, hid_ss, hid_rs, core_ss, core_rs, mp_ss, mp_rs, core2_ss, core2_rs, mp2_ss, mp2_rs,
    nf_ss, nf_rs, nfc_ss, nfc_rs, dp_ss, dp_rs, dpc_ss, dpc_rs,
    sq_ss, sq_rs, sq2_ss, sq2_rs, st_ss, st_rs, sc_ss, sc_rs,
    rx_ss, rx_rs, rz_ss, rz_rs, rx2_ss, rx2_rs, rz2_ss, rz2_rs,
    az_ss, az_rs, azz_ss, azz_rs, ax_ss, ax_rs, axf_ss, axf_rs, azf_ss, azf_rs, axz_ss, axz_rs,
):
    dp = lax.axis_index("dp")
    mp = lax.axis_index("mp")
    x, zl = lax.rem(dp, 4), dp // 4
    yz, c = mp // 2, lax.rem(mp, 2)
    y, zh = yz // 2, lax.rem(yz, 2)
    pos = x * 2 + zl

    def at_dp(dx, dz):
        return (lax.rem(zl + dz, 2) * 4 + lax.rem(x + dx, 4), mp)

    def at_mp(k, dc=0):
        return (dp, yz_of(k) * 2 + lax.rem(c + dc, 2))

    def yz_of(k):
        return lax.rem(y + k // 2, 4) * 2 + lax.rem(zh + k % 2, 2)

    def yz_from(k):
        return lax.rem(y + 4 - k // 2, 4) * 2 + lax.rem(zh + k % 2, 2)

    zpeer = at_dp(0, 1)
    sibling = at_mp(0, 1)
    dp_offs = [(k % 4, k // 4) for k in (6, 2, 5, 7, 1, 3, 4)]
    mp_offs = [5, 4, 3, 7, 2, 6, 1]
    mp15 = [(k, 1) for k in [*mp_offs, 0]] + [(k, 0) for k in mp_offs]

    def rc(src, dst, ss, rs, dev):
        return pltpu.make_async_remote_copy(
            src_ref=src, dst_ref=dst, send_sem=ss, recv_sem=rs, device_id=dev, device_id_type=MESH
        )

    def load_w(i):
        return pltpu.make_async_copy(w_ref.at[pl.ds(i * ROWS, ROWS)], stage.at[i], stage_sem.at[i])

    def load_e(i):
        slot = lax.rem(i, 4)
        return pltpu.make_async_copy(
            e_ref.at[pl.ds(i * ROWS, ROWS)], stage.at[slot], stage_sem.at[slot]
        )

    for i in range(4):
        load_w(i).start()

    barrier = pltpu.get_barrier_semaphore()
    for o in dp_offs:
        pl.semaphore_signal(barrier, inc=1, device_id=at_dp(*o), device_id_type=MESH)
    for k, dc in mp15:
        pl.semaphore_signal(barrier, inc=1, device_id=at_mp(k, dc), device_id_type=MESH)
    pl.semaphore_wait(barrier, len(dp_offs) + len(mp15))

    def send_hid(q):
        return rc(
            hid_ref, hid_all.at[pl.ds(pos * 64, 64)], hid_ss.at[q], hid_rs.at[q], at_dp(*dp_offs[q])
        )

    for q in range(7):
        send_hid(q).start()
    hid_all[pl.ds(pos * 64, 64), :] = hid_ref[...]

    def relay(slot, out, first):
        def body(i, carry):
            r = pltpu.einshape("vjl->jvl", stage[slot, pl.ds(pl.multiple_of(i * 64, 64), 64)])
            s = pl.multiple_of(first + i * 64, 64)
            for j in range(16):
                at = ((j % 2) * 8 + j // 2) * FB
                out[pl.ds(s, 64), at : at + FB] = r[j]
            return carry

        lax.fori_loop(0, ROWS // 64, body, 0)

    for i in range(4):
        load_w(i).wait()
        relay(i, w_flat, i * ROWS)
        load_e(i).start()

    for q in range(7):
        send_hid(q).wait_recv()

    def core_copy(buf, ss, rs, t):
        return rc(
            ps.at[1 - c, pl.ds(t * 2, 2)], buf.at[pl.ds(t * 2, 2)], ss.at[t], rs.at[t], sibling
        )

    def mp_copy(buf, ss, rs, k):
        return rc(ps2.at[yz_of(k)], buf.at[k], ss.at[k], rs.at[k], at_mp(k))

    def product(lhs, weight, cbuf, css, crs):
        for side in (1, 0):
            who = lax.rem(c + side, 2)

            def body(t, carry, who=who, side=side):
                col = pl.multiple_of(who * 1024 + t * 256, 256)
                r = dot(lhs[...], weight[:, pl.ds(col, 256)], NN).astype(BF)
                ps[who, t * 2] = r[:, :FB]
                ps[who, t * 2 + 1] = r[:, FB:]
                if side:
                    core_copy(cbuf, css, crs, t).start()
                return carry

            lax.fori_loop(0, 4, body, 0)

    def exchange(cbuf, css, crs, mbuf, mss, mrs):
        for t in range(4):
            core_copy(cbuf, css, crs, t).wait_recv()
        for k in [*mp_offs, 0]:
            b = yz_of(k)
            ps2[b] = (ps[c, b].astype(F32) + cbuf[b].astype(F32)).astype(BF)
            if k:
                mp_copy(mbuf, mss, mrs, k).start()

    def collect(cbuf, css, crs, mbuf, mss, mrs):
        total = ps[c, yz].astype(F32) + cbuf[yz].astype(F32)
        for k in mp_offs:
            mp_copy(mbuf, mss, mrs, k).wait_recv()
            total = total + mbuf[k].astype(F32)
        for k in mp_offs:
            mp_copy(mbuf, mss, mrs, k).wait_send()
        for t in range(4):
            core_copy(cbuf, css, crs, t).wait_send()
        return total

    product(hid_all, w_flat, core_in, core_ss, core_rs)
    exchange(core_in, core_ss, core_rs, mp_in, mp_ss, mp_rs)

    def relay_e(i, carry):
        load_e(i).wait()
        relay(lax.rem(i, 4), e_flat, i * ROWS)

        @pl.when(i + 4 < V // ROWS)
        def _():
            load_e(i + 4).start()

        return carry

    lax.fori_loop(0, V // ROWS, relay_e, 0)
    for i in range(8):
        hid_t[i * FB : (i + 1) * FB, :] = hid_all[:, i * FB : (i + 1) * FB].T

    pre = collect(core_in, core_ss, core_rs, mp_in, mp_ss, mp_rs)
    pre_s[...] = pre
    own = hid_all[:, pl.ds(pl.multiple_of(dp * FB, FB), FB)].astype(F32)
    act = own + pre / (1.0 + jnp.exp(-pre))
    act_s[...] = act
    gain = gain_ref[...]
    nb[...] = (act * gain).astype(BF)

    def cols(buf, core, b):
        return buf.at[:, pl.ds(pl.multiple_of((core * 8 + b) * FB, FB), FB)]

    def ag_copy(buf, ss, rs, k):
        return rc(nb, cols(buf, c, yz), ss.at[k], rs.at[k], at_mp(k))

    def ag_pass(buf, ss, rs, k):
        at = cols(buf, c, yz_from(k))
        return rc(nb if k == 0 else at, at, ss.at[k], rs.at[k], sibling)

    def gather_start(buf, ss, rs, css, crs):
        for k in mp_offs:
            ag_copy(buf, ss, rs, k).start()
        ag_pass(buf, css, crs, 0).start()
        buf[:, pl.ds(pl.multiple_of((c * 8 + yz) * FB, FB), FB)] = nb[...]

    def gather_end(buf, ss, rs, css, crs):
        for k in reversed(mp_offs):
            ag_copy(buf, ss, rs, k).wait_recv()
            ag_pass(buf, css, crs, k).start()
        for k in range(8):
            ag_pass(buf, css, crs, k).wait_recv()
        for k in range(8):
            ag_pass(buf, css, crs, k).wait_send()
        for k in mp_offs:
            ag_copy(buf, ss, rs, k).wait_send()

    gather_start(nf, nf_ss, nf_rs, nfc_ss, nfc_rs)

    def send_sq(q):
        k, dc = mp15[q]
        return rc(sq_own, sq_in.at[mp], sq_ss.at[q], sq_rs.at[q], at_mp(k, dc))

    squares = act * act
    for i in range(4):
        row = jnp.sum(squares[i * FB : (i + 1) * FB, :].T, axis=0, keepdims=True)
        sq_own[:, i * FB : (i + 1) * FB] = jnp.broadcast_to(row, (8, FB))
    for q in range(15):
        send_sq(q).start()
    sq_in[mp] = sq_own[...]

    gather_end(nf, nf_ss, nf_rs, nfc_ss, nfc_rs)

    def send_sq2(q):
        return rc(sq_sum, sq_in2.at[dp], sq2_ss.at[q], sq2_rs.at[q], at_dp(*dp_offs[q]))

    for q in range(15):
        send_sq(q).wait_recv()
    sq_sum[...] = jnp.sum(sq_in[...], axis=0)
    for q in range(7):
        send_sq2(q).start()
    sq_in2[dp] = sq_sum[...]

    def rows_of(xx, zz):
        return pl.ds(pl.multiple_of((xx * 2 + zz) * 64, 64), 64)

    def xd(d):
        return lax.rem(x + d, 4)

    def rz_copy(i, d):
        return rc(
            lz.at[i, rows_of(xd(d), 1 - zl)], rz.at[i, d], rz_ss.at[i, d], rz_rs.at[i, d], zpeer
        )

    def rx_copy(i, d):
        src = lx.at[i, pl.ds(pl.multiple_of(xd(d) * 128, 128), 128)]
        return rc(src, rx.at[i, d - 1], rx_ss.at[i, d - 1], rx_rs.at[i, d - 1], at_dp(d, 0))

    def rx2_copy(i):
        return rc(sx2.at[i], rx2.at[i], rx2_ss.at[i], rx2_rs.at[i], zpeer)

    def rz2_copy(i, d):
        return rc(
            sz2.at[i, d - 1], rz2.at[i, d - 1], rz2_ss.at[i, d - 1], rz2_rs.at[i, d - 1], at_dp(d, 0)
        )

    def zcol(i):
        return pl.ds(pl.multiple_of(i * CH, CH), HALF)

    def xcol(i):
        return pl.ds(pl.multiple_of(i * CH + HALF, HALF), HALF)

    def logits_chunk(i):
        at = pl.multiple_of(i * CH, CH)
        lz[i] = dot(nf[...], e_flat[pl.ds(at, HALF), :], NT).astype(BF)
        for d in (2, 1, 3, 0):
            rz_copy(i, d).start()
        lx[i] = dot(nf[...], e_flat[pl.ds(at + HALF, HALF), :], NT).astype(BF)
        for d in (2, 1, 3):
            rx_copy(i, d).start()

    def second_step(i):
        for d in (1, 3, 2):
            rx_copy(i, d).wait_recv()
        base = pl.multiple_of(x * 128, 128)
        for mine in (False, True):
            zz = zl if mine else 1 - zl
            off = pl.multiple_of(zz * 64, 64)
            s = lx[i, pl.ds(base + off, 64)].astype(F32)
            for d in range(3):
                s = s + rx[i, d, pl.ds(off, 64)].astype(F32)
            if mine:
                lg[:, xcol(i)] = s
            else:
                sx2[i] = s.astype(BF)
                rx2_copy(i).start()
        for d in (2, 1, 3, 0):
            rz_copy(i, d).wait_recv()
            s = lz[i, rows_of(xd(d), zl)].astype(F32) + rz[i, d].astype(F32)
            if d:
                sz2[i, d - 1] = s.astype(BF)
                rz2_copy(i, d).start()
            else:
                lg[:, zcol(i)] = s

    def rs_loop(i, carry):
        @pl.when(i < NCH)
        def _():
            logits_chunk(i)

        @pl.when(i > 0)
        def _():
            second_step(i - 1)

        return carry

    lax.fori_loop(0, NCH + 1, rs_loop, 0)

    for q in range(7):
        send_sq2(q).wait_recv()
    mean = jnp.sum(sq_in2[...], axis=0)[:1, :] / D
    inv_row = lax.rsqrt(mean + 1e-05)
    for i in range(4):
        part = jnp.broadcast_to(inv_row[:, i * FB : (i + 1) * FB], (FB, FB))
        inv_s[i * FB : (i + 1) * FB, :] = part.T

    def rs_end(i, carry):
        rx2_copy(i).wait_recv()
        lg[:, xcol(i)] = lg[:, xcol(i)] + rx2[i].astype(F32)
        s = lg[:, zcol(i)]
        for d in (1, 3, 2):
            rz2_copy(i, d).wait_recv()
            s = s + rz2[i, d - 1].astype(F32)
        lg[:, zcol(i)] = s
        return carry

    lax.fori_loop(0, NCH, rs_end, 0)

    my_rows = pl.ds(pl.multiple_of(pos * 64, 64), 64)
    inv_own = inv_s[my_rows, :][:, :1]
    lane = lax.broadcasted_iota(jnp.int32, (64, FB), 1)
    tgt = tgt_ref[...][:, :1]

    def scaled(i):
        at = pl.ds(pl.multiple_of(i * HALF, HALF), HALF)
        return lg[:, at], lax.broadcasted_iota(jnp.int32, (64, HALF), 1) + i * HALF

    def max_body(i, m):
        at = pl.ds(pl.multiple_of(i * HALF, HALF), HALF)
        v = lg[:, at] * inv_own
        lg[:, at] = v
        return jnp.maximum(m, jnp.max(v, axis=1, keepdims=True))

    m = lax.fori_loop(0, V // HALF, max_body, jnp.full((64, 1), -jnp.inf, F32))

    def sum_body(i, carry):
        s, sl, pk = carry
        v, ids = scaled(i)
        p = jnp.exp(v - m)
        s = s + jnp.sum(p, axis=1, keepdims=True)
        sl = sl + jnp.sum(p * v, axis=1, keepdims=True)
        pk = pk + jnp.sum(jnp.where(ids == tgt, v, 0.0), axis=1, keepdims=True)
        return s, sl, pk

    zero = jnp.zeros((64, 1), F32)
    s, sl, pk = lax.fori_loop(0, V // HALF, sum_body, (zero, zero, zero))
    tsq[...] = jnp.zeros((FB, FB), F32)
    tsq[:64, :] = jnp.where(
        lane == 0, m, jnp.where(lane == 1, s, jnp.where(lane == 2, sl, jnp.where(lane == 3, pk, 0.0)))
    )
    st_own[...] = tsq[...].T[:8, :]

    def send_st(q):
        k, dc = mp15[q]
        return rc(st_own, st_in.at[mp], st_ss.at[q], st_rs.at[q], at_mp(k, dc))

    for q in range(15):
        send_st(q).start()
    st_in[mp] = st_own[...]
    for q in range(15):
        send_st(q).wait_recv()
    all_m = st_in[:, 0, :]
    top = jnp.max(all_m, axis=0, keepdims=True)
    scale = jnp.exp(all_m - top)
    total = jnp.sum(st_in[:, 1, :] * scale, axis=0, keepdims=True)
    total_l = jnp.sum(st_in[:, 2, :] * scale, axis=0, keepdims=True)
    picked = jnp.sum(st_in[:, 3, :], axis=0, keepdims=True)
    valid = lax.broadcasted_iota(jnp.int32, (1, FB), 1) < 64
    total = jnp.where(valid, total, 1.0)
    lse = top + jnp.log(total)
    moment = (total_l / total - picked) / T
    sub = lax.broadcasted_iota(jnp.int32, (FB, FB), 0)
    table = jnp.where(sub == 0, lse, jnp.where(sub == 1, moment, jnp.where(sub == 2, lse - picked, 0.0)))
    tsq[...] = table.T
    sc_all[pos] = tsq[:64, :]

    def send_sc(q):
        return rc(sc_all.at[pos], sc_all.at[pos], sc_ss.at[q], sc_rs.at[q], at_dp(*dp_offs[q]))

    for q in range(7):
        send_sc(q).start()
    lse_col = tsq[:64, :][:, :1]

    def dl_at(xx, zz, col):
        return dl.at[rows_of(xx, zz), col]

    def az_copy(i, d):
        a = dl_at(x, zl, zcol(i))
        return rc(a, a, az_ss.at[i, d - 1], az_rs.at[i, d - 1], at_dp(d, 0))

    def azz_copy(i):
        a = dl_at(x, zl, zcol(i))
        return rc(a, a, azz_ss.at[i], azz_rs.at[i], zpeer)

    def azf_copy(i, d):
        a = dl_at(lax.rem(x + 4 - d, 4), zl, zcol(i))
        return rc(a, a, azf_ss.at[i, d - 1], azf_rs.at[i, d - 1], zpeer)

    def ax_copy(i, d):
        a = dl_at(x, zl, xcol(i))
        return rc(a, a, ax_ss.at[i, d - 1], ax_rs.at[i, d - 1], at_dp(d, 0))

    def axz_copy(i):
        a = dl_at(x, zl, xcol(i))
        return rc(a, a, axz_ss.at[i], axz_rs.at[i], zpeer)

    def axf_copy(i, d):
        a = dl_at(x, 1 - zl, xcol(i))
        return rc(a, a, axf_ss.at[i, d - 1], axf_rs.at[i, d - 1], at_dp(d, 0))

    def dl_body(i, carry):
        for h in (0, 1):
            v, ids = scaled(2 * i + h)
            p = jnp.exp(v - lse_col)
            at = pl.ds(pl.multiple_of(i * CH + h * HALF, HALF), HALF)
            dl[my_rows, at] = ((p - (ids == tgt).astype(F32)) / T).astype(BF)
            if h:
                axz_copy(i).start()
                for d in (2, 1, 3):
                    ax_copy(i, d).start()
            else:
                for d in (2, 1, 3):
                    az_copy(i, d).start()
                azz_copy(i).start()
        return carry

    lax.fori_loop(0, NCH, dl_body, 0)

    def fwd_body(i, carry):
        axz_copy(i).wait_recv()
        for d in (2, 1, 3):
            axf_copy(i, d).start()
        for d in (1, 3, 2):
            az_copy(i, d).wait_recv()
            azf_copy(i, d).start()
        return carry

    lax.fori_loop(0, NCH, fwd_body, 0)

    def ag_end(i, carry):
        azz_copy(i).wait_recv()
        for d in (1, 3, 2):
            ax_copy(i, d).wait_recv()
            axf_copy(i, d).wait_recv()
            azf_copy(i, d).wait_recv()
        return carry

    lax.fori_loop(0, NCH, ag_end, 0)

    product(dl, e_flat, core_in2, core2_ss, core2_rs)
    exchange(core_in2, core2_ss, core2_rs, mp_in2, mp2_ss, mp2_rs)
    for q in range(7):
        send_sc(q).wait_recv()
    loss = jnp.zeros((64, 1), F32)
    for b in range(8):
        loss = loss + sc_all[b][:, 2:3]
    loss_ref[...] = jnp.broadcast_to(jnp.sum(loss, axis=0, keepdims=True) / T, (8, FB))
    dnormed = collect(core_in2, core2_ss, core2_rs, mp_in2, mp2_ss, mp2_rs)
    moments = jnp.concatenate([sc_all[b][:, 1:2] for b in range(8)], axis=0)
    inv = inv_s[...]
    act = act_s[...]
    pre = pre_s[...]
    dact = inv * gain * dnormed - act * (inv * inv * (moments / D))
    sig = 1.0 / (1.0 + jnp.exp(-pre))
    nb[...] = (dact * sig * (1.0 + pre * (1.0 - sig))).astype(BF)
    gather_start(dpf, dp_ss, dp_rs, dpc_ss, dpc_rs)
    gather_end(dpf, dp_ss, dp_rs, dpc_ss, dpc_rs)

    for q in range(7):
        send_hid(q).wait_send()
        send_sq2(q).wait_send()
        send_sc(q).wait_send()
    for q in range(15):
        send_sq(q).wait_send()
        send_st(q).wait_send()

    def drain(i, carry):
        rx2_copy(i).wait_send()
        azz_copy(i).wait_send()
        axz_copy(i).wait_send()
        for d in range(4):
            rz_copy(i, d).wait_send()
        for d in (1, 2, 3):
            rx_copy(i, d).wait_send()
            rz2_copy(i, d).wait_send()
            az_copy(i, d).wait_send()
            azf_copy(i, d).wait_send()
            ax_copy(i, d).wait_send()
            axf_copy(i, d).wait_send()
        return carry

    lax.fori_loop(0, NCH, drain, 0)


def head(hidden, weight, gain, embed, tgt):
    vm = pltpu.VMEM
    dma = pltpu.SemaphoreType.DMA
    scratch = [
        vm((V, 2048), BF), vm((1024, 2048), BF), vm((4, ROWS, 16, FB), BF), vm((T, 1024), BF),
        vm((2, 8, T, FB), BF), vm((8, T, FB), BF), vm((8, T, FB), BF), vm((8, T, FB), BF),
        vm((8, T, FB), BF), vm((8, T, FB), BF),
        vm((T, FB), F32), vm((T, FB), F32), vm((T, FB), BF), vm((T, 2048), BF),
        vm((8, T), F32), vm((16, 8, T), F32), vm((8, T), F32), vm((8, 8, T), F32), vm((T, FB), F32),
        vm((NCH, T, HALF), BF), vm((NCH, T, HALF), BF),
        vm((NCH, 3, 128, HALF), BF), vm((NCH, 4, 64, HALF), BF),
        vm((NCH, 64, HALF), BF), vm((NCH, 64, HALF), BF), vm((NCH, 3, 64, HALF), BF), vm((NCH, 3, 64, HALF), BF),
        vm((64, V), F32), vm((FB, FB), F32), vm((8, FB), F32), vm((16, 8, FB), F32),
        vm((8, 64, FB), F32), vm((T, V), BF),
        dma((4,)),
    ]
    counts = [
        (7,), (4,), (8,), (4,), (8,), (8,), (8,), (8,), (8,), (15,), (7,), (15,), (7,),
        (NCH, 3), (NCH, 4), (NCH,), (NCH, 3),
        (NCH, 3), (NCH,), (NCH, 3), (NCH, 3), (NCH, 3), (NCH,),
    ]
    for n in counts:
        scratch += [dma(n), dma(n)]
    vspec = pl.BlockSpec(memory_space=pltpu.VMEM)
    anyspec = pl.BlockSpec(memory_space=pl.ANY)
    return pl.pallas_call(
        head_kernel,
        name="head",
        out_shape=(
            jax.ShapeDtypeStruct((T, 2048), BF),
            jax.ShapeDtypeStruct((1024, T), BF),
            jax.ShapeDtypeStruct((8, FB), F32),
        ),
        in_specs=[vspec, anyspec, vspec, anyspec, vspec],
        out_specs=(vspec, vspec, vspec),
        scratch_shapes=scratch,
        compiler_params=pltpu.CompilerParams(
            collective_id=0, has_side_effects=True, vmem_limit_bytes=62 << 20
        ),
    )(hidden, weight, gain, embed, tgt)


def grad_kernel(hid_t, dpf, out):
    r = dot(hid_t[...], dpf[...], NN).astype(BF)
    for j in range(16):
        at = ((j % 2) * 8 + j // 2) * FB
        out[:, j, :] = r[:, at : at + FB]


def weight_gradient(hid_t, dpf):
    rows = 128
    return pl.pallas_call(
        grad_kernel,
        name="weight_gradient",
        grid=(1024 // rows,),
        out_shape=jax.ShapeDtypeStruct((1024, 16, FB), BF),
        in_specs=[
            pl.BlockSpec((rows, T), lambda i: (i, 0)),
            pl.BlockSpec((T, 2048), lambda i: (0, 0)),
        ],
        out_specs=pl.BlockSpec((rows, 16, FB), lambda i: (i, 0, 0)),
        compiler_params=pltpu.CompilerParams(vmem_limit_bytes=32 << 20),
    )(hid_t, dpf)


def on_device(hidden_rows, head_weight, norm_gain, vocab_embed, targets):
    dp = lax.axis_index("dp")
    mp = lax.axis_index("mp")
    mine = lax.dynamic_slice_in_dim(targets, dp * 64, 64, 0) - mp * V
    dpf, hid_t, loss = head(
        hidden_rows,
        head_weight.reshape(1024, 16, FB),
        norm_gain.reshape(1, FB),
        vocab_embed.reshape(V, 16, FB),
        jnp.broadcast_to(mine[:, None], (64, FB)),
    )
    grad = weight_gradient(hid_t, dpf)
    return grad.reshape(head_weight.shape), loss[0, 0]


def solution(mesh):
    return jax.shard_map(
        on_device,
        mesh=mesh,
        in_specs=(
            P("dp", "mp"),
            P("mp", None, "dp", None),
            P("mp", "dp", None),
            P("mp", None, "dp", None),
            P(),
        ),
        out_specs=(P("mp", None, "dp", None), P()),
        check_vma=False,
    )
```

```python
import jax
import jax.numpy as jnp
from jax import lax
from jax.experimental import pallas as pl
from jax.experimental.pallas import tpu as pltpu
from jax.sharding import PartitionSpec as P

MESH = pl.DeviceIdType.MESH
BF = jnp.bfloat16
F32 = jnp.float32
T, D, V, FB = 512, 16384, 4096, 128
CH = 1024
HALF = 512
NCH = V // CH
ROWS = 256
CODE = 32000.0
PRE_BOUND = 60.0 * 0.046875 * 2048 * 1.01
GRAD_BOUND = 6.0 * 2 / T * 1.01
NT = (((1,), (1,)), ((), ()))
NN = (((1,), (0,)), ((), ()))


def dot(a, b, dims):
    return lax.dot_general(a, b, dims, preferred_element_type=F32)


def head_kernel(
    hid_ref, w_ref, gain_ref, e_ref, tgt_ref, all_tgt_ref,
    dpf, hid_t, loss_ref,
    e_flat, w_flat, stage, hid_all, ps, acc, core_in, ps2, mp_in, oh, ct,
    pre_s, act_s, nb, nf, sq_own, sq_in, sq_sum, sq_in2, inv_s,
    lz, lx, rx, rz, sx2, rx2, sz2, rz2, lg, tsq, st_own, st_in, sc_all, dl,
    stage_sem, hid_ss, hid_rs, core_ss, core_rs, mp_ss, mp_rs, core2_ss, core2_rs, mp2_ss, mp2_rs,
    nf_ss, nf_rs, nfc_ss, nfc_rs, dp_ss, dp_rs, dpc_ss, dpc_rs,
    sq_ss, sq_rs, sq2_ss, sq2_rs, st_ss, st_rs, sc_ss, sc_rs,
    rx_ss, rx_rs, rz_ss, rz_rs, rx2_ss, rx2_rs, rz2_ss, rz2_rs,
    az_ss, az_rs, azz_ss, azz_rs, ax_ss, ax_rs, axf_ss, axf_rs, azf_ss, azf_rs, axz_ss, axz_rs,
):
    dp = lax.axis_index("dp")
    mp = lax.axis_index("mp")
    x, zl = lax.rem(dp, 4), dp // 4
    yz, c = mp // 2, lax.rem(mp, 2)
    y, zh = yz // 2, lax.rem(yz, 2)
    pos = x * 2 + zl

    def at_dp(dx, dz):
        return (lax.rem(zl + dz, 2) * 4 + lax.rem(x + dx, 4), mp)

    def at_mp(k, dc=0):
        return (dp, yz_of(k) * 2 + lax.rem(c + dc, 2))

    def yz_of(k):
        return lax.rem(y + k // 2, 4) * 2 + lax.rem(zh + k % 2, 2)

    def yz_from(k):
        return lax.rem(y + 4 - k // 2, 4) * 2 + lax.rem(zh + k % 2, 2)

    zpeer = at_dp(0, 1)
    sibling = at_mp(0, 1)
    dp_offs = [(k % 4, k // 4) for k in (6, 2, 5, 7, 1, 3, 4)]
    mp_offs = [5, 4, 3, 7, 2, 6, 1]
    mp15 = [(k, 1) for k in [*mp_offs, 0]] + [(k, 0) for k in mp_offs]

    def rc(src, dst, ss, rs, dev):
        return pltpu.make_async_remote_copy(
            src_ref=src, dst_ref=dst, send_sem=ss, recv_sem=rs, device_id=dev, device_id_type=MESH
        )

    def load_w(i):
        return pltpu.make_async_copy(w_ref.at[pl.ds(i * ROWS, ROWS)], stage.at[i], stage_sem.at[i])

    def load_e(i):
        slot = lax.rem(i, 4)
        return pltpu.make_async_copy(
            e_ref.at[pl.ds(i * ROWS, ROWS)], stage.at[slot], stage_sem.at[slot]
        )

    for i in range(4):
        load_w(i).start()

    barrier = pltpu.get_barrier_semaphore()
    for o in dp_offs:
        pl.semaphore_signal(barrier, inc=1, device_id=at_dp(*o), device_id_type=MESH)
    for k, dc in mp15:
        pl.semaphore_signal(barrier, inc=1, device_id=at_mp(k, dc), device_id_type=MESH)
    pl.semaphore_wait(barrier, len(dp_offs) + len(mp15))

    def send_hid(q):
        return rc(
            hid_ref, hid_all.at[pl.ds(pos * 64, 64)], hid_ss.at[q], hid_rs.at[q], at_dp(*dp_offs[q])
        )

    for q in range(7):
        send_hid(q).start()
    hid_all[pl.ds(pos * 64, 64), :] = hid_ref[...]

    def relay(slot, out, first):
        def body(i, carry):
            r = pltpu.einshape("vjl->jvl", stage[slot, pl.ds(pl.multiple_of(i * 64, 64), 64)])
            s = pl.multiple_of(first + i * 64, 64)
            for j in range(16):
                at = ((j % 2) * 8 + j // 2) * FB
                out[pl.ds(s, 64), at : at + FB] = r[j]
            return carry

        lax.fori_loop(0, ROWS // 64, body, 0)

    for i in range(4):
        load_w(i).wait()
        relay(i, w_flat, i * ROWS)
        load_e(i).start()

    for q in range(7):
        send_hid(q).wait_recv()

    def core_copy(ss, rs, t):
        return rc(ps.at[pl.ds(t * 2, 2)], core_in.at[pl.ds(t * 2, 2)], ss.at[t], rs.at[t], sibling)

    def mp_copy(ss, rs, k):
        return rc(ps2.at[yz_of(k)], mp_in.at[k], ss.at[k], rs.at[k], at_mp(k))

    def product(tile, css, crs):
        for side in (1, 0):
            who = lax.rem(c + side, 2)

            def body(t, carry, who=who, side=side):
                first = who * 8 + t * 2
                r = tile(first, pl.ds(pl.multiple_of(first * FB, 2 * FB), 2 * FB))
                if side:
                    ps[t * 2] = r[:, :FB].astype(BF)
                    ps[t * 2 + 1] = r[:, FB:].astype(BF)
                    core_copy(css, crs, t).start()
                else:
                    acc[first] = r[:, :FB]
                    acc[first + 1] = r[:, FB:]
                return carry

            lax.fori_loop(0, 4, body, 0)

    def encode(v, bound):
        root = lax.rsqrt(lax.rsqrt(jnp.abs(v) * (CODE**4 / bound)))
        code = (root + 0.5).astype(jnp.int32)
        return jnp.where(v < 0, -code, code).astype(jnp.int16)

    def decode(code, bound):
        root = code.astype(F32) * (1.0 / CODE)
        return root * jnp.abs(root) * (root * root) * bound

    def exchange(css, crs, mss, mrs, bound):
        for t in range(4):
            core_copy(css, crs, t).wait_recv()
        for k in mp_offs:
            b = yz_of(k)
            ps2[b] = encode(acc[c * 8 + b] + core_in[b].astype(F32), bound)
            mp_copy(mss, mrs, k).start()

    def collect(css, crs, mss, mrs, bound):
        total = acc[c * 8 + yz] + core_in[yz].astype(F32)
        for k in mp_offs:
            mp_copy(mss, mrs, k).wait_recv()
            total = total + decode(mp_in[k], bound)
        for k in mp_offs:
            mp_copy(mss, mrs, k).wait_send()
        for t in range(4):
            core_copy(css, crs, t).wait_send()
        return total

    product(lambda first, col: dot(hid_all[...], w_flat[:, col], NN), core_ss, core_rs)
    exchange(core_ss, core_rs, mp_ss, mp_rs, PRE_BOUND)

    def relay_e(i, carry):
        load_e(i).wait()
        relay(lax.rem(i, 4), e_flat, i * ROWS)

        @pl.when(i + 4 < V // ROWS)
        def _():
            load_e(i + 4).start()

        return carry

    lax.fori_loop(0, V // ROWS, relay_e, 0)
    for i in range(8):
        hid_t[i * FB : (i + 1) * FB, :] = hid_all[:, i * FB : (i + 1) * FB].T

    pre = collect(core_ss, core_rs, mp_ss, mp_rs, PRE_BOUND)
    pre_s[...] = pre
    own = hid_all[:, pl.ds(pl.multiple_of(dp * FB, FB), FB)].astype(F32)
    act = own + pre / (1.0 + jnp.exp(-pre))
    act_s[...] = act
    gain = gain_ref[...]
    nb[...] = (act * gain).astype(BF)

    def cols(buf, core, b):
        return buf.at[:, pl.ds(pl.multiple_of((core * 8 + b) * FB, FB), FB)]

    def ag_copy(buf, ss, rs, k):
        return rc(nb, cols(buf, c, yz), ss.at[k], rs.at[k], at_mp(k))

    def ag_pass(buf, ss, rs, k):
        at = cols(buf, c, yz_from(k))
        return rc(nb if k == 0 else at, at, ss.at[k], rs.at[k], sibling)

    def gather_start(buf, ss, rs, css, crs):
        for k in mp_offs:
            ag_copy(buf, ss, rs, k).start()
        ag_pass(buf, css, crs, 0).start()
        buf[:, pl.ds(pl.multiple_of((c * 8 + yz) * FB, FB), FB)] = nb[...]

    def gather_end(buf, ss, rs, css, crs):
        for k in reversed(mp_offs):
            ag_copy(buf, ss, rs, k).wait_recv()
            ag_pass(buf, css, crs, k).start()
        for k in range(8):
            ag_pass(buf, css, crs, k).wait_recv()
        for k in range(8):
            ag_pass(buf, css, crs, k).wait_send()
        for k in mp_offs:
            ag_copy(buf, ss, rs, k).wait_send()

    gather_start(nf, nf_ss, nf_rs, nfc_ss, nfc_rs)

    def send_sq(q):
        k, dc = mp15[q]
        return rc(sq_own, sq_in.at[mp], sq_ss.at[q], sq_rs.at[q], at_mp(k, dc))

    squares = act * act
    for i in range(4):
        row = jnp.sum(squares[i * FB : (i + 1) * FB, :].T, axis=0, keepdims=True)
        sq_own[:, i * FB : (i + 1) * FB] = jnp.broadcast_to(row, (8, FB))
    for q in range(15):
        send_sq(q).start()
    sq_in[mp] = sq_own[...]

    all_tgt = all_tgt_ref[...][:, :1]
    for i in range(NCH):
        ids = lax.broadcasted_iota(jnp.int32, (T, HALF), 1) + i * CH
        lz[i] = (ids == all_tgt).astype(BF)
        lx[i] = (ids + HALF == all_tgt).astype(BF)

    def pick_body(n, carry):
        col = pl.ds(pl.multiple_of(n * 256, 256), 256)
        r = jnp.zeros((T, 256), F32)
        for i in range(NCH):
            r = r + dot(lz[i], e_flat[i * CH : i * CH + HALF, col], NN)
            r = r + dot(lx[i], e_flat[i * CH + HALF : (i + 1) * CH, col], NN)
        oh[:, col] = r.astype(BF)
        return carry

    lax.fori_loop(0, 8, pick_body, 0)

    gather_end(nf, nf_ss, nf_rs, nfc_ss, nfc_rs)

    def send_sq2(q):
        return rc(sq_sum, sq_in2.at[dp], sq2_ss.at[q], sq2_rs.at[q], at_dp(*dp_offs[q]))

    for q in range(15):
        send_sq(q).wait_recv()
    sq_sum[...] = jnp.sum(sq_in[...], axis=0)
    for q in range(7):
        send_sq2(q).start()
    sq_in2[dp] = sq_sum[...]

    def rows_of(xx, zz):
        return pl.ds(pl.multiple_of((xx * 2 + zz) * 64, 64), 64)

    def xd(d):
        return lax.rem(x + d, 4)

    def rz_copy(i, d):
        return rc(
            lz.at[i, rows_of(xd(d), 1 - zl)], rz.at[i, d], rz_ss.at[i, d], rz_rs.at[i, d], zpeer
        )

    def rx_copy(i, d):
        src = lx.at[i, pl.ds(pl.multiple_of(xd(d) * 128, 128), 128)]
        return rc(src, rx.at[i, d - 1], rx_ss.at[i, d - 1], rx_rs.at[i, d - 1], at_dp(d, 0))

    def rx2_copy(i):
        return rc(sx2.at[i], rx2.at[i], rx2_ss.at[i], rx2_rs.at[i], zpeer)

    def rz2_copy(i, d):
        return rc(
            sz2.at[i, d - 1], rz2.at[i, d - 1], rz2_ss.at[i, d - 1], rz2_rs.at[i, d - 1], at_dp(d, 0)
        )

    def zcol(i):
        return pl.ds(pl.multiple_of(i * CH, CH), HALF)

    def xcol(i):
        return pl.ds(pl.multiple_of(i * CH + HALF, HALF), HALF)

    def logits_chunk(i):
        at = pl.multiple_of(i * CH, CH)
        lz[i] = dot(nf[...], e_flat[pl.ds(at, HALF), :], NT).astype(BF)
        for d in (2, 1, 3, 0):
            rz_copy(i, d).start()
        lx[i] = dot(nf[...], e_flat[pl.ds(at + HALF, HALF), :], NT).astype(BF)
        for d in (2, 1, 3):
            rx_copy(i, d).start()

    def second_step(i):
        for d in (1, 3, 2):
            rx_copy(i, d).wait_recv()
        base = pl.multiple_of(x * 128, 128)
        for mine in (False, True):
            zz = zl if mine else 1 - zl
            off = pl.multiple_of(zz * 64, 64)
            s = lx[i, pl.ds(base + off, 64)].astype(F32)
            for d in range(3):
                s = s + rx[i, d, pl.ds(off, 64)].astype(F32)
            if mine:
                lg[:, xcol(i)] = s
            else:
                sx2[i] = s.astype(BF)
                rx2_copy(i).start()
        for d in (2, 1, 3, 0):
            rz_copy(i, d).wait_recv()
            s = lz[i, rows_of(xd(d), zl)].astype(F32) + rz[i, d].astype(F32)
            if d:
                sz2[i, d - 1] = s.astype(BF)
                rz2_copy(i, d).start()
            else:
                lg[:, zcol(i)] = s

    def rs_loop(i, carry):
        @pl.when(i < NCH)
        def _():
            logits_chunk(i)

        @pl.when(i > 0)
        def _():
            second_step(i - 1)

        return carry

    lax.fori_loop(0, NCH + 1, rs_loop, 0)

    for q in range(7):
        send_sq2(q).wait_recv()
    mean = jnp.sum(sq_in2[...], axis=0)[:1, :] / D
    inv_row = lax.rsqrt(mean + 1e-05)
    for i in range(4):
        part = jnp.broadcast_to(inv_row[:, i * FB : (i + 1) * FB], (FB, FB))
        inv_s[i * FB : (i + 1) * FB, :] = part.T

    def rs_end(i, carry):
        rx2_copy(i).wait_recv()
        lg[:, xcol(i)] = lg[:, xcol(i)] + rx2[i].astype(F32)
        s = lg[:, zcol(i)]
        for d in (1, 3, 2):
            rz2_copy(i, d).wait_recv()
            s = s + rz2[i, d - 1].astype(F32)
        lg[:, zcol(i)] = s
        return carry

    lax.fori_loop(0, NCH, rs_end, 0)

    def dl_at(xx, zz, col):
        return dl.at[rows_of(xx, zz), col]

    def az_copy(i, d):
        a = dl_at(x, zl, zcol(i))
        return rc(a, a, az_ss.at[i, d - 1], az_rs.at[i, d - 1], at_dp(d, 0))

    def azz_copy(i):
        a = dl_at(x, zl, zcol(i))
        return rc(a, a, azz_ss.at[i], azz_rs.at[i], zpeer)

    def azf_copy(i, d):
        a = dl_at(lax.rem(x + 4 - d, 4), zl, zcol(i))
        return rc(a, a, azf_ss.at[i, d - 1], azf_rs.at[i, d - 1], zpeer)

    def ax_copy(i, d):
        a = dl_at(x, zl, xcol(i))
        return rc(a, a, ax_ss.at[i, d - 1], ax_rs.at[i, d - 1], at_dp(d, 0))

    def axz_copy(i):
        a = dl_at(x, zl, xcol(i))
        return rc(a, a, axz_ss.at[i], axz_rs.at[i], zpeer)

    def axf_copy(i, d):
        a = dl_at(x, 1 - zl, xcol(i))
        return rc(a, a, axf_ss.at[i, d - 1], axf_rs.at[i, d - 1], at_dp(d, 0))

    my_rows = pl.ds(pl.multiple_of(pos * 64, 64), 64)
    inv_own = inv_s[my_rows, :][:, :1]
    lane = lax.broadcasted_iota(jnp.int32, (64, FB), 1)
    tgt = tgt_ref[...][:, :1]

    def max_body(i, m):
        at = pl.ds(pl.multiple_of(i * HALF, HALF), HALF)
        v = lg[:, at] * inv_own
        lg[:, at] = v
        return jnp.maximum(m, jnp.max(v, axis=1, keepdims=True))

    m = lax.fori_loop(0, V // HALF, max_body, jnp.full((64, 1), -jnp.inf, F32))

    def exp_body(i, carry):
        s, sl, pk = carry
        for h in (0, 1):
            at = pl.ds(pl.multiple_of(i * CH + h * HALF, HALF), HALF)
            ids = lax.broadcasted_iota(jnp.int32, (64, HALF), 1) + (i * CH + h * HALF)
            v = lg[:, at]
            p = jnp.exp(v - m)
            dl[my_rows, at] = p.astype(BF)
            if h:
                axz_copy(i).start()
                for d in (2, 1, 3):
                    ax_copy(i, d).start()
            else:
                for d in (2, 1, 3):
                    az_copy(i, d).start()
                azz_copy(i).start()
            s = s + jnp.sum(p, axis=1, keepdims=True)
            sl = sl + jnp.sum(p * v, axis=1, keepdims=True)
            pk = pk + jnp.sum(jnp.where(ids == tgt, v, 0.0), axis=1, keepdims=True)
        return s, sl, pk

    zero = jnp.zeros((64, 1), F32)
    s, sl, pk = lax.fori_loop(0, NCH, exp_body, (zero, zero, zero))
    tsq[...] = jnp.zeros((FB, FB), F32)
    tsq[:64, :] = jnp.where(
        lane == 0, m, jnp.where(lane == 1, s, jnp.where(lane == 2, sl, jnp.where(lane == 3, pk, 0.0)))
    )
    st_own[...] = tsq[...].T[:8, :]

    def send_st(q):
        k, dc = mp15[q]
        return rc(st_own, st_in.at[mp], st_ss.at[q], st_rs.at[q], at_mp(k, dc))

    for q in range(15):
        send_st(q).start()
    st_in[mp] = st_own[...]

    def fwd_body(i, carry):
        axz_copy(i).wait_recv()
        for d in (2, 1, 3):
            axf_copy(i, d).start()
        for d in (1, 3, 2):
            az_copy(i, d).wait_recv()
            azf_copy(i, d).start()
        return carry

    lax.fori_loop(0, 2, fwd_body, 0)

    for q in range(15):
        send_st(q).wait_recv()
    all_m = st_in[:, 0, :]
    top = jnp.max(all_m, axis=0, keepdims=True)
    scale = jnp.exp(all_m - top)
    total = jnp.sum(st_in[:, 1, :] * scale, axis=0, keepdims=True)
    total_l = jnp.sum(st_in[:, 2, :] * scale, axis=0, keepdims=True)
    picked = jnp.sum(st_in[:, 3, :], axis=0, keepdims=True)
    valid = lax.broadcasted_iota(jnp.int32, (1, FB), 1) < 64
    total = jnp.where(valid, total, 1.0)
    lse = top + jnp.log(total)
    moment = (total_l / total - picked) / T
    factor = jnp.exp(st_own[:1, :] - lse) / T
    sub = lax.broadcasted_iota(jnp.int32, (FB, FB), 0)
    table = jnp.where(sub == 0, factor, jnp.where(sub == 1, moment, jnp.where(sub == 2, lse - picked, 0.0)))
    tsq[...] = table.T
    sc_all[pos] = tsq[:64, :]

    def send_sc(q):
        return rc(sc_all.at[pos], sc_all.at[pos], sc_ss.at[q], sc_rs.at[q], at_dp(*dp_offs[q]))

    for q in range(7):
        send_sc(q).start()

    lax.fori_loop(2, NCH, fwd_body, 0)

    def ag_end(i):
        azz_copy(i).wait_recv()
        for d in (1, 3, 2):
            ax_copy(i, d).wait_recv()
            axf_copy(i, d).wait_recv()
            azf_copy(i, d).wait_recv()

    def part(i, col):
        at = pl.multiple_of(i * CH, CH)
        return dot(dl[:, pl.ds(at, CH)], e_flat[pl.ds(at, CH), col], NN)

    for i in range(NCH - 1):
        ag_end(i)

        def part_body(t, carry, i=i):
            r = part(i, pl.ds(pl.multiple_of(t * 256, 256), 256))
            for h in (0, 1):
                v = r[:, h * FB : (h + 1) * FB]
                acc[t * 2 + h] = v if i == 0 else acc[t * 2 + h] + v
            return carry

        lax.fori_loop(0, 8, part_body, 0)

    for q in range(7):
        send_sc(q).wait_recv()
    loss = jnp.zeros((64, 1), F32)
    for b in range(8):
        loss = loss + sc_all[b][:, 2:3]
        ct[b * 64 : (b + 1) * 64, :] = jnp.broadcast_to(sc_all[b][:, 0:1], (64, FB))
    loss_ref[...] = jnp.broadcast_to(jnp.sum(loss, axis=0, keepdims=True) / T, (8, FB))
    ag_end(NCH - 1)

    def last_tile(first, col):
        r = part(NCH - 1, col)
        f = ct[...]
        own_row = oh[:, col].astype(F32) / T
        return jnp.concatenate(
            [(acc[first + h] + r[:, h * FB : (h + 1) * FB]) * f - own_row[:, h * FB : (h + 1) * FB] for h in (0, 1)],
            axis=1,
        )

    product(last_tile, core2_ss, core2_rs)
    exchange(core2_ss, core2_rs, mp2_ss, mp2_rs, GRAD_BOUND)
    dnormed = collect(core2_ss, core2_rs, mp2_ss, mp2_rs, GRAD_BOUND)
    moments = jnp.concatenate([sc_all[b][:, 1:2] for b in range(8)], axis=0)
    inv = inv_s[...]
    act = act_s[...]
    pre = pre_s[...]
    dact = inv * gain * dnormed - act * (inv * inv * (moments / D))
    sig = 1.0 / (1.0 + jnp.exp(-pre))
    nb[...] = (dact * sig * (1.0 + pre * (1.0 - sig))).astype(BF)
    gather_start(dpf, dp_ss, dp_rs, dpc_ss, dpc_rs)
    gather_end(dpf, dp_ss, dp_rs, dpc_ss, dpc_rs)

    for q in range(7):
        send_hid(q).wait_send()
        send_sq2(q).wait_send()
        send_sc(q).wait_send()
    for q in range(15):
        send_sq(q).wait_send()
        send_st(q).wait_send()

    def drain(i, carry):
        rx2_copy(i).wait_send()
        azz_copy(i).wait_send()
        axz_copy(i).wait_send()
        for d in range(4):
            rz_copy(i, d).wait_send()
        for d in (1, 2, 3):
            rx_copy(i, d).wait_send()
            rz2_copy(i, d).wait_send()
            az_copy(i, d).wait_send()
            azf_copy(i, d).wait_send()
            ax_copy(i, d).wait_send()
            axf_copy(i, d).wait_send()
        return carry

    lax.fori_loop(0, NCH, drain, 0)


def head(hidden, weight, gain, embed, tgt, all_tgt):
    vm = pltpu.VMEM
    dma = pltpu.SemaphoreType.DMA
    scratch = [
        vm((V, 2048), BF), vm((1024, 2048), BF), vm((4, ROWS, 16, FB), BF), vm((T, 1024), BF),
        vm((8, T, FB), BF), vm((16, T, FB), F32), vm((8, T, FB), BF), vm((8, T, FB), jnp.int16),
        vm((8, T, FB), jnp.int16), vm((T, 2048), BF), vm((T, FB), F32),
        vm((T, FB), F32), vm((T, FB), F32), vm((T, FB), BF), vm((T, 2048), BF),
        vm((8, T), F32), vm((16, 8, T), F32), vm((8, T), F32), vm((8, 8, T), F32), vm((T, FB), F32),
        vm((NCH, T, HALF), BF), vm((NCH, T, HALF), BF),
        vm((NCH, 3, 128, HALF), BF), vm((NCH, 4, 64, HALF), BF),
        vm((NCH, 64, HALF), BF), vm((NCH, 64, HALF), BF), vm((NCH, 3, 64, HALF), BF), vm((NCH, 3, 64, HALF), BF),
        vm((64, V), F32), vm((FB, FB), F32), vm((8, FB), F32), vm((16, 8, FB), F32),
        vm((8, 64, FB), F32), vm((T, V), BF),
        dma((4,)),
    ]
    counts = [
        (7,), (4,), (8,), (4,), (8,), (8,), (8,), (8,), (8,), (15,), (7,), (15,), (7,),
        (NCH, 3), (NCH, 4), (NCH,), (NCH, 3),
        (NCH, 3), (NCH,), (NCH, 3), (NCH, 3), (NCH, 3), (NCH,),
    ]
    for n in counts:
        scratch += [dma(n), dma(n)]
    vspec = pl.BlockSpec(memory_space=pltpu.VMEM)
    anyspec = pl.BlockSpec(memory_space=pl.ANY)
    return pl.pallas_call(
        head_kernel,
        name="head",
        out_shape=(
            jax.ShapeDtypeStruct((T, 2048), BF),
            jax.ShapeDtypeStruct((1024, T), BF),
            jax.ShapeDtypeStruct((8, FB), F32),
        ),
        in_specs=[vspec, anyspec, vspec, anyspec, vspec, vspec],
        out_specs=(vspec, vspec, vspec),
        scratch_shapes=scratch,
        compiler_params=pltpu.CompilerParams(
            collective_id=0, has_side_effects=True, vmem_limit_bytes=62 << 20
        ),
    )(hidden, weight, gain, embed, tgt, all_tgt)


def grad_kernel(hid_t, dpf, out):
    r = dot(hid_t[...], dpf[...], NN).astype(BF)
    blocks = jnp.stack([r[:, ((j % 2) * 8 + j // 2) * FB :][:, :FB] for j in range(16)])
    out[...] = pltpu.einshape("jvl->vjl", blocks)


def weight_gradient(hid_t, dpf):
    rows = 128
    return pl.pallas_call(
        grad_kernel,
        name="weight_gradient",
        grid=(1024 // rows,),
        out_shape=jax.ShapeDtypeStruct((1024, 16, FB), BF),
        in_specs=[
            pl.BlockSpec((rows, T), lambda i: (i, 0)),
            pl.BlockSpec((T, 2048), lambda i: (0, 0)),
        ],
        out_specs=pl.BlockSpec((rows, 16, FB), lambda i: (i, 0, 0)),
        compiler_params=pltpu.CompilerParams(vmem_limit_bytes=32 << 20),
    )(hid_t, dpf)


def on_device(hidden_rows, head_weight, norm_gain, vocab_embed, targets):
    dp = lax.axis_index("dp")
    mp = lax.axis_index("mp")
    local = targets - mp * V
    mine = lax.dynamic_slice_in_dim(local, dp * 64, 64, 0)
    ordered = local.reshape(2, 4, 64).transpose(1, 0, 2).reshape(T)
    dpf, hid_t, loss = head(
        hidden_rows,
        head_weight.reshape(1024, 16, FB),
        norm_gain.reshape(1, FB),
        vocab_embed.reshape(V, 16, FB),
        jnp.broadcast_to(mine[:, None], (64, FB)),
        jnp.broadcast_to(ordered[:, None], (T, FB)),
    )
    grad = weight_gradient(hid_t, dpf)
    return grad.reshape(head_weight.shape), loss[0, 0]


def solution(mesh):
    return jax.shard_map(
        on_device,
        mesh=mesh,
        in_specs=(
            P("dp", "mp"),
            P("mp", None, "dp", None),
            P("mp", "dp", None),
            P("mp", None, "dp", None),
            P(),
        ),
        out_specs=(P("mp", None, "dp", None), P()),
        check_vma=False,
    )
```

```python
import jax
import jax.numpy as jnp
from jax import lax
from jax.experimental import pallas as pl
from jax.experimental.pallas import tpu as pltpu
from jax.sharding import PartitionSpec as P

MESH = pl.DeviceIdType.MESH
BF = jnp.bfloat16
F32 = jnp.float32
T, D, V, FB = 512, 16384, 4096, 128
TH = T // 2
TR = 32
CH = 2048
HALF = 1024
NG = 4
ROWS = 256
CODE = 32000.0
PRE_BOUND = 60.0 * 0.046875 * 2048 * 1.01
GRAD_BOUND = 6.0 * 2 / T * 1.01
NT = (((1,), (1,)), ((), ()))
NN = (((1,), (0,)), ((), ()))


def dot(a, b, dims):
    return lax.dot_general(a, b, dims, preferred_element_type=F32)


def head_kernel(
    hid_ref, w_ref, gain_ref, e_ref, tgt_ref,
    grad_ref, loss_ref,
    e_flat, w_flat, stage, hid_all, hid_t, ps, acc, core_in, ps2, mp_in, oh, ct, tcol,
    pre_s, act_s, nb, nf, dpf, sq_own, sq_in, sq_sum, sq_in2, inv_s,
    lz, lx, rx, rz, sx2, rx2, sz2, rz2, lg, tsq, st_own, st_in, sc_all, dl,
    stage_sem, out_sem,
    hid_ss, hid_rs, core_ss, core_rs, mp_ss, mp_rs, core2_ss, core2_rs, mp2_ss, mp2_rs,
    nf_ss, nf_rs, nfc_ss, nfc_rs, dp_ss, dp_rs, dpc_ss, dpc_rs,
    sq_ss, sq_rs, sq2_ss, sq2_rs, st_ss, st_rs, sc_ss, sc_rs,
    rx_ss, rx_rs, rz_ss, rz_rs, rx2_ss, rx2_rs, rz2_ss, rz2_rs,
    az_ss, az_rs, azz_ss, azz_rs, ax_ss, ax_rs, axf_ss, axf_rs, azf_ss, azf_rs, axz_ss, axz_rs,
):
    dp = lax.axis_index("dp")
    mp = lax.axis_index("mp")
    x, zl = lax.rem(dp, 4), dp // 4
    yz, c = mp // 2, lax.rem(mp, 2)
    y, zh = yz // 2, lax.rem(yz, 2)
    pos = x * 2 + zl

    def at_dp(dx, dz):
        return (lax.rem(zl + dz, 2) * 4 + lax.rem(x + dx, 4), mp)

    def at_mp(k, dc=0):
        return (dp, yz_of(k) * 2 + lax.rem(c + dc, 2))

    def yz_of(k):
        return lax.rem(y + k // 2, 4) * 2 + lax.rem(zh + k % 2, 2)

    def yz_from(k):
        return lax.rem(y + 4 - k // 2, 4) * 2 + lax.rem(zh + k % 2, 2)

    zpeer = at_dp(0, 1)
    sibling = at_mp(0, 1)
    dp_offs = [(k % 4, k // 4) for k in (6, 2, 5, 7, 1, 3, 4)]
    mp_offs = [5, 4, 3, 7, 2, 6, 1]
    mp15 = [(k, 1) for k in [*mp_offs, 0]] + [(k, 0) for k in mp_offs]

    def rc(src, dst, ss, rs, dev):
        return pltpu.make_async_remote_copy(
            src_ref=src, dst_ref=dst, send_sem=ss, recv_sem=rs, device_id=dev, device_id_type=MESH
        )

    def load_w(i):
        return pltpu.make_async_copy(w_ref.at[pl.ds(i * ROWS, ROWS)], stage.at[i], stage_sem.at[i])

    def load_e(i):
        slot = lax.rem(i, 4)
        return pltpu.make_async_copy(
            e_ref.at[pl.ds(i * ROWS, ROWS)], stage.at[slot], stage_sem.at[slot]
        )

    for i in range(4):
        load_w(i).start()

    barrier = pltpu.get_barrier_semaphore()
    for o in dp_offs:
        pl.semaphore_signal(barrier, inc=1, device_id=at_dp(*o), device_id_type=MESH)
    for k, dc in mp15:
        pl.semaphore_signal(barrier, inc=1, device_id=at_mp(k, dc), device_id_type=MESH)
    pl.semaphore_wait(barrier, len(dp_offs) + len(mp15))

    def tok(p):
        return pl.ds(pl.multiple_of(p * TR, TR), TR)

    def send_hid(q, h):
        return rc(
            hid_ref.at[pl.ds(h * TR, TR)], hid_all.at[h, tok(pos)],
            hid_ss.at[q, h], hid_rs.at[q, h], at_dp(*dp_offs[q]),
        )

    for h in (0, 1):
        for q in range(7):
            send_hid(q, h).start()
        hid_all[h, tok(pos), :] = hid_ref[h * TR : (h + 1) * TR, :]

    def relay(slot, out, first):
        def body(i, carry):
            r = pltpu.einshape("vjl->jvl", stage[slot, pl.ds(pl.multiple_of(i * 64, 64), 64)])
            s = pl.multiple_of(first + i * 64, 64)
            for j in range(16):
                at = ((j % 2) * 8 + j // 2) * FB
                out[pl.ds(s, 64), at : at + FB] = r[j]
            return carry

        lax.fori_loop(0, ROWS // 64, body, 0)

    def relay_e(i, carry):
        load_e(i).wait()
        relay(lax.rem(i, 4), e_flat, i * ROWS)

        @pl.when(i + 4 < V // ROWS)
        def _():
            load_e(i + 4).start()

        return carry

    for i in range(4):
        load_w(i).wait()
        relay(i, w_flat, i * ROWS)
        load_e(i).start()

    local_tgt = tgt_ref[...].astype(F32) - (mp * V).astype(F32)
    for i in range(4):
        part = jnp.broadcast_to(local_tgt[:, i * FB : (i + 1) * FB], (FB, FB)).T
        for j in (0, 1):
            block = i * 2 + j
            at = ((block % 4) * 2 + block // 4) * TR
            for h in (0, 1):
                first = j * 64 + h * TR
                tcol[h, at : at + TR, :] = part[first : first + TR, :]

    def zcol(i):
        return pl.ds(pl.multiple_of(i * CH, CH), HALF)

    def xcol(i):
        return pl.ds(pl.multiple_of(i * CH + HALF, HALF), HALF)

    for h in (0, 1):
        for i in (0, 1):
            ids = (lax.broadcasted_iota(jnp.int32, (TH, HALF), 1) + i * CH).astype(F32)
            want = tcol[h, :, :1]
            lz[h * 2 + i] = (ids == want).astype(BF)
            lx[h * 2 + i] = (ids + HALF == want).astype(BF)

    def pick_body(n, carry):
        col = pl.ds(pl.multiple_of(n * 256, 256), 256)
        for h in (0, 1):
            r = jnp.zeros((TH, 256), F32)
            for i in (0, 1):
                r = r + dot(lz[h * 2 + i], e_flat[i * CH : i * CH + HALF, col], NN)
                r = r + dot(lx[h * 2 + i], e_flat[i * CH + HALF : (i + 1) * CH, col], NN)
            oh[h, :, col] = r.astype(BF)
        return carry

    lax.fori_loop(0, 8, relay_e, 0)

    def core_copy(h, ss, rs, t):
        two = pl.ds(t * 2, 2)
        return rc(ps.at[h, two], core_in.at[h, two], ss.at[h, t], rs.at[h, t], sibling)

    def mp_copy(h, ss, rs, k):
        return rc(ps2.at[h, yz_of(k)], mp_in.at[h, k], ss.at[h, k], rs.at[h, k], at_mp(k))

    def product(h, tile, css, crs, side):
        who = lax.rem(c + side, 2)

        def body(t, carry):
            first = who * 8 + t * 2
            r = tile(first, pl.ds(pl.multiple_of(first * FB, 2 * FB), 2 * FB))
            if side:
                ps[h, t * 2] = r[:, :FB].astype(BF)
                ps[h, t * 2 + 1] = r[:, FB:].astype(BF)
                core_copy(h, css, crs, t).start()
            else:
                acc[h, first] = r[:, :FB]
                acc[h, first + 1] = r[:, FB:]
            return carry

        lax.fori_loop(0, 4, body, 0)

    def encode(v, bound):
        root = lax.rsqrt(lax.rsqrt(jnp.abs(v) * (CODE**4 / bound)))
        code = (root + 0.5).astype(jnp.int32)
        return jnp.where(v < 0, -code, code).astype(jnp.int16)

    def decode(code, bound):
        root = code.astype(F32) * (1.0 / CODE)
        return root * jnp.abs(root) * (root * root) * bound

    def exchange(h, css, crs, mss, mrs, bound):
        for t in range(4):
            core_copy(h, css, crs, t).wait_recv()
        for k in mp_offs:
            b = yz_of(k)
            ps2[h, b] = encode(acc[h, c * 8 + b] + core_in[h, b].astype(F32), bound)
            mp_copy(h, mss, mrs, k).start()

    def collect(h, css, crs, mss, mrs, bound):
        total = acc[h, c * 8 + yz] + core_in[h, yz].astype(F32)
        for k in mp_offs:
            mp_copy(h, mss, mrs, k).wait_recv()
            total = total + decode(mp_in[h, k], bound)
        for k in mp_offs:
            mp_copy(h, mss, mrs, k).wait_send()
        for t in range(4):
            core_copy(h, css, crs, t).wait_send()
        return total

    for h in (0, 1):
        for q in range(7):
            send_hid(q, h).wait_recv()
        for side in (1, 0):
            product(h, lambda first, col, h=h: dot(hid_all[h], w_flat[:, col], NN), core_ss, core_rs, side)
        exchange(h, core_ss, core_rs, mp_ss, mp_rs, PRE_BOUND)

    lax.fori_loop(8, V // ROWS, relay_e, 0)
    lax.fori_loop(0, 2, pick_body, 0)

    gain = gain_ref[...]

    def cols(core, b):
        return pl.ds(pl.multiple_of((core * 8 + b) * FB, FB), FB)

    def ag_copy(buf, h, ss, rs, k):
        return rc(nb.at[h], buf.at[h, :, cols(c, yz)], ss.at[h, k], rs.at[h, k], at_mp(k))

    def ag_pass(buf, h, ss, rs, k):
        at = buf.at[h, :, cols(c, yz_from(k))]
        return rc(nb.at[h] if k == 0 else at, at, ss.at[h, k], rs.at[h, k], sibling)

    def gather_start(buf, h, ss, rs, css, crs):
        for k in mp_offs:
            ag_copy(buf, h, ss, rs, k).start()
        ag_pass(buf, h, css, crs, 0).start()
        buf[h, :, cols(c, yz)] = nb[h]

    def gather_mid(buf, h, ss, rs, css, crs):
        for k in reversed(mp_offs):
            ag_copy(buf, h, ss, rs, k).wait_recv()
            ag_pass(buf, h, css, crs, k).start()

    def gather_end(buf, h, ss, rs, css, crs):
        for k in range(8):
            ag_pass(buf, h, css, crs, k).wait_recv()
        for k in range(8):
            ag_pass(buf, h, css, crs, k).wait_send()
        for k in mp_offs:
            ag_copy(buf, h, ss, rs, k).wait_send()

    nf_sems = (nf_ss, nf_rs, nfc_ss, nfc_rs)
    dp_sems = (dp_ss, dp_rs, dpc_ss, dpc_rs)

    def activate(h):
        pre = collect(h, core_ss, core_rs, mp_ss, mp_rs, PRE_BOUND)
        pre_s[h] = pre
        own = hid_all[h, :, pl.ds(pl.multiple_of(dp * FB, FB), FB)].astype(F32)
        act = own + pre / (1.0 + jnp.exp(-pre))
        act_s[h] = act
        nb[h] = (act * gain).astype(BF)
        gather_start(nf, h, *nf_sems)
        squares = act * act
        for i in (0, 1):
            row = jnp.sum(squares[i * FB : (i + 1) * FB, :].T, axis=0, keepdims=True)
            at = h * TH + i * FB
            sq_own[:, at : at + FB] = jnp.broadcast_to(row, (8, FB))

    def send_sq(q):
        k, dc = mp15[q]
        return rc(sq_own, sq_in.at[mp], sq_ss.at[q], sq_rs.at[q], at_mp(k, dc))

    activate(0)
    lax.fori_loop(2, 4, pick_body, 0)
    activate(1)
    for q in range(15):
        send_sq(q).start()
    sq_in[mp] = sq_own[...]
    lax.fori_loop(4, 6, pick_body, 0)
    gather_mid(nf, 0, *nf_sems)
    lax.fori_loop(6, 8, pick_body, 0)
    gather_end(nf, 0, *nf_sems)

    def rows_of(xx, zz):
        return tok(xx * 2 + zz)

    def xd(d):
        return lax.rem(x + d, 4)

    def rz_copy(g, d):
        return rc(
            lz.at[g, rows_of(xd(d), 1 - zl)], rz.at[g, d], rz_ss.at[g, d], rz_rs.at[g, d], zpeer
        )

    def rx_copy(g, d):
        src = lx.at[g, pl.ds(pl.multiple_of(xd(d) * 2 * TR, 2 * TR), 2 * TR)]
        return rc(src, rx.at[g, d - 1], rx_ss.at[g, d - 1], rx_rs.at[g, d - 1], at_dp(d, 0))

    def rx2_copy(g):
        return rc(sx2.at[g], rx2.at[g], rx2_ss.at[g], rx2_rs.at[g], zpeer)

    def rz2_copy(g, d):
        return rc(
            sz2.at[g, d - 1], rz2.at[g, d - 1], rz2_ss.at[g, d - 1], rz2_rs.at[g, d - 1], at_dp(d, 0)
        )

    def logits_chunk(g):
        h, i = g // 2, g % 2
        lz[g] = dot(nf[h], e_flat[i * CH : i * CH + HALF, :], NT).astype(BF)
        for d in (2, 1, 3, 0):
            rz_copy(g, d).start()
        lx[g] = dot(nf[h], e_flat[i * CH + HALF : (i + 1) * CH, :], NT).astype(BF)
        for d in (2, 1, 3):
            rx_copy(g, d).start()

    def second_step(g):
        h, i = g // 2, g % 2
        for d in (1, 3, 2):
            rx_copy(g, d).wait_recv()
        base = pl.multiple_of(x * 2 * TR, 2 * TR)
        for mine in (False, True):
            off = pl.multiple_of((zl if mine else 1 - zl) * TR, TR)
            s = lx[g, pl.ds(base + off, TR)].astype(F32)
            for d in range(3):
                s = s + rx[g, d, pl.ds(off, TR)].astype(F32)
            if mine:
                lg[h, :, xcol(i)] = s
            else:
                sx2[g] = s.astype(BF)
                rx2_copy(g).start()
        for d in (2, 1, 3, 0):
            rz_copy(g, d).wait_recv()
            s = lz[g, rows_of(xd(d), zl)].astype(F32) + rz[g, d].astype(F32)
            if d:
                sz2[g, d - 1] = s.astype(BF)
                rz2_copy(g, d).start()
            else:
                lg[h, :, zcol(i)] = s

    def rs_end(g):
        h, i = g // 2, g % 2
        rx2_copy(g).wait_recv()
        lg[h, :, xcol(i)] = lg[h, :, xcol(i)] + rx2[g].astype(F32)
        s = lg[h, :, zcol(i)]
        for d in (1, 3, 2):
            rz2_copy(g, d).wait_recv()
            s = s + rz2[g, d - 1].astype(F32)
        lg[h, :, zcol(i)] = s

    def dl_at(h, xx, zz, col):
        return dl.at[h, rows_of(xx, zz), col]

    def az_copy(g, d):
        a = dl_at(g // 2, x, zl, zcol(g % 2))
        return rc(a, a, az_ss.at[g, d - 1], az_rs.at[g, d - 1], at_dp(d, 0))

    def azz_copy(g):
        a = dl_at(g // 2, x, zl, zcol(g % 2))
        return rc(a, a, azz_ss.at[g], azz_rs.at[g], zpeer)

    def azf_copy(g, d):
        a = dl_at(g // 2, lax.rem(x + 4 - d, 4), zl, zcol(g % 2))
        return rc(a, a, azf_ss.at[g, d - 1], azf_rs.at[g, d - 1], zpeer)

    def ax_copy(g, d):
        a = dl_at(g // 2, x, zl, xcol(g % 2))
        return rc(a, a, ax_ss.at[g, d - 1], ax_rs.at[g, d - 1], at_dp(d, 0))

    def axz_copy(g):
        a = dl_at(g // 2, x, zl, xcol(g % 2))
        return rc(a, a, axz_ss.at[g], axz_rs.at[g], zpeer)

    def axf_copy(g, d):
        a = dl_at(g // 2, x, 1 - zl, xcol(g % 2))
        return rc(a, a, axf_ss.at[g, d - 1], axf_rs.at[g, d - 1], at_dp(d, 0))

    lane = lax.broadcasted_iota(jnp.int32, (TR, FB), 1)

    def send_st(h, q):
        k, dc = mp15[q]
        return rc(st_own.at[h], st_in.at[h, mp], st_ss.at[h, q], st_rs.at[h, q], at_mp(k, dc))

    def softmax(h):
        inv_own = inv_s[h, tok(pos), :][:, :1]
        want = tcol[h, tok(pos), :][:, :1]
        m = jnp.full((TR, 1), -jnp.inf, F32)
        for j in range(V // HALF):
            v = lg[h, :, j * HALF : (j + 1) * HALF] * inv_own
            lg[h, :, j * HALF : (j + 1) * HALF] = v
            m = jnp.maximum(m, jnp.max(v, axis=1, keepdims=True))
        s, sl, pk = (jnp.zeros((TR, 1), F32) for _ in range(3))
        for j in range(V // HALF):
            ids = (lax.broadcasted_iota(jnp.int32, (TR, HALF), 1) + j * HALF).astype(F32)
            v = lg[h, :, j * HALF : (j + 1) * HALF]
            p = jnp.exp(v - m)
            dl[h, tok(pos), j * HALF : (j + 1) * HALF] = p.astype(BF)
            g = h * 2 + j // 2
            if j % 2:
                axz_copy(g).start()
                for d in (2, 1, 3):
                    ax_copy(g, d).start()
            else:
                for d in (2, 1, 3):
                    az_copy(g, d).start()
                azz_copy(g).start()
            s = s + jnp.sum(p, axis=1, keepdims=True)
            sl = sl + jnp.sum(p * v, axis=1, keepdims=True)
            pk = pk + jnp.sum(jnp.where(ids == want, v, 0.0), axis=1, keepdims=True)
        tsq[...] = jnp.zeros((FB, FB), F32)
        tsq[:TR, :] = jnp.where(
            lane == 0, m, jnp.where(lane == 1, s, jnp.where(lane == 2, sl, jnp.where(lane == 3, pk, 0.0)))
        )
        st_own[h] = tsq[...].T[:8, :]
        for q in range(15):
            send_st(h, q).start()
        st_in[h, mp] = st_own[h]

    def forward(g):
        axz_copy(g).wait_recv()
        for d in (2, 1, 3):
            axf_copy(g, d).start()
        for d in (1, 3, 2):
            az_copy(g, d).wait_recv()
            azf_copy(g, d).start()

    def ag_end(g):
        azz_copy(g).wait_recv()
        for d in (1, 3, 2):
            ax_copy(g, d).wait_recv()
            axf_copy(g, d).wait_recv()
            azf_copy(g, d).wait_recv()

    def send_sc(h, q):
        a = sc_all.at[h, pos]
        return rc(a, a, sc_ss.at[h, q], sc_rs.at[h, q], at_dp(*dp_offs[q]))

    def statistics(h):
        for q in range(15):
            send_st(h, q).wait_recv()
        all_m = st_in[h, :, 0, :]
        top = jnp.max(all_m, axis=0, keepdims=True)
        scale = jnp.exp(all_m - top)
        total = jnp.sum(st_in[h, :, 1, :] * scale, axis=0, keepdims=True)
        total_l = jnp.sum(st_in[h, :, 2, :] * scale, axis=0, keepdims=True)
        picked = jnp.sum(st_in[h, :, 3, :], axis=0, keepdims=True)
        valid = lax.broadcasted_iota(jnp.int32, (1, FB), 1) < TR
        total = jnp.where(valid, total, 1.0)
        lse = top + jnp.log(total)
        moment = (total_l / total - picked) / T
        factor = jnp.exp(st_own[h, :1, :] - lse) / T
        sub = lax.broadcasted_iota(jnp.int32, (FB, FB), 0)
        table = jnp.where(sub == 0, factor, jnp.where(sub == 1, moment, jnp.where(sub == 2, lse - picked, 0.0)))
        tsq[...] = table.T
        sc_all[h, pos] = tsq[:TR, :]
        for q in range(7):
            send_sc(h, q).start()

    def factors(h):
        for q in range(7):
            send_sc(h, q).wait_recv()
        for b in range(8):
            ct[h, b * TR : (b + 1) * TR, :] = jnp.broadcast_to(sc_all[h, b][:, 0:1], (TR, FB))

    def scaled_tile(h, first, col, r):
        f = ct[h]
        own_row = oh[h, :, col].astype(F32) / T
        return jnp.concatenate(
            [r[:, b * FB : (b + 1) * FB] * f - own_row[:, b * FB : (b + 1) * FB] for b in (0, 1)], axis=1
        )

    def early_part(h):
        def body(t, carry):
            r = dot(dl[h, :, :CH], e_flat[:CH, pl.ds(pl.multiple_of(t * 256, 256), 256)], NN)
            acc[h, t * 2] = r[:, :FB]
            acc[h, t * 2 + 1] = r[:, FB:]
            return carry

        lax.fori_loop(0, 8, body, 0)

    def late_tile(h):
        def tile(first, col):
            r = dot(dl[h, :, CH:], e_flat[CH:, col], NN)
            return scaled_tile(h, first, col, r + jnp.concatenate([acc[h, first], acc[h, first + 1]], axis=1))

        return tile

    def whole_tile(h):
        return lambda first, col: scaled_tile(h, first, col, dot(dl[h], e_flat[:, col], NN))

    def pre_gradient(h):
        dnormed = collect(h, core2_ss, core2_rs, mp2_ss, mp2_rs, GRAD_BOUND)
        moments = jnp.concatenate([sc_all[h, b][:, 1:2] for b in range(8)], axis=0)
        inv, act, pre = inv_s[h], act_s[h], pre_s[h]
        dact = inv * gain * dnormed - act * (inv * inv * (moments / D))
        sig = 1.0 / (1.0 + jnp.exp(-pre))
        nb[h] = (dact * sig * (1.0 + pre * (1.0 - sig))).astype(BF)
        gather_start(dpf, h, *dp_sems)

    logits_chunk(0)
    logits_chunk(1)
    gather_mid(nf, 1, *nf_sems)
    second_step(0)
    gather_end(nf, 1, *nf_sems)
    logits_chunk(2)
    second_step(1)
    logits_chunk(3)

    def send_sq2(q):
        return rc(sq_sum, sq_in2.at[dp], sq2_ss.at[q], sq2_rs.at[q], at_dp(*dp_offs[q]))

    for q in range(15):
        send_sq(q).wait_recv()
    sq_sum[...] = jnp.sum(sq_in[...], axis=0)
    for q in range(7):
        send_sq2(q).start()
    sq_in2[dp] = sq_sum[...]
    for h in (0, 1):
        for i in range(8):
            hid_t[i * FB : (i + 1) * FB, h * TH : (h + 1) * TH] = hid_all[h, :, i * FB : (i + 1) * FB].T

    second_step(2)
    for q in range(7):
        send_sq2(q).wait_recv()
    mean = jnp.sum(sq_in2[...], axis=0)[:1, :] / D
    inv_row = lax.rsqrt(mean + 1e-05)
    for h in (0, 1):
        for i in (0, 1):
            at = h * TH + i * FB
            inv_s[h, i * FB : (i + 1) * FB, :] = jnp.broadcast_to(inv_row[:, at : at + FB], (FB, FB)).T

    rs_end(0)
    rs_end(1)
    softmax(0)
    second_step(3)
    forward(0)
    rs_end(2)
    rs_end(3)
    softmax(1)
    forward(1)
    statistics(0)
    ag_end(0)
    ag_end(1)
    factors(0)
    product(0, whole_tile(0), core2_ss, core2_rs, 1)
    forward(2)
    product(0, whole_tile(0), core2_ss, core2_rs, 0)
    exchange(0, core2_ss, core2_rs, mp2_ss, mp2_rs, GRAD_BOUND)
    statistics(1)
    forward(3)
    ag_end(2)
    early_part(1)
    pre_gradient(0)
    factors(1)
    ag_end(3)
    product(1, late_tile(1), core2_ss, core2_rs, 1)
    gather_mid(dpf, 0, *dp_sems)
    product(1, late_tile(1), core2_ss, core2_rs, 0)
    exchange(1, core2_ss, core2_rs, mp2_ss, mp2_rs, GRAD_BOUND)
    loss = jnp.zeros((TR, 1), F32)
    for h in (0, 1):
        for b in range(8):
            loss = loss + sc_all[h, b][:, 2:3]
    loss_ref[...] = jnp.sum(loss, axis=0, keepdims=True) / T
    gather_end(dpf, 0, *dp_sems)
    pre_gradient(1)

    def grad_copy(n, col):
        return pltpu.make_async_copy(w_flat.at[:, col], grad_ref.at[:, col], out_sem.at[n])

    def grad_tile(n, core, dy):
        first = core * 8 + lax.rem(y + 4 - dy, 4) * 2
        col = pl.ds(pl.multiple_of(first * FB, 2 * FB), 2 * FB)
        r = dot(hid_t[:, :TH], dpf[0, :, col], NN) + dot(hid_t[:, TH:], dpf[1, :, col], NN)
        w_flat[:, col] = r.astype(BF)
        grad_copy(n, col).start()
        return n, col

    tiles = []
    for dy in (0, 1, 3, 2):
        for k in (dy * 2, dy * 2 + 1):
            if k:
                ag_copy(dpf, 1, dp_ss, dp_rs, k).wait_recv()
                ag_pass(dpf, 1, dpc_ss, dpc_rs, k).start()
        tiles.append(grad_tile(len(tiles), c, dy))
    for dy in (0, 1, 3, 2):
        for k in (dy * 2, dy * 2 + 1):
            ag_pass(dpf, 1, dpc_ss, dpc_rs, k).wait_recv()
        tiles.append(grad_tile(len(tiles), 1 - c, dy))
    for k in range(8):
        ag_pass(dpf, 1, dpc_ss, dpc_rs, k).wait_send()
    for k in mp_offs:
        ag_copy(dpf, 1, dp_ss, dp_rs, k).wait_send()

    for q in range(7):
        send_sq2(q).wait_send()
        for h in (0, 1):
            send_hid(q, h).wait_send()
            send_sc(h, q).wait_send()
    for q in range(15):
        send_sq(q).wait_send()
        for h in (0, 1):
            send_st(h, q).wait_send()

    def drain(g, carry):
        rx2_copy(g).wait_send()
        azz_copy(g).wait_send()
        axz_copy(g).wait_send()
        for d in range(4):
            rz_copy(g, d).wait_send()
        for d in (1, 2, 3):
            rx_copy(g, d).wait_send()
            rz2_copy(g, d).wait_send()
            az_copy(g, d).wait_send()
            azf_copy(g, d).wait_send()
            ax_copy(g, d).wait_send()
            axf_copy(g, d).wait_send()
        return carry

    lax.fori_loop(0, NG, drain, 0)
    for n, col in tiles:
        grad_copy(n, col).wait()


def head(hidden, weight, gain, embed, targets):
    vm = pltpu.VMEM
    dma = pltpu.SemaphoreType.DMA
    scratch = [
        vm((V, 2048), BF), vm((1024, 2048), BF), vm((4, ROWS, 16, FB), BF), vm((2, TH, 1024), BF), vm((1024, T), BF),
        vm((2, 8, TH, FB), BF), vm((2, 16, TH, FB), F32), vm((2, 8, TH, FB), BF), vm((2, 8, TH, FB), jnp.int16),
        vm((2, 8, TH, FB), jnp.int16), vm((2, TH, 2048), BF), vm((2, TH, FB), F32), vm((2, TH, FB), F32),
        vm((2, TH, FB), F32), vm((2, TH, FB), F32), vm((2, TH, FB), BF), vm((2, TH, 2048), BF), vm((2, TH, 2048), BF),
        vm((8, T), F32), vm((16, 8, T), F32), vm((8, T), F32), vm((8, 8, T), F32), vm((2, TH, FB), F32),
        vm((NG, TH, HALF), BF), vm((NG, TH, HALF), BF),
        vm((NG, 3, 2 * TR, HALF), BF), vm((NG, 4, TR, HALF), BF),
        vm((NG, TR, HALF), BF), vm((NG, TR, HALF), BF), vm((NG, 3, TR, HALF), BF), vm((NG, 3, TR, HALF), BF),
        vm((2, TR, V), F32), vm((FB, FB), F32), vm((2, 8, FB), F32), vm((2, 16, 8, FB), F32),
        vm((2, 8, TR, FB), F32), vm((2, TH, V), BF),
        dma((4,)), dma((8,)),
    ]
    counts = [
        (7, 2), (2, 4), (2, 8), (2, 4), (2, 8), (2, 8), (2, 8), (2, 8), (2, 8), (15,), (7,), (2, 15), (2, 7),
        (NG, 3), (NG, 4), (NG,), (NG, 3),
        (NG, 3), (NG,), (NG, 3), (NG, 3), (NG, 3), (NG,),
    ]
    for n in counts:
        scratch += [dma(n), dma(n)]
    vspec = pl.BlockSpec(memory_space=pltpu.VMEM)
    anyspec = pl.BlockSpec(memory_space=pl.ANY)
    return pl.pallas_call(
        head_kernel,
        name="head",
        out_shape=(jax.ShapeDtypeStruct((1024, 2048), BF), jax.ShapeDtypeStruct((1, 1), F32)),
        in_specs=[vspec, anyspec, vspec, anyspec, vspec],
        out_specs=(anyspec, vspec),
        scratch_shapes=scratch,
        compiler_params=pltpu.CompilerParams(
            collective_id=0, has_side_effects=True, vmem_limit_bytes=62 << 20
        ),
    )(hidden, weight, gain, embed, targets)


def order_kernel(grad, out):
    blocks = jnp.stack([grad[:, ((j % 2) * 8 + j // 2) * FB :][:, :FB] for j in range(16)])
    out[...] = pltpu.einshape("jvl->vjl", blocks)


def in_order(grad):
    rows = 128
    return pl.pallas_call(
        order_kernel,
        name="in_order",
        grid=(1024 // rows,),
        out_shape=jax.ShapeDtypeStruct((1024, 16, FB), BF),
        in_specs=[pl.BlockSpec((rows, 2048), lambda i: (i, 0))],
        out_specs=pl.BlockSpec((rows, 16, FB), lambda i: (i, 0, 0)),
        compiler_params=pltpu.CompilerParams(vmem_limit_bytes=62 << 20),
    )(grad)


def on_device(hidden_rows, head_weight, norm_gain, vocab_embed, targets):
    grad, loss = head(
        hidden_rows,
        head_weight.reshape(1024, 16, FB),
        norm_gain.reshape(1, FB),
        vocab_embed.reshape(V, 16, FB),
        targets.reshape(1, T),
    )
    return in_order(grad).reshape(head_weight.shape), loss.reshape(())


def solution(mesh):
    return jax.shard_map(
        on_device,
        mesh=mesh,
        in_specs=(
            P("dp", "mp"),
            P("mp", None, "dp", None),
            P("mp", "dp", None),
            P("mp", None, "dp", None),
            P(),
        ),
        out_specs=(P("mp", None, "dp", None), P()),
        check_vma=False,
    )
```

```python
import jax
import jax.numpy as jnp
from jax import lax
from jax.experimental import pallas as pl
from jax.experimental.pallas import tpu as pltpu
from jax.sharding import PartitionSpec as P

MESH = pl.DeviceIdType.MESH
BF = jnp.bfloat16
F32 = jnp.float32
T, D, V, FB = 512, 16384, 4096, 128
TH = T // 2
TR = 32
CH = 2048
HALF = 1024
NG = 4
ROWS = 256
CODE = 32000.0
PRE_BOUND = 60.0 * 0.046875 * 2048 * 1.01
GRAD_BOUND = 6.0 * 2 / T * 1.01
NT = (((1,), (1,)), ((), ()))
NN = (((1,), (0,)), ((), ()))


def dot(a, b, dims):
    return lax.dot_general(a, b, dims, preferred_element_type=F32)


def head_kernel(
    hid_ref, w_ref, gain_ref, e_ref, tgt_ref,
    grad_ref, loss_ref,
    e_flat, w_flat, stage, hid_all, hid_t, ps, acc, core_in, ps2, mp_in, oh, ct, tcol,
    pre_s, act_s, nb, nf, dpf, sq_own, sq_in, sq_sum, sq_in2, inv_s,
    lz, lx, rx, rz, sx2, rx2, sz2, rz2, lg, tsq, st_own, st_in, sc_all, dl,
    stage_sem, out_sem,
    hid_ss, hid_rs, core_ss, core_rs, mp_ss, mp_rs, core2_ss, core2_rs, mp2_ss, mp2_rs,
    nf_ss, nf_rs, nfc_ss, nfc_rs, dp_ss, dp_rs, dpc_ss, dpc_rs,
    sq_ss, sq_rs, sq2_ss, sq2_rs, st_ss, st_rs, sc_ss, sc_rs,
    rx_ss, rx_rs, rz_ss, rz_rs, rx2_ss, rx2_rs, rz2_ss, rz2_rs,
    az_ss, az_rs, azz_ss, azz_rs, ax_ss, ax_rs, axf_ss, axf_rs, azf_ss, azf_rs, axz_ss, axz_rs,
):
    dp = lax.axis_index("dp")
    mp = lax.axis_index("mp")
    x, zl = lax.rem(dp, 4), dp // 4
    yz, c = mp // 2, lax.rem(mp, 2)
    y, zh = yz // 2, lax.rem(yz, 2)
    pos = x * 2 + zl

    def at_dp(dx, dz):
        return (lax.rem(zl + dz, 2) * 4 + lax.rem(x + dx, 4), mp)

    def at_mp(k, dc=0):
        return (dp, yz_of(k) * 2 + lax.rem(c + dc, 2))

    def yz_of(k):
        return lax.rem(y + k // 2, 4) * 2 + lax.rem(zh + k % 2, 2)

    def yz_from(k):
        return lax.rem(y + 4 - k // 2, 4) * 2 + lax.rem(zh + k % 2, 2)

    zpeer = at_dp(0, 1)
    sibling = at_mp(0, 1)
    dp_offs = [(k % 4, k // 4) for k in (6, 2, 5, 7, 1, 3, 4)]
    mp_offs = [5, 4, 3, 7, 2, 6, 1]
    mp15 = [(k, 1) for k in [*mp_offs, 0]] + [(k, 0) for k in mp_offs]

    def rc(src, dst, ss, rs, dev):
        return pltpu.make_async_remote_copy(
            src_ref=src, dst_ref=dst, send_sem=ss, recv_sem=rs, device_id=dev, device_id_type=MESH
        )

    def load_w(i):
        return pltpu.make_async_copy(w_ref.at[pl.ds(i * ROWS, ROWS)], stage.at[i], stage_sem.at[i])

    def load_e(i):
        slot = lax.rem(i, 4)
        return pltpu.make_async_copy(
            e_ref.at[pl.ds(i * ROWS, ROWS)], stage.at[slot], stage_sem.at[slot]
        )

    for i in range(4):
        load_w(i).start()

    barrier = pltpu.get_barrier_semaphore()
    for o in dp_offs:
        pl.semaphore_signal(barrier, inc=1, device_id=at_dp(*o), device_id_type=MESH)
    for k, dc in mp15:
        pl.semaphore_signal(barrier, inc=1, device_id=at_mp(k, dc), device_id_type=MESH)
    pl.semaphore_wait(barrier, len(dp_offs) + len(mp15))

    def tok(p):
        return pl.ds(pl.multiple_of(p * TR, TR), TR)

    def send_hid(q, h):
        return rc(
            hid_ref.at[pl.ds(h * TR, TR)], hid_all.at[h, tok(pos)],
            hid_ss.at[q, h], hid_rs.at[q, h], at_dp(*dp_offs[q]),
        )

    for h in (0, 1):
        for q in range(7):
            send_hid(q, h).start()
        hid_all[h, tok(pos), :] = hid_ref[h * TR : (h + 1) * TR, :]

    def relay(slot, out, first):
        def body(i, carry):
            r = pltpu.einshape("vjl->jvl", stage[slot, pl.ds(pl.multiple_of(i * 64, 64), 64)])
            s = pl.multiple_of(first + i * 64, 64)
            for j in range(16):
                at = ((j % 2) * 8 + j // 2) * FB
                out[pl.ds(s, 64), at : at + FB] = r[j]
            return carry

        lax.fori_loop(0, ROWS // 64, body, 0)

    def relay_e(i, carry):
        load_e(i).wait()
        relay(lax.rem(i, 4), e_flat, i * ROWS)

        @pl.when(i + 4 < V // ROWS)
        def _():
            load_e(i + 4).start()

        return carry

    for i in range(4):
        load_w(i).wait()
        relay(i, w_flat, i * ROWS)
        load_e(i).start()

    local_tgt = tgt_ref[...].astype(F32) - (mp * V).astype(F32)
    for i in range(4):
        part = jnp.broadcast_to(local_tgt[:, i * FB : (i + 1) * FB], (FB, FB)).T
        for j in (0, 1):
            block = i * 2 + j
            at = ((block % 4) * 2 + block // 4) * TR
            for h in (0, 1):
                first = j * 64 + h * TR
                tcol[h, at : at + TR, :] = part[first : first + TR, :]

    def zcol(i):
        return pl.ds(pl.multiple_of(i * CH, CH), HALF)

    def xcol(i):
        return pl.ds(pl.multiple_of(i * CH + HALF, HALF), HALF)

    for h in (0, 1):
        for i in (0, 1):
            ids = (lax.broadcasted_iota(jnp.int32, (TH, HALF), 1) + i * CH).astype(F32)
            want = tcol[h, :, :1]
            lz[h * 2 + i] = (ids == want).astype(BF)
            lx[h * 2 + i] = (ids + HALF == want).astype(BF)

    def pick_body(n, carry):
        col = pl.ds(pl.multiple_of(n * 256, 256), 256)
        for h in (0, 1):
            r = jnp.zeros((TH, 256), F32)
            for i in (0, 1):
                r = r + dot(lz[h * 2 + i], e_flat[i * CH : i * CH + HALF, col], NN)
                r = r + dot(lx[h * 2 + i], e_flat[i * CH + HALF : (i + 1) * CH, col], NN)
            oh[h, :, col] = r.astype(BF)
        return carry

    lax.fori_loop(0, 8, relay_e, 0)

    def core_copy(h, ss, rs, t):
        two = pl.ds(t * 2, 2)
        return rc(ps.at[h, two], core_in.at[h, two], ss.at[h, t], rs.at[h, t], sibling)

    def mp_copy(h, ss, rs, k):
        return rc(ps2.at[h, yz_of(k)], mp_in.at[h, k], ss.at[h, k], rs.at[h, k], at_mp(k))

    def product(h, tile, css, crs, side):
        who = lax.rem(c + side, 2)

        def body(t, carry):
            first = who * 8 + t * 2
            r = tile(first, pl.ds(pl.multiple_of(first * FB, 2 * FB), 2 * FB))
            if side:
                ps[h, t * 2] = r[:, :FB].astype(BF)
                ps[h, t * 2 + 1] = r[:, FB:].astype(BF)
                core_copy(h, css, crs, t).start()
            else:
                acc[h, first] = r[:, :FB]
                acc[h, first + 1] = r[:, FB:]
            return carry

        lax.fori_loop(0, 4, body, 0)

    def encode(v, bound):
        root = lax.rsqrt(lax.rsqrt(jnp.abs(v) * (CODE**4 / bound)))
        code = (root + 0.5).astype(jnp.int32)
        return jnp.where(v < 0, -code, code).astype(jnp.int16)

    def decode(code, bound):
        root = code.astype(F32) * (1.0 / CODE)
        return root * jnp.abs(root) * (root * root) * bound

    def exchange(h, css, crs, mss, mrs, bound):
        for t in range(4):
            core_copy(h, css, crs, t).wait_recv()
        for k in mp_offs:
            b = yz_of(k)
            ps2[h, b] = encode(acc[h, c * 8 + b] + core_in[h, b].astype(F32), bound)
            mp_copy(h, mss, mrs, k).start()

    def collect(h, css, crs, mss, mrs, bound):
        total = acc[h, c * 8 + yz] + core_in[h, yz].astype(F32)
        for k in mp_offs:
            mp_copy(h, mss, mrs, k).wait_recv()
            total = total + decode(mp_in[h, k], bound)
        for k in mp_offs:
            mp_copy(h, mss, mrs, k).wait_send()
        for t in range(4):
            core_copy(h, css, crs, t).wait_send()
        return total

    for h in (0, 1):
        for q in range(7):
            send_hid(q, h).wait_recv()
        for side in (1, 0):
            product(h, lambda first, col, h=h: dot(hid_all[h], w_flat[:, col], NN), core_ss, core_rs, side)
        exchange(h, core_ss, core_rs, mp_ss, mp_rs, PRE_BOUND)

    lax.fori_loop(8, V // ROWS, relay_e, 0)
    lax.fori_loop(0, 2, pick_body, 0)

    gain = gain_ref[...]

    def cols(core, b):
        return pl.ds(pl.multiple_of((core * 8 + b) * FB, FB), FB)

    def ag_copy(buf, h, ss, rs, k):
        return rc(nb.at[h], buf.at[h, :, cols(c, yz)], ss.at[h, k], rs.at[h, k], at_mp(k))

    def ag_pass(buf, h, ss, rs, k):
        at = buf.at[h, :, cols(c, yz_from(k))]
        return rc(nb.at[h] if k == 0 else at, at, ss.at[h, k], rs.at[h, k], sibling)

    def gather_start(buf, h, ss, rs, css, crs):
        for k in mp_offs:
            ag_copy(buf, h, ss, rs, k).start()
        ag_pass(buf, h, css, crs, 0).start()
        buf[h, :, cols(c, yz)] = nb[h]

    def gather_mid(buf, h, ss, rs, css, crs):
        for k in reversed(mp_offs):
            ag_copy(buf, h, ss, rs, k).wait_recv()
            ag_pass(buf, h, css, crs, k).start()

    def gather_end(buf, h, ss, rs, css, crs):
        for k in range(8):
            ag_pass(buf, h, css, crs, k).wait_recv()
        for k in range(8):
            ag_pass(buf, h, css, crs, k).wait_send()
        for k in mp_offs:
            ag_copy(buf, h, ss, rs, k).wait_send()

    nf_sems = (nf_ss, nf_rs, nfc_ss, nfc_rs)
    dp_sems = (dp_ss, dp_rs, dpc_ss, dpc_rs)

    def activate(h):
        pre = collect(h, core_ss, core_rs, mp_ss, mp_rs, PRE_BOUND)
        pre_s[h] = pre
        own = hid_all[h, :, pl.ds(pl.multiple_of(dp * FB, FB), FB)].astype(F32)
        act = own + pre / (1.0 + jnp.exp(-pre))
        act_s[h] = act
        nb[h] = (act * gain).astype(BF)
        gather_start(nf, h, *nf_sems)
        squares = act * act
        for i in (0, 1):
            row = jnp.sum(squares[i * FB : (i + 1) * FB, :].T, axis=0, keepdims=True)
            at = h * TH + i * FB
            sq_own[:, at : at + FB] = jnp.broadcast_to(row, (8, FB))

    def send_sq(q):
        k, dc = mp15[q]
        return rc(sq_own, sq_in.at[mp], sq_ss.at[q], sq_rs.at[q], at_mp(k, dc))

    activate(0)
    lax.fori_loop(2, 4, pick_body, 0)
    activate(1)
    for q in range(15):
        send_sq(q).start()
    sq_in[mp] = sq_own[...]
    lax.fori_loop(4, 6, pick_body, 0)
    gather_mid(nf, 0, *nf_sems)
    lax.fori_loop(6, 8, pick_body, 0)
    gather_end(nf, 0, *nf_sems)

    def rows_of(xx, zz):
        return tok(xx * 2 + zz)

    def xd(d):
        return lax.rem(x + d, 4)

    def rz_copy(g, d):
        return rc(
            lz.at[g, rows_of(xd(d), 1 - zl)], rz.at[g, d], rz_ss.at[g, d], rz_rs.at[g, d], zpeer
        )

    def rx_copy(g, d):
        src = lx.at[g, pl.ds(pl.multiple_of(xd(d) * 2 * TR, 2 * TR), 2 * TR)]
        return rc(src, rx.at[g, d - 1], rx_ss.at[g, d - 1], rx_rs.at[g, d - 1], at_dp(d, 0))

    def rx2_copy(g):
        return rc(sx2.at[g], rx2.at[g], rx2_ss.at[g], rx2_rs.at[g], zpeer)

    def rz2_copy(g, d):
        return rc(
            sz2.at[g, d - 1], rz2.at[g, d - 1], rz2_ss.at[g, d - 1], rz2_rs.at[g, d - 1], at_dp(d, 0)
        )

    def logits_chunk(g):
        h, i = g // 2, g % 2
        lz[g] = dot(nf[h], e_flat[i * CH : i * CH + HALF, :], NT).astype(BF)
        for d in (2, 1, 3, 0):
            rz_copy(g, d).start()
        lx[g] = dot(nf[h], e_flat[i * CH + HALF : (i + 1) * CH, :], NT).astype(BF)
        for d in (2, 1, 3):
            rx_copy(g, d).start()

    def second_step(g):
        h, i = g // 2, g % 2
        for d in (1, 3, 2):
            rx_copy(g, d).wait_recv()
        base = pl.multiple_of(x * 2 * TR, 2 * TR)
        for mine in (False, True):
            off = pl.multiple_of((zl if mine else 1 - zl) * TR, TR)
            s = lx[g, pl.ds(base + off, TR)].astype(F32)
            for d in range(3):
                s = s + rx[g, d, pl.ds(off, TR)].astype(F32)
            if mine:
                lg[h, :, xcol(i)] = s
            else:
                sx2[g] = s.astype(BF)
                rx2_copy(g).start()
        for d in (2, 1, 3, 0):
            rz_copy(g, d).wait_recv()
            s = lz[g, rows_of(xd(d), zl)].astype(F32) + rz[g, d].astype(F32)
            if d:
                sz2[g, d - 1] = s.astype(BF)
                rz2_copy(g, d).start()
            else:
                lg[h, :, zcol(i)] = s

    def rs_end(g):
        h, i = g // 2, g % 2
        rx2_copy(g).wait_recv()
        lg[h, :, xcol(i)] = lg[h, :, xcol(i)] + rx2[g].astype(F32)
        s = lg[h, :, zcol(i)]
        for d in (1, 3, 2):
            rz2_copy(g, d).wait_recv()
            s = s + rz2[g, d - 1].astype(F32)
        lg[h, :, zcol(i)] = s

    def dl_at(h, xx, zz, col):
        return dl.at[h, rows_of(xx, zz), col]

    def az_copy(g, d):
        a = dl_at(g // 2, x, zl, zcol(g % 2))
        return rc(a, a, az_ss.at[g, d - 1], az_rs.at[g, d - 1], at_dp(d, 0))

    def azz_copy(g):
        a = dl_at(g // 2, x, zl, zcol(g % 2))
        return rc(a, a, azz_ss.at[g], azz_rs.at[g], zpeer)

    def azf_copy(g, d):
        a = dl_at(g // 2, lax.rem(x + 4 - d, 4), zl, zcol(g % 2))
        return rc(a, a, azf_ss.at[g, d - 1], azf_rs.at[g, d - 1], zpeer)

    def ax_copy(g, d):
        a = dl_at(g // 2, x, zl, xcol(g % 2))
        return rc(a, a, ax_ss.at[g, d - 1], ax_rs.at[g, d - 1], at_dp(d, 0))

    def axz_copy(g):
        a = dl_at(g // 2, x, zl, xcol(g % 2))
        return rc(a, a, axz_ss.at[g], axz_rs.at[g], zpeer)

    def axf_copy(g, d):
        a = dl_at(g // 2, x, 1 - zl, xcol(g % 2))
        return rc(a, a, axf_ss.at[g, d - 1], axf_rs.at[g, d - 1], at_dp(d, 0))

    lane = lax.broadcasted_iota(jnp.int32, (TR, FB), 1)

    def send_st(h, q):
        k, dc = mp15[q]
        return rc(st_own.at[h], st_in.at[h, mp], st_ss.at[h, q], st_rs.at[h, q], at_mp(k, dc))

    def softmax(h):
        inv_own = inv_s[h, tok(pos), :][:, :1]
        want = tcol[h, tok(pos), :][:, :1]
        m = jnp.full((TR, 1), -jnp.inf, F32)
        for j in range(V // HALF):
            v = lg[h, :, j * HALF : (j + 1) * HALF] * inv_own
            lg[h, :, j * HALF : (j + 1) * HALF] = v
            m = jnp.maximum(m, jnp.max(v, axis=1, keepdims=True))
        s, sl, pk = (jnp.zeros((TR, 1), F32) for _ in range(3))
        for j in range(V // HALF):
            ids = (lax.broadcasted_iota(jnp.int32, (TR, HALF), 1) + j * HALF).astype(F32)
            v = lg[h, :, j * HALF : (j + 1) * HALF]
            p = jnp.exp(v - m)
            dl[h, tok(pos), j * HALF : (j + 1) * HALF] = p.astype(BF)
            g = h * 2 + j // 2
            if j % 2:
                axz_copy(g).start()
                for d in (2, 1, 3):
                    ax_copy(g, d).start()
            else:
                for d in (2, 1, 3):
                    az_copy(g, d).start()
                azz_copy(g).start()
            s = s + jnp.sum(p, axis=1, keepdims=True)
            sl = sl + jnp.sum(p * v, axis=1, keepdims=True)
            pk = pk + jnp.sum(jnp.where(ids == want, v, 0.0), axis=1, keepdims=True)
        tsq[...] = jnp.zeros((FB, FB), F32)
        tsq[:TR, :] = jnp.where(
            lane == 0, m, jnp.where(lane == 1, s, jnp.where(lane == 2, sl, jnp.where(lane == 3, pk, 0.0)))
        )
        st_own[h] = tsq[...].T[:8, :]
        for q in range(15):
            send_st(h, q).start()
        st_in[h, mp] = st_own[h]

    def forward(g):
        axz_copy(g).wait_recv()
        for d in (2, 1, 3):
            axf_copy(g, d).start()
        for d in (1, 3, 2):
            az_copy(g, d).wait_recv()
            azf_copy(g, d).start()

    def ag_end(g):
        azz_copy(g).wait_recv()
        for d in (1, 3, 2):
            ax_copy(g, d).wait_recv()
            axf_copy(g, d).wait_recv()
            azf_copy(g, d).wait_recv()

    def send_sc(h, q):
        a = sc_all.at[h, pos]
        return rc(a, a, sc_ss.at[h, q], sc_rs.at[h, q], at_dp(*dp_offs[q]))

    def statistics(h):
        for q in range(15):
            send_st(h, q).wait_recv()
        all_m = st_in[h, :, 0, :]
        top = jnp.max(all_m, axis=0, keepdims=True)
        scale = jnp.exp(all_m - top)
        total = jnp.sum(st_in[h, :, 1, :] * scale, axis=0, keepdims=True)
        total_l = jnp.sum(st_in[h, :, 2, :] * scale, axis=0, keepdims=True)
        picked = jnp.sum(st_in[h, :, 3, :], axis=0, keepdims=True)
        valid = lax.broadcasted_iota(jnp.int32, (1, FB), 1) < TR
        total = jnp.where(valid, total, 1.0)
        lse = top + jnp.log(total)
        moment = (total_l / total - picked) / T
        factor = jnp.exp(st_own[h, :1, :] - lse) / T
        sub = lax.broadcasted_iota(jnp.int32, (FB, FB), 0)
        table = jnp.where(sub == 0, factor, jnp.where(sub == 1, moment, jnp.where(sub == 2, lse - picked, 0.0)))
        tsq[...] = table.T
        sc_all[h, pos] = tsq[:TR, :]
        for q in range(7):
            send_sc(h, q).start()

    def factors(h):
        for q in range(7):
            send_sc(h, q).wait_recv()
        for b in range(8):
            ct[h, b * TR : (b + 1) * TR, :] = jnp.broadcast_to(sc_all[h, b][:, 0:1], (TR, FB))

    def scaled_tile(h, first, col, r):
        f = ct[h]
        own_row = oh[h, :, col].astype(F32) / T
        return jnp.concatenate(
            [r[:, b * FB : (b + 1) * FB] * f - own_row[:, b * FB : (b + 1) * FB] for b in (0, 1)], axis=1
        )

    def early_part(h):
        def body(t, carry):
            r = dot(dl[h, :, :CH], e_flat[:CH, pl.ds(pl.multiple_of(t * 256, 256), 256)], NN)
            acc[h, t * 2] = r[:, :FB]
            acc[h, t * 2 + 1] = r[:, FB:]
            return carry

        lax.fori_loop(0, 8, body, 0)

    def late_tile(h):
        def tile(first, col):
            r = dot(dl[h, :, CH:], e_flat[CH:, col], NN)
            return scaled_tile(h, first, col, r + jnp.concatenate([acc[h, first], acc[h, first + 1]], axis=1))

        return tile

    def whole_tile(h):
        return lambda first, col: scaled_tile(h, first, col, dot(dl[h], e_flat[:, col], NN))

    def pre_gradient(h):
        dnormed = collect(h, core2_ss, core2_rs, mp2_ss, mp2_rs, GRAD_BOUND)
        moments = jnp.concatenate([sc_all[h, b][:, 1:2] for b in range(8)], axis=0)
        inv, act, pre = inv_s[h], act_s[h], pre_s[h]
        dact = inv * gain * dnormed - act * (inv * inv * (moments / D))
        sig = 1.0 / (1.0 + jnp.exp(-pre))
        nb[h] = (dact * sig * (1.0 + pre * (1.0 - sig))).astype(BF)
        gather_start(dpf, h, *dp_sems)

    def send_sq2(q):
        return rc(sq_sum, sq_in2.at[dp], sq2_ss.at[q], sq2_rs.at[q], at_dp(*dp_offs[q]))

    def send_squares():
        for q in range(15):
            send_sq(q).wait_recv()
        sq_sum[...] = jnp.sum(sq_in[...], axis=0)
        for q in range(7):
            send_sq2(q).start()
        sq_in2[dp] = sq_sum[...]

    def norms():
        for q in range(7):
            send_sq2(q).wait_recv()
        mean = jnp.sum(sq_in2[...], axis=0)[:1, :] / D
        inv_row = lax.rsqrt(mean + 1e-05)
        for h in (0, 1):
            for i in (0, 1):
                at = h * TH + i * FB
                inv_s[h, i * FB : (i + 1) * FB, :] = jnp.broadcast_to(inv_row[:, at : at + FB], (FB, FB)).T

    logits_chunk(0)
    logits_chunk(1)
    gather_mid(nf, 1, *nf_sems)
    send_squares()
    gather_end(nf, 1, *nf_sems)
    logits_chunk(2)
    second_step(0)
    logits_chunk(3)
    second_step(1)
    norms()
    second_step(2)
    rs_end(0)
    rs_end(1)
    softmax(0)
    second_step(3)
    forward(0)
    forward(1)
    rs_end(2)
    rs_end(3)
    softmax(1)
    statistics(0)
    ag_end(0)
    ag_end(1)
    factors(0)
    product(0, whole_tile(0), core2_ss, core2_rs, 1)
    product(0, whole_tile(0), core2_ss, core2_rs, 0)
    exchange(0, core2_ss, core2_rs, mp2_ss, mp2_rs, GRAD_BOUND)
    forward(2)
    forward(3)
    statistics(1)
    pre_gradient(0)
    ag_end(2)
    early_part(1)
    factors(1)
    ag_end(3)
    product(1, late_tile(1), core2_ss, core2_rs, 1)
    gather_mid(dpf, 0, *dp_sems)
    product(1, late_tile(1), core2_ss, core2_rs, 0)
    exchange(1, core2_ss, core2_rs, mp2_ss, mp2_rs, GRAD_BOUND)
    for h in (0, 1):
        for i in range(8):
            hid_t[i * FB : (i + 1) * FB, h * TH : (h + 1) * TH] = hid_all[h, :, i * FB : (i + 1) * FB].T
    loss = jnp.zeros((TR, 1), F32)
    for h in (0, 1):
        for b in range(8):
            loss = loss + sc_all[h, b][:, 2:3]
    loss_ref[...] = jnp.sum(loss, axis=0, keepdims=True) / T
    gather_end(dpf, 0, *dp_sems)
    pre_gradient(1)

    def grad_copy(n, col):
        return pltpu.make_async_copy(w_flat.at[:, col], grad_ref.at[:, col], out_sem.at[n])

    def grad_tile(n, core, dy):
        first = core * 8 + lax.rem(y + 4 - dy, 4) * 2
        col = pl.ds(pl.multiple_of(first * FB, 2 * FB), 2 * FB)
        r = dot(hid_t[:, :TH], dpf[0, :, col], NN) + dot(hid_t[:, TH:], dpf[1, :, col], NN)
        w_flat[:, col] = r.astype(BF)
        grad_copy(n, col).start()
        return n, col

    tiles = []
    for dy in (0, 1, 3, 2):
        for k in (dy * 2, dy * 2 + 1):
            if k:
                ag_copy(dpf, 1, dp_ss, dp_rs, k).wait_recv()
                ag_pass(dpf, 1, dpc_ss, dpc_rs, k).start()
        tiles.append(grad_tile(len(tiles), c, dy))
    for dy in (0, 1, 3, 2):
        for k in (dy * 2, dy * 2 + 1):
            ag_pass(dpf, 1, dpc_ss, dpc_rs, k).wait_recv()
        tiles.append(grad_tile(len(tiles), 1 - c, dy))
    for k in range(8):
        ag_pass(dpf, 1, dpc_ss, dpc_rs, k).wait_send()
    for k in mp_offs:
        ag_copy(dpf, 1, dp_ss, dp_rs, k).wait_send()

    for q in range(7):
        send_sq2(q).wait_send()
        for h in (0, 1):
            send_hid(q, h).wait_send()
            send_sc(h, q).wait_send()
    for q in range(15):
        send_sq(q).wait_send()
        for h in (0, 1):
            send_st(h, q).wait_send()

    def drain(g, carry):
        rx2_copy(g).wait_send()
        azz_copy(g).wait_send()
        axz_copy(g).wait_send()
        for d in range(4):
            rz_copy(g, d).wait_send()
        for d in (1, 2, 3):
            rx_copy(g, d).wait_send()
            rz2_copy(g, d).wait_send()
            az_copy(g, d).wait_send()
            azf_copy(g, d).wait_send()
            ax_copy(g, d).wait_send()
            axf_copy(g, d).wait_send()
        return carry

    lax.fori_loop(0, NG, drain, 0)
    for n, col in tiles:
        grad_copy(n, col).wait()


def head(hidden, weight, gain, embed, targets):
    vm = pltpu.VMEM
    dma = pltpu.SemaphoreType.DMA
    scratch = [
        vm((V, 2048), BF), vm((1024, 2048), BF), vm((4, ROWS, 16, FB), BF), vm((2, TH, 1024), BF), vm((1024, T), BF),
        vm((2, 8, TH, FB), BF), vm((2, 16, TH, FB), F32), vm((2, 8, TH, FB), BF), vm((2, 8, TH, FB), jnp.int16),
        vm((2, 8, TH, FB), jnp.int16), vm((2, TH, 2048), BF), vm((2, TH, FB), F32), vm((2, TH, FB), F32),
        vm((2, TH, FB), F32), vm((2, TH, FB), F32), vm((2, TH, FB), BF), vm((2, TH, 2048), BF), vm((2, TH, 2048), BF),
        vm((8, T), F32), vm((16, 8, T), F32), vm((8, T), F32), vm((8, 8, T), F32), vm((2, TH, FB), F32),
        vm((NG, TH, HALF), BF), vm((NG, TH, HALF), BF),
        vm((NG, 3, 2 * TR, HALF), BF), vm((NG, 4, TR, HALF), BF),
        vm((NG, TR, HALF), BF), vm((NG, TR, HALF), BF), vm((NG, 3, TR, HALF), BF), vm((NG, 3, TR, HALF), BF),
        vm((2, TR, V), F32), vm((FB, FB), F32), vm((2, 8, FB), F32), vm((2, 16, 8, FB), F32),
        vm((2, 8, TR, FB), F32), vm((2, TH, V), BF),
        dma((4,)), dma((8,)),
    ]
    counts = [
        (7, 2), (2, 4), (2, 8), (2, 4), (2, 8), (2, 8), (2, 8), (2, 8), (2, 8), (15,), (7,), (2, 15), (2, 7),
        (NG, 3), (NG, 4), (NG,), (NG, 3),
        (NG, 3), (NG,), (NG, 3), (NG, 3), (NG, 3), (NG,),
    ]
    for n in counts:
        scratch += [dma(n), dma(n)]
    vspec = pl.BlockSpec(memory_space=pltpu.VMEM)
    anyspec = pl.BlockSpec(memory_space=pl.ANY)
    return pl.pallas_call(
        head_kernel,
        name="head",
        out_shape=(jax.ShapeDtypeStruct((1024, 2048), BF), jax.ShapeDtypeStruct((1, 1), F32)),
        in_specs=[vspec, anyspec, vspec, anyspec, vspec],
        out_specs=(anyspec, vspec),
        scratch_shapes=scratch,
        compiler_params=pltpu.CompilerParams(
            collective_id=0, has_side_effects=True, vmem_limit_bytes=62 << 20
        ),
    )(hidden, weight, gain, embed, targets)


def order_kernel(grad, out):
    blocks = jnp.stack([grad[:, ((j % 2) * 8 + j // 2) * FB :][:, :FB] for j in range(16)])
    out[...] = pltpu.einshape("jvl->vjl", blocks)


def in_order(grad):
    rows = 512
    return pl.pallas_call(
        order_kernel,
        name="in_order",
        grid=(1024 // rows,),
        out_shape=jax.ShapeDtypeStruct((1024, 16, FB), BF),
        in_specs=[pl.BlockSpec((rows, 2048), lambda i: (i, 0))],
        out_specs=pl.BlockSpec((rows, 16, FB), lambda i: (i, 0, 0)),
        compiler_params=pltpu.CompilerParams(vmem_limit_bytes=62 << 20),
    )(grad)


def on_device(hidden_rows, head_weight, norm_gain, vocab_embed, targets):
    grad, loss = head(
        hidden_rows,
        head_weight.reshape(1024, 16, FB),
        norm_gain.reshape(1, FB),
        vocab_embed.reshape(V, 16, FB),
        targets.reshape(1, T),
    )
    return in_order(grad).reshape(head_weight.shape), loss.reshape(())


def solution(mesh):
    return jax.shard_map(
        on_device,
        mesh=mesh,
        in_specs=(
            P("dp", "mp"),
            P("mp", None, "dp", None),
            P("mp", "dp", None),
            P("mp", None, "dp", None),
            P(),
        ),
        out_specs=(P("mp", None, "dp", None), P()),
        check_vma=False,
    )
```

```python
import jax
import jax.numpy as jnp
from jax import lax
from jax.experimental import pallas as pl
from jax.experimental.pallas import tpu as pltpu
from jax.sharding import PartitionSpec as P

MESH = pl.DeviceIdType.MESH
BF = jnp.bfloat16
F32 = jnp.float32
T, D, V, FB = 512, 16384, 4096, 128
TH = T // 2
TR = 32
CH = 2048
HALF = 1024
NG = 4
ROWS = 256
CODE = 32000.0
PRE_BOUND = 60.0 * 0.046875 * 2048 * 1.01
GRAD_BOUND = 6.0 * 2 / T * 1.01
NT = (((1,), (1,)), ((), ()))
NN = (((1,), (0,)), ((), ()))


def dot(a, b, dims):
    return lax.dot_general(a, b, dims, preferred_element_type=F32)


def head_kernel(
    hid_ref, w_ref, gain_ref, e_ref, tgt_ref,
    grad_ref, loss_ref,
    e_flat, w_flat, stage, hid_all, hid_t, ps, acc, core_in, ps2, mp_in, oh, ct, tcol,
    pre_s, act_s, nb, nf, dpf, sq_own, sq_in, sq_sum, sq_in2, inv_s,
    lz, lx, rx, rxf, sxc, rz, sx2, rx2, szf, szn, rzf, szc, rz2, lg, tsq, st_own, st_in, sc_all, dl,
    stage_sem, out_sem,
    hid_ss, hid_rs, core_ss, core_rs, mp_ss, mp_rs, core2_ss, core2_rs, mp2_ss, mp2_rs,
    nf_ss, nf_rs, nfc_ss, nfc_rs, dp_ss, dp_rs, dpc_ss, dpc_rs,
    sq_ss, sq_rs, sq2_ss, sq2_rs, st_ss, st_rs, sc_ss, sc_rs,
    rxf_ss, rxf_rs, rxn_ss, rxn_rs, rxc_ss, rxc_rs, rz_ss, rz_rs, rx2_ss, rx2_rs,
    rzf_ss, rzf_rs, rzn_ss, rzn_rs, rzc_ss, rzc_rs,
    az_ss, az_rs, azh_ss, azh_rs, azz_ss, azz_rs, azf_ss, azf_rs, ax_ss, ax_rs, axh_ss, axh_rs,
    axz_ss, axz_rs, axf_ss, axf_rs, axg_ss, axg_rs,
):
    dp = lax.axis_index("dp")
    mp = lax.axis_index("mp")
    x, zl = lax.rem(dp, 4), dp // 4
    yz, c = mp // 2, lax.rem(mp, 2)
    y, zh = yz // 2, lax.rem(yz, 2)
    pos = x * 2 + zl

    def at_dp(dx, dz):
        return (lax.rem(zl + dz, 2) * 4 + lax.rem(x + dx, 4), mp)

    def at_mp(k, dc=0):
        return (dp, yz_of(k) * 2 + lax.rem(c + dc, 2))

    def yz_of(k):
        return lax.rem(y + k // 2, 4) * 2 + lax.rem(zh + k % 2, 2)

    def yz_from(k):
        return lax.rem(y + 4 - k // 2, 4) * 2 + lax.rem(zh + k % 2, 2)

    zpeer = at_dp(0, 1)
    sibling = at_mp(0, 1)
    dp_offs = [(k % 4, k // 4) for k in (6, 2, 5, 7, 1, 3, 4)]
    mp_offs = [5, 4, 3, 7, 2, 6, 1]
    mp15 = [(k, 1) for k in [*mp_offs, 0]] + [(k, 0) for k in mp_offs]

    def rc(src, dst, ss, rs, dev):
        return pltpu.make_async_remote_copy(
            src_ref=src, dst_ref=dst, send_sem=ss, recv_sem=rs, device_id=dev, device_id_type=MESH
        )

    def load_w(i):
        return pltpu.make_async_copy(w_ref.at[pl.ds(i * ROWS, ROWS)], stage.at[i], stage_sem.at[i])

    def load_e(i):
        slot = lax.rem(i, 4)
        return pltpu.make_async_copy(
            e_ref.at[pl.ds(i * ROWS, ROWS)], stage.at[slot], stage_sem.at[slot]
        )

    for i in range(4):
        load_w(i).start()

    barrier = pltpu.get_barrier_semaphore()
    for o in dp_offs:
        pl.semaphore_signal(barrier, inc=1, device_id=at_dp(*o), device_id_type=MESH)
    for k, dc in mp15:
        pl.semaphore_signal(barrier, inc=1, device_id=at_mp(k, dc), device_id_type=MESH)
    pl.semaphore_wait(barrier, len(dp_offs) + len(mp15))

    def tok(p):
        return pl.ds(pl.multiple_of(p * TR, TR), TR)

    def send_hid(q, h):
        return rc(
            hid_ref.at[pl.ds(h * TR, TR)], hid_all.at[h, tok(pos)],
            hid_ss.at[q, h], hid_rs.at[q, h], at_dp(*dp_offs[q]),
        )

    for h in (0, 1):
        for q in range(7):
            send_hid(q, h).start()
        hid_all[h, tok(pos), :] = hid_ref[h * TR : (h + 1) * TR, :]

    def relay(slot, out, first):
        def body(i, carry):
            r = pltpu.einshape("vjl->jvl", stage[slot, pl.ds(pl.multiple_of(i * 64, 64), 64)])
            s = pl.multiple_of(first + i * 64, 64)
            for j in range(16):
                at = ((j % 2) * 8 + j // 2) * FB
                out[pl.ds(s, 64), at : at + FB] = r[j]
            return carry

        lax.fori_loop(0, ROWS // 64, body, 0)

    def relay_e(i, carry):
        load_e(i).wait()
        relay(lax.rem(i, 4), e_flat, i * ROWS)

        @pl.when(i + 4 < V // ROWS)
        def _():
            load_e(i + 4).start()

        return carry

    for i in range(4):
        load_w(i).wait()
        relay(i, w_flat, i * ROWS)
        load_e(i).start()

    local_tgt = tgt_ref[...].astype(F32) - (mp * V).astype(F32)
    for i in range(4):
        part = jnp.broadcast_to(local_tgt[:, i * FB : (i + 1) * FB], (FB, FB)).T
        for j in (0, 1):
            block = i * 2 + j
            at = ((block % 4) * 2 + block // 4) * TR
            for h in (0, 1):
                first = j * 64 + h * TR
                tcol[h, at : at + TR, :] = part[first : first + TR, :]

    def zcol(i):
        return pl.ds(pl.multiple_of(i * CH, CH), HALF)

    def xcol(i):
        return pl.ds(pl.multiple_of(i * CH + HALF, HALF), HALF)

    for h in (0, 1):
        for i in (0, 1):
            ids = (lax.broadcasted_iota(jnp.int32, (TH, HALF), 1) + i * CH).astype(F32)
            want = tcol[h, :, :1]
            lz[h * 2 + i] = (ids == want).astype(BF)
            lx[h * 2 + i] = (ids + HALF == want).astype(BF)

    def pick_body(n, carry):
        col = pl.ds(pl.multiple_of(n * 256, 256), 256)
        for h in (0, 1):
            r = jnp.zeros((TH, 256), F32)
            for i in (0, 1):
                r = r + dot(lz[h * 2 + i], e_flat[i * CH : i * CH + HALF, col], NN)
                r = r + dot(lx[h * 2 + i], e_flat[i * CH + HALF : (i + 1) * CH, col], NN)
            oh[h, :, col] = r.astype(BF)
        return carry

    lax.fori_loop(0, 8, relay_e, 0)

    def core_copy(h, ss, rs, t):
        two = pl.ds(t * 2, 2)
        return rc(ps.at[h, two], core_in.at[h, two], ss.at[h, t], rs.at[h, t], sibling)

    def mp_copy(h, ss, rs, k):
        return rc(ps2.at[h, yz_of(k)], mp_in.at[h, k], ss.at[h, k], rs.at[h, k], at_mp(k))

    def product(h, tile, css, crs, side):
        who = lax.rem(c + side, 2)

        def body(t, carry):
            first = who * 8 + t * 2
            r = tile(first, pl.ds(pl.multiple_of(first * FB, 2 * FB), 2 * FB))
            if side:
                ps[h, t * 2] = r[:, :FB].astype(BF)
                ps[h, t * 2 + 1] = r[:, FB:].astype(BF)
                core_copy(h, css, crs, t).start()
            else:
                acc[h, first] = r[:, :FB]
                acc[h, first + 1] = r[:, FB:]
            return carry

        lax.fori_loop(0, 4, body, 0)

    def encode(v, bound):
        root = lax.rsqrt(lax.rsqrt(jnp.abs(v) * (CODE**4 / bound)))
        code = (root + 0.5).astype(jnp.int32)
        return jnp.where(v < 0, -code, code).astype(jnp.int16)

    def decode(code, bound):
        root = code.astype(F32) * (1.0 / CODE)
        return root * jnp.abs(root) * (root * root) * bound

    def exchange(h, css, crs, mss, mrs, bound):
        for t in range(4):
            core_copy(h, css, crs, t).wait_recv()
        for k in mp_offs:
            b = yz_of(k)
            ps2[h, b] = encode(acc[h, c * 8 + b] + core_in[h, b].astype(F32), bound)
            mp_copy(h, mss, mrs, k).start()

    def collect(h, css, crs, mss, mrs, bound):
        total = acc[h, c * 8 + yz] + core_in[h, yz].astype(F32)
        for k in mp_offs:
            mp_copy(h, mss, mrs, k).wait_recv()
            total = total + decode(mp_in[h, k], bound)
        for k in mp_offs:
            mp_copy(h, mss, mrs, k).wait_send()
        for t in range(4):
            core_copy(h, css, crs, t).wait_send()
        return total

    for h in (0, 1):
        for q in range(7):
            send_hid(q, h).wait_recv()
        for side in (1, 0):
            product(h, lambda first, col, h=h: dot(hid_all[h], w_flat[:, col], NN), core_ss, core_rs, side)
        exchange(h, core_ss, core_rs, mp_ss, mp_rs, PRE_BOUND)

    lax.fori_loop(8, V // ROWS, relay_e, 0)
    lax.fori_loop(0, 2, pick_body, 0)

    gain = gain_ref[...]

    def cols(core, b):
        return pl.ds(pl.multiple_of((core * 8 + b) * FB, FB), FB)

    def ag_copy(buf, h, ss, rs, k):
        return rc(nb.at[h], buf.at[h, :, cols(c, yz)], ss.at[h, k], rs.at[h, k], at_mp(k))

    def ag_pass(buf, h, ss, rs, k):
        at = buf.at[h, :, cols(c, yz_from(k))]
        return rc(nb.at[h] if k == 0 else at, at, ss.at[h, k], rs.at[h, k], sibling)

    def gather_start(buf, h, ss, rs, css, crs):
        for k in mp_offs:
            ag_copy(buf, h, ss, rs, k).start()
        ag_pass(buf, h, css, crs, 0).start()
        buf[h, :, cols(c, yz)] = nb[h]

    def gather_mid(buf, h, ss, rs, css, crs):
        for k in reversed(mp_offs):
            ag_copy(buf, h, ss, rs, k).wait_recv()
            ag_pass(buf, h, css, crs, k).start()

    def gather_end(buf, h, ss, rs, css, crs):
        for k in range(8):
            ag_pass(buf, h, css, crs, k).wait_recv()
        for k in range(8):
            ag_pass(buf, h, css, crs, k).wait_send()
        for k in mp_offs:
            ag_copy(buf, h, ss, rs, k).wait_send()

    nf_sems = (nf_ss, nf_rs, nfc_ss, nfc_rs)
    dp_sems = (dp_ss, dp_rs, dpc_ss, dpc_rs)

    def activate(h):
        pre = collect(h, core_ss, core_rs, mp_ss, mp_rs, PRE_BOUND)
        pre_s[h] = pre
        own = hid_all[h, :, pl.ds(pl.multiple_of(dp * FB, FB), FB)].astype(F32)
        act = own + pre / (1.0 + jnp.exp(-pre))
        act_s[h] = act
        nb[h] = (act * gain).astype(BF)
        gather_start(nf, h, *nf_sems)
        squares = act * act
        for i in (0, 1):
            row = jnp.sum(squares[i * FB : (i + 1) * FB, :].T, axis=0, keepdims=True)
            at = h * TH + i * FB
            sq_own[:, at : at + FB] = jnp.broadcast_to(row, (8, FB))

    def send_sq(q):
        k, dc = mp15[q]
        return rc(sq_own, sq_in.at[mp], sq_ss.at[q], sq_rs.at[q], at_mp(k, dc))

    activate(0)
    lax.fori_loop(2, 4, pick_body, 0)
    activate(1)
    for q in range(15):
        send_sq(q).start()
    sq_in[mp] = sq_own[...]
    lax.fori_loop(4, 6, pick_body, 0)
    gather_mid(nf, 0, *nf_sems)
    lax.fori_loop(6, 8, pick_body, 0)
    gather_end(nf, 0, *nf_sems)

    def rows_of(xx, zz):
        return tok(xx * 2 + zz)

    def xd(d):
        return lax.rem(x + d, 4)

    def rz_copy(g, d):
        return rc(
            lz.at[g, rows_of(xd(d), 1 - zl)], rz.at[g, d], rz_ss.at[g, d], rz_rs.at[g, d], zpeer
        )

    def way(k):
        return at_dp(1 if k == 0 else 3, 0)

    def to(k):
        return xd(1 if k == 0 else 3)

    def source(k):
        return xd(3 if k == 0 else 1)

    def block(xx, half):
        return pl.ds(pl.multiple_of(xx * 2 * TR + half * TR, TR), TR)

    def part(half):
        return pl.ds(half * (TR // 2), TR // 2)

    def pair(ss, rs, g, k):
        return (ss.at[g, k], rs.at[g, k], way(k))

    def rxf_copy(g, k):
        return rc(lx.at[g, block(xd(2), k)], rxf.at[g, k], *pair(rxf_ss, rxf_rs, g, k))

    def rxn_copy(g, k):
        here = pl.ds((1 - k) * TR, TR)
        return rc(lx.at[g, block(to(k), 1 - k)], rx.at[g, k, here], *pair(rxn_ss, rxn_rs, g, k))

    def rxc_copy(g, k):
        return rc(sxc.at[g, k], rx.at[g, k, pl.ds(k * TR, TR)], *pair(rxc_ss, rxc_rs, g, k))

    def rx2_copy(g):
        return rc(sx2.at[g], rx2.at[g], rx2_ss.at[g], rx2_rs.at[g], zpeer)

    def rzf_copy(g, k):
        return rc(szf.at[g, part(k)], rzf.at[g, k], *pair(rzf_ss, rzf_rs, g, k))

    def rzn_copy(g, k):
        return rc(szn.at[g, k], rz2.at[g, k, part(1 - k)], *pair(rzn_ss, rzn_rs, g, k))

    def rzc_copy(g, k):
        return rc(szc.at[g, k], rz2.at[g, k, part(k)], *pair(rzc_ss, rzc_rs, g, k))

    def logits_chunk(g):
        h, i = g // 2, g % 2
        lx[g] = dot(nf[h], e_flat[i * CH + HALF : (i + 1) * CH, :], NT).astype(BF)
        for k in (0, 1):
            rxf_copy(g, k).start()
        for k in (0, 1):
            rxn_copy(g, k).start()
        lz[g] = dot(nf[h], e_flat[i * CH : i * CH + HALF, :], NT).astype(BF)
        for d in (2, 1, 3, 0):
            rz_copy(g, d).start()

    def combine_x(g):
        for k in (0, 1):
            rxf_copy(g, k).wait_recv()
            sxc[g, k] = (lx[g, block(to(k), k)].astype(F32) + rxf[g, k].astype(F32)).astype(BF)
            rxc_copy(g, k).start()

    def z_sum(g, d, rows):
        first = pl.multiple_of((xd(d) * 2 + zl) * TR + rows[0], TR // 2)
        return lz[g, pl.ds(first, rows[1])].astype(F32) + rz[g, d, rows[0] : rows[0] + rows[1]].astype(F32)

    def second_step(g):
        h, i = g // 2, g % 2
        rz_copy(g, 2).wait_recv()
        szf[g] = z_sum(g, 2, (0, TR)).astype(BF)
        for k in (0, 1):
            rzf_copy(g, k).start()
        for k in (0, 1):
            d = 1 if k == 0 else 3
            rz_copy(g, d).wait_recv()
            szn[g, k] = z_sum(g, d, ((1 - k) * (TR // 2), TR // 2)).astype(BF)
            rzn_copy(g, k).start()
        rz_copy(g, 0).wait_recv()
        lg[h, :, zcol(i)] = z_sum(g, 0, (0, TR))
        for k in (0, 1):
            rxn_copy(g, k).wait_recv()
            rxc_copy(g, k).wait_recv()
        for mine in (False, True):
            zz = zl if mine else 1 - zl
            off = pl.multiple_of(zz * TR, TR)
            s = lx[g, block(x, zz)].astype(F32)
            for k in (0, 1):
                s = s + rx[g, k, pl.ds(off, TR)].astype(F32)
            if mine:
                lg[h, :, xcol(i)] = s
            else:
                sx2[g] = s.astype(BF)
                rx2_copy(g).start()

    def combine_z(g):
        for k in (0, 1):
            rzf_copy(g, k).wait_recv()
            own = z_sum(g, 1 if k == 0 else 3, (k * (TR // 2), TR // 2))
            szc[g, k] = (own + rzf[g, k].astype(F32)).astype(BF)
            rzc_copy(g, k).start()

    def rs_end(g):
        h, i = g // 2, g % 2
        rx2_copy(g).wait_recv()
        lg[h, :, xcol(i)] = lg[h, :, xcol(i)] + rx2[g].astype(F32)
        s = lg[h, :, zcol(i)]
        for k in (0, 1):
            rzn_copy(g, k).wait_recv()
            rzc_copy(g, k).wait_recv()
            s = s + rz2[g, k].astype(F32)
        lg[h, :, zcol(i)] = s

    def dl_at(h, xx, zz, col):
        return dl.at[h, rows_of(xx, zz), col]

    def half_at(h, xx, zz, k, col):
        first = pl.multiple_of((xx * 2 + zz) * TR + k * (TR // 2), TR // 2)
        return dl.at[h, pl.ds(first, TR // 2), col]

    def az_copy(g, k):
        a = dl_at(g // 2, x, zl, zcol(g % 2))
        return rc(a, a, *pair(az_ss, az_rs, g, k))

    def azh_copy(g, k):
        a = half_at(g // 2, source(k), zl, k, zcol(g % 2))
        return rc(a, a, *pair(azh_ss, azh_rs, g, k))

    def azz_copy(g):
        a = dl_at(g // 2, x, zl, zcol(g % 2))
        return rc(a, a, azz_ss.at[g], azz_rs.at[g], zpeer)

    def azf_copy(g, d):
        a = dl_at(g // 2, xd(d), zl, zcol(g % 2))
        return rc(a, a, azf_ss.at[g, d - 1], azf_rs.at[g, d - 1], zpeer)

    def ax_copy(g, k):
        a = dl_at(g // 2, x, zl, xcol(g % 2))
        return rc(a, a, *pair(ax_ss, ax_rs, g, k))

    def axh_copy(g, k):
        a = half_at(g // 2, source(k), zl, k, xcol(g % 2))
        return rc(a, a, *pair(axh_ss, axh_rs, g, k))

    def axz_copy(g):
        a = dl_at(g // 2, x, zl, xcol(g % 2))
        return rc(a, a, axz_ss.at[g], axz_rs.at[g], zpeer)

    def axf_copy(g, k):
        a = dl_at(g // 2, x, 1 - zl, xcol(g % 2))
        return rc(a, a, *pair(axf_ss, axf_rs, g, k))

    def axg_copy(g, k):
        a = half_at(g // 2, source(k), 1 - zl, k, xcol(g % 2))
        return rc(a, a, *pair(axg_ss, axg_rs, g, k))

    lane = lax.broadcasted_iota(jnp.int32, (TR, FB), 1)

    def send_st(h, q):
        k, dc = mp15[q]
        return rc(st_own.at[h], st_in.at[h, mp], st_ss.at[h, q], st_rs.at[h, q], at_mp(k, dc))

    def softmax(h):
        inv_own = inv_s[h, tok(pos), :][:, :1]
        want = tcol[h, tok(pos), :][:, :1]
        m = jnp.full((TR, 1), -jnp.inf, F32)
        for j in range(V // HALF):
            v = lg[h, :, j * HALF : (j + 1) * HALF] * inv_own
            lg[h, :, j * HALF : (j + 1) * HALF] = v
            m = jnp.maximum(m, jnp.max(v, axis=1, keepdims=True))
        s, sl, pk = (jnp.zeros((TR, 1), F32) for _ in range(3))
        for j in range(V // HALF):
            ids = (lax.broadcasted_iota(jnp.int32, (TR, HALF), 1) + j * HALF).astype(F32)
            v = lg[h, :, j * HALF : (j + 1) * HALF]
            p = jnp.exp(v - m)
            dl[h, tok(pos), j * HALF : (j + 1) * HALF] = p.astype(BF)
            g = h * 2 + j // 2
            if j % 2:
                axz_copy(g).start()
                for k in (0, 1):
                    ax_copy(g, k).start()
            else:
                for k in (0, 1):
                    az_copy(g, k).start()
                azz_copy(g).start()
            s = s + jnp.sum(p, axis=1, keepdims=True)
            sl = sl + jnp.sum(p * v, axis=1, keepdims=True)
            pk = pk + jnp.sum(jnp.where(ids == want, v, 0.0), axis=1, keepdims=True)
        tsq[...] = jnp.zeros((FB, FB), F32)
        tsq[:TR, :] = jnp.where(
            lane == 0, m, jnp.where(lane == 1, s, jnp.where(lane == 2, sl, jnp.where(lane == 3, pk, 0.0)))
        )
        st_own[h] = tsq[...].T[:8, :]
        for q in range(15):
            send_st(h, q).start()
        st_in[h, mp] = st_own[h]

    def forward(g):
        axz_copy(g).wait_recv()
        for k in (0, 1):
            axf_copy(g, k).start()
        for k in (0, 1):
            az_copy(g, k).wait_recv()
            azh_copy(g, k).start()
            azf_copy(g, 3 if k == 0 else 1).start()
        for k in (0, 1):
            ax_copy(g, k).wait_recv()
            axh_copy(g, k).start()

    def forward_far(g):
        for k in (0, 1):
            axf_copy(g, k).wait_recv()
            axg_copy(g, k).start()
        for k in (0, 1):
            azh_copy(g, k).wait_recv()
        azf_copy(g, 2).start()

    def ag_end(g):
        azz_copy(g).wait_recv()
        for k in (0, 1):
            axh_copy(g, k).wait_recv()
            axg_copy(g, k).wait_recv()
        for d in (1, 2, 3):
            azf_copy(g, d).wait_recv()

    def send_sc(h, q):
        a = sc_all.at[h, pos]
        return rc(a, a, sc_ss.at[h, q], sc_rs.at[h, q], at_dp(*dp_offs[q]))

    def statistics(h):
        for q in range(15):
            send_st(h, q).wait_recv()
        all_m = st_in[h, :, 0, :]
        top = jnp.max(all_m, axis=0, keepdims=True)
        scale = jnp.exp(all_m - top)
        total = jnp.sum(st_in[h, :, 1, :] * scale, axis=0, keepdims=True)
        total_l = jnp.sum(st_in[h, :, 2, :] * scale, axis=0, keepdims=True)
        picked = jnp.sum(st_in[h, :, 3, :], axis=0, keepdims=True)
        valid = lax.broadcasted_iota(jnp.int32, (1, FB), 1) < TR
        total = jnp.where(valid, total, 1.0)
        lse = top + jnp.log(total)
        moment = (total_l / total - picked) / T
        factor = jnp.exp(st_own[h, :1, :] - lse) / T
        sub = lax.broadcasted_iota(jnp.int32, (FB, FB), 0)
        table = jnp.where(sub == 0, factor, jnp.where(sub == 1, moment, jnp.where(sub == 2, lse - picked, 0.0)))
        tsq[...] = table.T
        sc_all[h, pos] = tsq[:TR, :]
        for q in range(7):
            send_sc(h, q).start()

    def factors(h):
        for q in range(7):
            send_sc(h, q).wait_recv()
        for b in range(8):
            ct[h, b * TR : (b + 1) * TR, :] = jnp.broadcast_to(sc_all[h, b][:, 0:1], (TR, FB))

    def scaled_tile(h, first, col, r):
        f = ct[h]
        own_row = oh[h, :, col].astype(F32) / T
        return jnp.concatenate(
            [r[:, b * FB : (b + 1) * FB] * f - own_row[:, b * FB : (b + 1) * FB] for b in (0, 1)], axis=1
        )

    def early_part(h):
        def body(t, carry):
            r = dot(dl[h, :, :CH], e_flat[:CH, pl.ds(pl.multiple_of(t * 256, 256), 256)], NN)
            acc[h, t * 2] = r[:, :FB]
            acc[h, t * 2 + 1] = r[:, FB:]
            return carry

        lax.fori_loop(0, 8, body, 0)

    def late_tile(h):
        def tile(first, col):
            r = dot(dl[h, :, CH:], e_flat[CH:, col], NN)
            return scaled_tile(h, first, col, r + jnp.concatenate([acc[h, first], acc[h, first + 1]], axis=1))

        return tile

    def whole_tile(h):
        return lambda first, col: scaled_tile(h, first, col, dot(dl[h], e_flat[:, col], NN))

    def pre_gradient(h):
        dnormed = collect(h, core2_ss, core2_rs, mp2_ss, mp2_rs, GRAD_BOUND)
        moments = jnp.concatenate([sc_all[h, b][:, 1:2] for b in range(8)], axis=0)
        inv, act, pre = inv_s[h], act_s[h], pre_s[h]
        dact = inv * gain * dnormed - act * (inv * inv * (moments / D))
        sig = 1.0 / (1.0 + jnp.exp(-pre))
        nb[h] = (dact * sig * (1.0 + pre * (1.0 - sig))).astype(BF)
        gather_start(dpf, h, *dp_sems)

    def send_sq2(q):
        return rc(sq_sum, sq_in2.at[dp], sq2_ss.at[q], sq2_rs.at[q], at_dp(*dp_offs[q]))

    def send_squares():
        for q in range(15):
            send_sq(q).wait_recv()
        sq_sum[...] = jnp.sum(sq_in[...], axis=0)
        for q in range(7):
            send_sq2(q).start()
        sq_in2[dp] = sq_sum[...]

    def norms():
        for q in range(7):
            send_sq2(q).wait_recv()
        mean = jnp.sum(sq_in2[...], axis=0)[:1, :] / D
        inv_row = lax.rsqrt(mean + 1e-05)
        for h in (0, 1):
            for i in (0, 1):
                at = h * TH + i * FB
                inv_s[h, i * FB : (i + 1) * FB, :] = jnp.broadcast_to(inv_row[:, at : at + FB], (FB, FB)).T

    logits_chunk(0)
    logits_chunk(1)
    gather_mid(nf, 1, *nf_sems)
    combine_x(0)
    send_squares()
    gather_end(nf, 1, *nf_sems)
    logits_chunk(2)
    combine_x(1)
    second_step(0)
    logits_chunk(3)
    combine_x(2)
    second_step(1)
    combine_z(0)
    norms()
    combine_x(3)
    second_step(2)
    combine_z(1)
    rs_end(0)
    rs_end(1)
    softmax(0)
    second_step(3)
    combine_z(2)
    combine_z(3)
    forward(0)
    forward(1)
    rs_end(2)
    rs_end(3)
    softmax(1)
    forward_far(0)
    forward_far(1)
    statistics(0)
    ag_end(0)
    ag_end(1)
    factors(0)
    product(0, whole_tile(0), core2_ss, core2_rs, 1)
    forward(2)
    forward(3)
    product(0, whole_tile(0), core2_ss, core2_rs, 0)
    forward_far(2)
    exchange(0, core2_ss, core2_rs, mp2_ss, mp2_rs, GRAD_BOUND)
    forward_far(3)
    statistics(1)
    pre_gradient(0)
    ag_end(2)
    early_part(1)
    factors(1)
    ag_end(3)
    product(1, late_tile(1), core2_ss, core2_rs, 1)
    gather_mid(dpf, 0, *dp_sems)
    product(1, late_tile(1), core2_ss, core2_rs, 0)
    exchange(1, core2_ss, core2_rs, mp2_ss, mp2_rs, GRAD_BOUND)
    for h in (0, 1):
        for i in range(8):
            hid_t[i * FB : (i + 1) * FB, h * TH : (h + 1) * TH] = hid_all[h, :, i * FB : (i + 1) * FB].T
    loss = jnp.zeros((TR, 1), F32)
    for h in (0, 1):
        for b in range(8):
            loss = loss + sc_all[h, b][:, 2:3]
    loss_ref[...] = jnp.sum(loss, axis=0, keepdims=True) / T
    gather_end(dpf, 0, *dp_sems)
    pre_gradient(1)

    def grad_copy(n, col):
        return pltpu.make_async_copy(w_flat.at[:, col], grad_ref.at[:, col], out_sem.at[n])

    def grad_tile(n, core, dy):
        first = core * 8 + lax.rem(y + 4 - dy, 4) * 2
        col = pl.ds(pl.multiple_of(first * FB, 2 * FB), 2 * FB)
        r = dot(hid_t[:, :TH], dpf[0, :, col], NN) + dot(hid_t[:, TH:], dpf[1, :, col], NN)
        w_flat[:, col] = r.astype(BF)
        grad_copy(n, col).start()
        return n, col

    tiles = []
    for dy in (0, 1, 3, 2):
        for k in (dy * 2, dy * 2 + 1):
            if k:
                ag_copy(dpf, 1, dp_ss, dp_rs, k).wait_recv()
                ag_pass(dpf, 1, dpc_ss, dpc_rs, k).start()
        tiles.append(grad_tile(len(tiles), c, dy))
    for dy in (0, 1, 3, 2):
        for k in (dy * 2, dy * 2 + 1):
            ag_pass(dpf, 1, dpc_ss, dpc_rs, k).wait_recv()
        tiles.append(grad_tile(len(tiles), 1 - c, dy))
    for k in range(8):
        ag_pass(dpf, 1, dpc_ss, dpc_rs, k).wait_send()
    for k in mp_offs:
        ag_copy(dpf, 1, dp_ss, dp_rs, k).wait_send()

    for q in range(7):
        send_sq2(q).wait_send()
        for h in (0, 1):
            send_hid(q, h).wait_send()
            send_sc(h, q).wait_send()
    for q in range(15):
        send_sq(q).wait_send()
        for h in (0, 1):
            send_st(h, q).wait_send()

    def drain(g, carry):
        rx2_copy(g).wait_send()
        azz_copy(g).wait_send()
        axz_copy(g).wait_send()
        for d in range(4):
            rz_copy(g, d).wait_send()
        for d in (1, 2, 3):
            azf_copy(g, d).wait_send()
        for k in (0, 1):
            rxf_copy(g, k).wait_send()
            rxn_copy(g, k).wait_send()
            rxc_copy(g, k).wait_send()
            rzf_copy(g, k).wait_send()
            rzn_copy(g, k).wait_send()
            rzc_copy(g, k).wait_send()
            az_copy(g, k).wait_send()
            azh_copy(g, k).wait_send()
            ax_copy(g, k).wait_send()
            axh_copy(g, k).wait_send()
            axf_copy(g, k).wait_send()
            axg_copy(g, k).wait_send()
        return carry

    lax.fori_loop(0, NG, drain, 0)
    for n, col in tiles:
        grad_copy(n, col).wait()


def head(hidden, weight, gain, embed, targets):
    vm = pltpu.VMEM
    dma = pltpu.SemaphoreType.DMA
    scratch = [
        vm((V, 2048), BF), vm((1024, 2048), BF), vm((4, ROWS, 16, FB), BF), vm((2, TH, 1024), BF), vm((1024, T), BF),
        vm((2, 8, TH, FB), BF), vm((2, 16, TH, FB), F32), vm((2, 8, TH, FB), BF), vm((2, 8, TH, FB), jnp.int16),
        vm((2, 8, TH, FB), jnp.int16), vm((2, TH, 2048), BF), vm((2, TH, FB), F32), vm((2, TH, FB), F32),
        vm((2, TH, FB), F32), vm((2, TH, FB), F32), vm((2, TH, FB), BF), vm((2, TH, 2048), BF), vm((2, TH, 2048), BF),
        vm((8, T), F32), vm((16, 8, T), F32), vm((8, T), F32), vm((8, 8, T), F32), vm((2, TH, FB), F32),
        vm((NG, TH, HALF), BF), vm((NG, TH, HALF), BF),
        vm((NG, 2, 2 * TR, HALF), BF), vm((NG, 2, TR, HALF), BF), vm((NG, 2, TR, HALF), BF), vm((NG, 4, TR, HALF), BF),
        vm((NG, TR, HALF), BF), vm((NG, TR, HALF), BF), vm((NG, TR, HALF), BF), vm((NG, 2, TR // 2, HALF), BF),
        vm((NG, 2, TR // 2, HALF), BF), vm((NG, 2, TR // 2, HALF), BF), vm((NG, 2, TR, HALF), BF),
        vm((2, TR, V), F32), vm((FB, FB), F32), vm((2, 8, FB), F32), vm((2, 16, 8, FB), F32),
        vm((2, 8, TR, FB), F32), vm((2, TH, V), BF),
        dma((4,)), dma((8,)),
    ]
    counts = [
        (7, 2), (2, 4), (2, 8), (2, 4), (2, 8), (2, 8), (2, 8), (2, 8), (2, 8), (15,), (7,), (2, 15), (2, 7),
        (NG, 2), (NG, 2), (NG, 2), (NG, 4), (NG,), (NG, 2), (NG, 2), (NG, 2),
        (NG, 2), (NG, 2), (NG,), (NG, 3), (NG, 2), (NG, 2), (NG,), (NG, 2), (NG, 2),
    ]
    for n in counts:
        scratch += [dma(n), dma(n)]
    vspec = pl.BlockSpec(memory_space=pltpu.VMEM)
    anyspec = pl.BlockSpec(memory_space=pl.ANY)
    return pl.pallas_call(
        head_kernel,
        name="head",
        out_shape=(jax.ShapeDtypeStruct((1024, 2048), BF), jax.ShapeDtypeStruct((1, 1), F32)),
        in_specs=[vspec, anyspec, vspec, anyspec, vspec],
        out_specs=(anyspec, vspec),
        scratch_shapes=scratch,
        compiler_params=pltpu.CompilerParams(
            collective_id=0, has_side_effects=True, vmem_limit_bytes=62 << 20
        ),
    )(hidden, weight, gain, embed, targets)


def order_kernel(grad, out):
    blocks = jnp.stack([grad[:, ((j % 2) * 8 + j // 2) * FB :][:, :FB] for j in range(16)])
    out[...] = pltpu.einshape("jvl->vjl", blocks)


def in_order(grad):
    rows = 512
    return pl.pallas_call(
        order_kernel,
        name="in_order",
        grid=(1024 // rows,),
        out_shape=jax.ShapeDtypeStruct((1024, 16, FB), BF),
        in_specs=[pl.BlockSpec((rows, 2048), lambda i: (i, 0))],
        out_specs=pl.BlockSpec((rows, 16, FB), lambda i: (i, 0, 0)),
        compiler_params=pltpu.CompilerParams(vmem_limit_bytes=62 << 20),
    )(grad)


def on_device(hidden_rows, head_weight, norm_gain, vocab_embed, targets):
    grad, loss = head(
        hidden_rows,
        head_weight.reshape(1024, 16, FB),
        norm_gain.reshape(1, FB),
        vocab_embed.reshape(V, 16, FB),
        targets.reshape(1, T),
    )
    return in_order(grad).reshape(head_weight.shape), loss.reshape(())


def solution(mesh):
    return jax.shard_map(
        on_device,
        mesh=mesh,
        in_specs=(
            P("dp", "mp"),
            P("mp", None, "dp", None),
            P("mp", "dp", None),
            P("mp", None, "dp", None),
            P(),
        ),
        out_specs=(P("mp", None, "dp", None), P()),
        check_vma=False,
    )
```

```python
import jax
import jax.numpy as jnp
from jax import lax
from jax.experimental import pallas as pl
from jax.experimental.pallas import tpu as pltpu
from jax.sharding import PartitionSpec as P

MESH = pl.DeviceIdType.MESH
BF = jnp.bfloat16
F32 = jnp.float32
T, D, V, FB = 512, 16384, 4096, 128
TH = T // 2
TR = 32
CH = 2048
ZW = 768
XW = CH - ZW
NG = 4
ROWS = 256
CODE = 32000.0
PRE_BOUND = 60.0 * 0.046875 * 2048 * 1.01
GRAD_BOUND = 6.0 * 2 / T * 1.01
NT = (((1,), (1,)), ((), ()))
NN = (((1,), (0,)), ((), ()))


def dot(a, b, dims):
    return lax.dot_general(a, b, dims, preferred_element_type=F32)


def head_kernel(
    hid_ref, w_ref, gain_ref, e_ref, tgt_ref,
    grad_ref, loss_ref,
    e_flat, w_flat, stage, hid_all, hid_t, ps, acc, core_in, ps2, mp_in, oh, ct, tcol,
    pre_s, act_s, nb, nf, dpf, sq_own, sq_in, sq_sum, sq_in2, inv_s,
    lz, lx, rx, rxf, sxc, rz, sx2, rx2, szf, szn, rzf, szc, rz2, lg, tsq, st_own, st_in, sc_all, dl,
    stage_sem, out_sem,
    hid_ss, hid_rs, core_ss, core_rs, mp_ss, mp_rs, core2_ss, core2_rs, mp2_ss, mp2_rs,
    nf_ss, nf_rs, nfc_ss, nfc_rs, dp_ss, dp_rs, dpc_ss, dpc_rs,
    sq_ss, sq_rs, sq2_ss, sq2_rs, st_ss, st_rs, sc_ss, sc_rs,
    rxf_ss, rxf_rs, rxn_ss, rxn_rs, rxc_ss, rxc_rs, rz_ss, rz_rs, rx2_ss, rx2_rs,
    rzf_ss, rzf_rs, rzn_ss, rzn_rs, rzc_ss, rzc_rs,
    az_ss, az_rs, azh_ss, azh_rs, azz_ss, azz_rs, azf_ss, azf_rs, ax_ss, ax_rs, axh_ss, axh_rs,
    axz_ss, axz_rs, axf_ss, axf_rs, axg_ss, axg_rs,
):
    dp = lax.axis_index("dp")
    mp = lax.axis_index("mp")
    x, zl = lax.rem(dp, 4), dp // 4
    yz, c = mp // 2, lax.rem(mp, 2)
    y, zh = yz // 2, lax.rem(yz, 2)
    pos = x * 2 + zl

    def at_dp(dx, dz):
        return (lax.rem(zl + dz, 2) * 4 + lax.rem(x + dx, 4), mp)

    def at_mp(k, dc=0):
        return (dp, yz_of(k) * 2 + lax.rem(c + dc, 2))

    def yz_of(k):
        return lax.rem(y + k // 2, 4) * 2 + lax.rem(zh + k % 2, 2)

    def yz_from(k):
        return lax.rem(y + 4 - k // 2, 4) * 2 + lax.rem(zh + k % 2, 2)

    zpeer = at_dp(0, 1)
    sibling = at_mp(0, 1)
    dp_offs = [(k % 4, k // 4) for k in (6, 2, 5, 7, 1, 3, 4)]
    mp_offs = [5, 4, 3, 7, 2, 6, 1]
    mp15 = [(k, 1) for k in [*mp_offs, 0]] + [(k, 0) for k in mp_offs]

    def rc(src, dst, ss, rs, dev):
        return pltpu.make_async_remote_copy(
            src_ref=src, dst_ref=dst, send_sem=ss, recv_sem=rs, device_id=dev, device_id_type=MESH
        )

    def load_w(i):
        return pltpu.make_async_copy(w_ref.at[pl.ds(i * ROWS, ROWS)], stage.at[i], stage_sem.at[i])

    def load_e(i):
        slot = lax.rem(i, 4)
        return pltpu.make_async_copy(
            e_ref.at[pl.ds(i * ROWS, ROWS)], stage.at[slot], stage_sem.at[slot]
        )

    for i in range(4):
        load_w(i).start()

    barrier = pltpu.get_barrier_semaphore()
    for o in dp_offs:
        pl.semaphore_signal(barrier, inc=1, device_id=at_dp(*o), device_id_type=MESH)
    for k, dc in mp15:
        pl.semaphore_signal(barrier, inc=1, device_id=at_mp(k, dc), device_id_type=MESH)
    pl.semaphore_wait(barrier, len(dp_offs) + len(mp15))

    def tok(p):
        return pl.ds(pl.multiple_of(p * TR, TR), TR)

    def send_hid(q, h):
        return rc(
            hid_ref.at[pl.ds(h * TR, TR)], hid_all.at[h, tok(pos)],
            hid_ss.at[q, h], hid_rs.at[q, h], at_dp(*dp_offs[q]),
        )

    for h in (0, 1):
        for q in range(7):
            send_hid(q, h).start()
        hid_all[h, tok(pos), :] = hid_ref[h * TR : (h + 1) * TR, :]

    def relay(slot, out, first):
        def body(i, carry):
            r = pltpu.einshape("vjl->jvl", stage[slot, pl.ds(pl.multiple_of(i * 64, 64), 64)])
            s = pl.multiple_of(first + i * 64, 64)
            for j in range(16):
                at = ((j % 2) * 8 + j // 2) * FB
                out[pl.ds(s, 64), at : at + FB] = r[j]
            return carry

        lax.fori_loop(0, ROWS // 64, body, 0)

    def relay_e(i, carry):
        load_e(i).wait()
        relay(lax.rem(i, 4), e_flat, i * ROWS)

        @pl.when(i + 4 < V // ROWS)
        def _():
            load_e(i + 4).start()

        return carry

    for i in range(4):
        load_w(i).wait()
        relay(i, w_flat, i * ROWS)
        load_e(i).start()

    local_tgt = tgt_ref[...].astype(F32) - (mp * V).astype(F32)
    for i in range(4):
        part = jnp.broadcast_to(local_tgt[:, i * FB : (i + 1) * FB], (FB, FB)).T
        for j in (0, 1):
            block = i * 2 + j
            at = ((block % 4) * 2 + block // 4) * TR
            for h in (0, 1):
                first = j * 64 + h * TR
                tcol[h, at : at + TR, :] = part[first : first + TR, :]

    def zcol(i):
        return pl.ds(pl.multiple_of(i * CH, CH), ZW)

    def xcol(i):
        return pl.ds(pl.multiple_of(i * CH + ZW, FB), XW)

    for h in (0, 1):
        for i in (0, 1):
            ids = (lax.broadcasted_iota(jnp.int32, (TH, CH), 1) + i * CH).astype(F32)
            want = tcol[h, :, :1]
            lz[h * 2 + i] = (ids[:, :ZW] == want).astype(BF)
            lx[h * 2 + i] = (ids[:, ZW:] == want).astype(BF)

    def pick_body(n, carry):
        col = pl.ds(pl.multiple_of(n * 256, 256), 256)
        for h in (0, 1):
            r = jnp.zeros((TH, 256), F32)
            for i in (0, 1):
                r = r + dot(lz[h * 2 + i], e_flat[i * CH : i * CH + ZW, col], NN)
                r = r + dot(lx[h * 2 + i], e_flat[i * CH + ZW : (i + 1) * CH, col], NN)
            oh[h, :, col] = r.astype(BF)
        return carry

    lax.fori_loop(0, 8, relay_e, 0)

    def core_copy(h, ss, rs, t):
        two = pl.ds(t * 2, 2)
        return rc(ps.at[h, two], core_in.at[h, two], ss.at[h, t], rs.at[h, t], sibling)

    def mp_copy(h, ss, rs, k):
        return rc(ps2.at[h, yz_of(k)], mp_in.at[h, k], ss.at[h, k], rs.at[h, k], at_mp(k))

    def product(h, tile, css, crs, side):
        who = lax.rem(c + side, 2)

        def body(t, carry):
            first = who * 8 + t * 2
            r = tile(first, pl.ds(pl.multiple_of(first * FB, 2 * FB), 2 * FB))
            if side:
                ps[h, t * 2] = r[:, :FB].astype(BF)
                ps[h, t * 2 + 1] = r[:, FB:].astype(BF)
                core_copy(h, css, crs, t).start()
            else:
                acc[h, first] = r[:, :FB]
                acc[h, first + 1] = r[:, FB:]
            return carry

        lax.fori_loop(0, 4, body, 0)

    def encode(v, bound):
        root = lax.rsqrt(lax.rsqrt(jnp.abs(v) * (CODE**4 / bound)))
        code = (root + 0.5).astype(jnp.int32)
        return jnp.where(v < 0, -code, code).astype(jnp.int16)

    def decode(code, bound):
        root = code.astype(F32) * (1.0 / CODE)
        return root * jnp.abs(root) * (root * root) * bound

    def exchange(h, css, crs, mss, mrs, bound):
        for t in range(4):
            core_copy(h, css, crs, t).wait_recv()
        for k in mp_offs:
            b = yz_of(k)
            ps2[h, b] = encode(acc[h, c * 8 + b] + core_in[h, b].astype(F32), bound)
            mp_copy(h, mss, mrs, k).start()

    def collect(h, css, crs, mss, mrs, bound):
        total = acc[h, c * 8 + yz] + core_in[h, yz].astype(F32)
        for k in mp_offs:
            mp_copy(h, mss, mrs, k).wait_recv()
            total = total + decode(mp_in[h, k], bound)
        for k in mp_offs:
            mp_copy(h, mss, mrs, k).wait_send()
        for t in range(4):
            core_copy(h, css, crs, t).wait_send()
        return total

    for h in (0, 1):
        for q in range(7):
            send_hid(q, h).wait_recv()
        for side in (1, 0):
            product(h, lambda first, col, h=h: dot(hid_all[h], w_flat[:, col], NN), core_ss, core_rs, side)
        exchange(h, core_ss, core_rs, mp_ss, mp_rs, PRE_BOUND)

    lax.fori_loop(8, V // ROWS, relay_e, 0)
    lax.fori_loop(0, 2, pick_body, 0)

    gain = gain_ref[...]

    def cols(core, b):
        return pl.ds(pl.multiple_of((core * 8 + b) * FB, FB), FB)

    def ag_copy(buf, h, ss, rs, k):
        return rc(nb.at[h], buf.at[h, :, cols(c, yz)], ss.at[h, k], rs.at[h, k], at_mp(k))

    def ag_pass(buf, h, ss, rs, k):
        at = buf.at[h, :, cols(c, yz_from(k))]
        return rc(nb.at[h] if k == 0 else at, at, ss.at[h, k], rs.at[h, k], sibling)

    def gather_start(buf, h, ss, rs, css, crs):
        for k in mp_offs:
            ag_copy(buf, h, ss, rs, k).start()
        ag_pass(buf, h, css, crs, 0).start()
        buf[h, :, cols(c, yz)] = nb[h]

    def gather_mid(buf, h, ss, rs, css, crs):
        for k in reversed(mp_offs):
            ag_copy(buf, h, ss, rs, k).wait_recv()
            ag_pass(buf, h, css, crs, k).start()

    def gather_end(buf, h, ss, rs, css, crs):
        for k in range(8):
            ag_pass(buf, h, css, crs, k).wait_recv()
        for k in range(8):
            ag_pass(buf, h, css, crs, k).wait_send()
        for k in mp_offs:
            ag_copy(buf, h, ss, rs, k).wait_send()

    nf_sems = (nf_ss, nf_rs, nfc_ss, nfc_rs)
    dp_sems = (dp_ss, dp_rs, dpc_ss, dpc_rs)

    def activate(h):
        pre = collect(h, core_ss, core_rs, mp_ss, mp_rs, PRE_BOUND)
        pre_s[h] = pre
        own = hid_all[h, :, pl.ds(pl.multiple_of(dp * FB, FB), FB)].astype(F32)
        act = own + pre / (1.0 + jnp.exp(-pre))
        act_s[h] = act
        nb[h] = (act * gain).astype(BF)
        gather_start(nf, h, *nf_sems)
        squares = act * act
        for i in (0, 1):
            row = jnp.sum(squares[i * FB : (i + 1) * FB, :].T, axis=0, keepdims=True)
            at = h * TH + i * FB
            sq_own[:, at : at + FB] = jnp.broadcast_to(row, (8, FB))

    def send_sq(q):
        k, dc = mp15[q]
        return rc(sq_own, sq_in.at[mp], sq_ss.at[q], sq_rs.at[q], at_mp(k, dc))

    activate(0)
    lax.fori_loop(2, 4, pick_body, 0)
    activate(1)
    for q in range(15):
        send_sq(q).start()
    sq_in[mp] = sq_own[...]
    lax.fori_loop(4, 6, pick_body, 0)
    gather_mid(nf, 0, *nf_sems)
    lax.fori_loop(6, 8, pick_body, 0)
    gather_end(nf, 0, *nf_sems)

    def rows_of(xx, zz):
        return tok(xx * 2 + zz)

    def xd(d):
        return lax.rem(x + d, 4)

    def rz_copy(g, d):
        return rc(
            lz.at[g, rows_of(xd(d), 1 - zl)], rz.at[g, d], rz_ss.at[g, d], rz_rs.at[g, d], zpeer
        )

    def way(k):
        return at_dp(1 if k == 0 else 3, 0)

    def to(k):
        return xd(1 if k == 0 else 3)

    def source(k):
        return xd(3 if k == 0 else 1)

    def block(xx, half):
        return pl.ds(pl.multiple_of(xx * 2 * TR + half * TR, TR), TR)

    def part(half):
        return pl.ds(half * (TR // 2), TR // 2)

    def pair(ss, rs, g, k):
        return (ss.at[g, k], rs.at[g, k], way(k))

    def rxf_copy(g, k):
        return rc(lx.at[g, block(xd(2), k)], rxf.at[g, k], *pair(rxf_ss, rxf_rs, g, k))

    def rxn_copy(g, k):
        here = pl.ds((1 - k) * TR, TR)
        return rc(lx.at[g, block(to(k), 1 - k)], rx.at[g, k, here], *pair(rxn_ss, rxn_rs, g, k))

    def rxc_copy(g, k):
        return rc(sxc.at[g, k], rx.at[g, k, pl.ds(k * TR, TR)], *pair(rxc_ss, rxc_rs, g, k))

    def rx2_copy(g):
        return rc(sx2.at[g], rx2.at[g], rx2_ss.at[g], rx2_rs.at[g], zpeer)

    def rzf_copy(g, k):
        return rc(szf.at[g, part(k)], rzf.at[g, k], *pair(rzf_ss, rzf_rs, g, k))

    def rzn_copy(g, k):
        return rc(szn.at[g, k], rz2.at[g, k, part(1 - k)], *pair(rzn_ss, rzn_rs, g, k))

    def rzc_copy(g, k):
        return rc(szc.at[g, k], rz2.at[g, k, part(k)], *pair(rzc_ss, rzc_rs, g, k))

    def logits_chunk(g):
        h, i = g // 2, g % 2
        lx[g] = dot(nf[h], e_flat[i * CH + ZW : (i + 1) * CH, :], NT).astype(BF)
        for k in (0, 1):
            rxf_copy(g, k).start()
        for k in (0, 1):
            rxn_copy(g, k).start()
        lz[g] = dot(nf[h], e_flat[i * CH : i * CH + ZW, :], NT).astype(BF)
        for d in (2, 1, 3, 0):
            rz_copy(g, d).start()

    def combine_x(g):
        for k in (0, 1):
            rxf_copy(g, k).wait_recv()
            sxc[g, k] = (lx[g, block(to(k), k)].astype(F32) + rxf[g, k].astype(F32)).astype(BF)
            rxc_copy(g, k).start()

    def z_sum(g, d, rows):
        first = pl.multiple_of((xd(d) * 2 + zl) * TR + rows[0], TR // 2)
        return lz[g, pl.ds(first, rows[1])].astype(F32) + rz[g, d, rows[0] : rows[0] + rows[1]].astype(F32)

    def second_step(g):
        h, i = g // 2, g % 2
        rz_copy(g, 2).wait_recv()
        szf[g] = z_sum(g, 2, (0, TR)).astype(BF)
        for k in (0, 1):
            rzf_copy(g, k).start()
        for k in (0, 1):
            d = 1 if k == 0 else 3
            rz_copy(g, d).wait_recv()
            szn[g, k] = z_sum(g, d, ((1 - k) * (TR // 2), TR // 2)).astype(BF)
            rzn_copy(g, k).start()
        rz_copy(g, 0).wait_recv()
        lg[h, :, zcol(i)] = z_sum(g, 0, (0, TR))
        for k in (0, 1):
            rxn_copy(g, k).wait_recv()
            rxc_copy(g, k).wait_recv()
        for mine in (False, True):
            zz = zl if mine else 1 - zl
            off = pl.multiple_of(zz * TR, TR)
            s = lx[g, block(x, zz)].astype(F32)
            for k in (0, 1):
                s = s + rx[g, k, pl.ds(off, TR)].astype(F32)
            if mine:
                lg[h, :, xcol(i)] = s
            else:
                sx2[g] = s.astype(BF)
                rx2_copy(g).start()

    def combine_z(g):
        for k in (0, 1):
            rzf_copy(g, k).wait_recv()
            own = z_sum(g, 1 if k == 0 else 3, (k * (TR // 2), TR // 2))
            szc[g, k] = (own + rzf[g, k].astype(F32)).astype(BF)
            rzc_copy(g, k).start()

    def rs_end(g):
        h, i = g // 2, g % 2
        rx2_copy(g).wait_recv()
        lg[h, :, xcol(i)] = lg[h, :, xcol(i)] + rx2[g].astype(F32)
        s = lg[h, :, zcol(i)]
        for k in (0, 1):
            rzn_copy(g, k).wait_recv()
            rzc_copy(g, k).wait_recv()
            s = s + rz2[g, k].astype(F32)
        lg[h, :, zcol(i)] = s

    def dl_at(h, xx, zz, col):
        return dl.at[h, rows_of(xx, zz), col]

    def half_at(h, xx, zz, k, col):
        first = pl.multiple_of((xx * 2 + zz) * TR + k * (TR // 2), TR // 2)
        return dl.at[h, pl.ds(first, TR // 2), col]

    def az_copy(g, k):
        a = dl_at(g // 2, x, zl, zcol(g % 2))
        return rc(a, a, *pair(az_ss, az_rs, g, k))

    def azh_copy(g, k):
        a = half_at(g // 2, source(k), zl, k, zcol(g % 2))
        return rc(a, a, *pair(azh_ss, azh_rs, g, k))

    def azz_copy(g):
        a = dl_at(g // 2, x, zl, zcol(g % 2))
        return rc(a, a, azz_ss.at[g], azz_rs.at[g], zpeer)

    def azf_copy(g, d):
        a = dl_at(g // 2, xd(d), zl, zcol(g % 2))
        return rc(a, a, azf_ss.at[g, d - 1], azf_rs.at[g, d - 1], zpeer)

    def ax_copy(g, k):
        a = dl_at(g // 2, x, zl, xcol(g % 2))
        return rc(a, a, *pair(ax_ss, ax_rs, g, k))

    def axh_copy(g, k):
        a = half_at(g // 2, source(k), zl, k, xcol(g % 2))
        return rc(a, a, *pair(axh_ss, axh_rs, g, k))

    def axz_copy(g):
        a = dl_at(g // 2, x, zl, xcol(g % 2))
        return rc(a, a, axz_ss.at[g], axz_rs.at[g], zpeer)

    def axf_copy(g, k):
        a = dl_at(g // 2, x, 1 - zl, xcol(g % 2))
        return rc(a, a, *pair(axf_ss, axf_rs, g, k))

    def axg_copy(g, k):
        a = half_at(g // 2, source(k), 1 - zl, k, xcol(g % 2))
        return rc(a, a, *pair(axg_ss, axg_rs, g, k))

    lane = lax.broadcasted_iota(jnp.int32, (TR, FB), 1)

    def send_st(h, q):
        k, dc = mp15[q]
        return rc(st_own.at[h], st_in.at[h, mp], st_ss.at[h, q], st_rs.at[h, q], at_mp(k, dc))

    def softmax(h):
        inv_own = inv_s[h, tok(pos), :][:, :1]
        want = tcol[h, tok(pos), :][:, :1]
        m = jnp.full((TR, 1), -jnp.inf, F32)
        spans = [(0, ZW), (ZW, XW), (CH, ZW), (CH + ZW, XW)]
        for at, wide in spans:
            v = lg[h, :, at : at + wide] * inv_own
            lg[h, :, at : at + wide] = v
            m = jnp.maximum(m, jnp.max(v, axis=1, keepdims=True))
        s, sl, pk = (jnp.zeros((TR, 1), F32) for _ in range(3))
        for j, (at, wide) in enumerate(spans):
            ids = (lax.broadcasted_iota(jnp.int32, (TR, wide), 1) + at).astype(F32)
            v = lg[h, :, at : at + wide]
            p = jnp.exp(v - m)
            dl[h, tok(pos), at : at + wide] = p.astype(BF)
            g = h * 2 + j // 2
            if j % 2:
                axz_copy(g).start()
                for k in (0, 1):
                    ax_copy(g, k).start()
            else:
                for k in (0, 1):
                    az_copy(g, k).start()
                azz_copy(g).start()
            s = s + jnp.sum(p, axis=1, keepdims=True)
            sl = sl + jnp.sum(p * v, axis=1, keepdims=True)
            pk = pk + jnp.sum(jnp.where(ids == want, v, 0.0), axis=1, keepdims=True)
        tsq[...] = jnp.zeros((FB, FB), F32)
        tsq[:TR, :] = jnp.where(
            lane == 0, m, jnp.where(lane == 1, s, jnp.where(lane == 2, sl, jnp.where(lane == 3, pk, 0.0)))
        )
        st_own[h] = tsq[...].T[:8, :]
        for q in range(15):
            send_st(h, q).start()
        st_in[h, mp] = st_own[h]

    def forward(g):
        axz_copy(g).wait_recv()
        for k in (0, 1):
            axf_copy(g, k).start()
        for k in (0, 1):
            az_copy(g, k).wait_recv()
            azh_copy(g, k).start()
            azf_copy(g, 3 if k == 0 else 1).start()
        for k in (0, 1):
            ax_copy(g, k).wait_recv()
            axh_copy(g, k).start()

    def forward_far(g):
        for k in (0, 1):
            axf_copy(g, k).wait_recv()
            axg_copy(g, k).start()
        for k in (0, 1):
            azh_copy(g, k).wait_recv()
        azf_copy(g, 2).start()

    def ag_end(g):
        azz_copy(g).wait_recv()
        for k in (0, 1):
            axh_copy(g, k).wait_recv()
            axg_copy(g, k).wait_recv()
        for d in (1, 2, 3):
            azf_copy(g, d).wait_recv()

    def send_sc(h, q):
        a = sc_all.at[h, pos]
        return rc(a, a, sc_ss.at[h, q], sc_rs.at[h, q], at_dp(*dp_offs[q]))

    def statistics(h):
        for q in range(15):
            send_st(h, q).wait_recv()
        all_m = st_in[h, :, 0, :]
        top = jnp.max(all_m, axis=0, keepdims=True)
        scale = jnp.exp(all_m - top)
        total = jnp.sum(st_in[h, :, 1, :] * scale, axis=0, keepdims=True)
        total_l = jnp.sum(st_in[h, :, 2, :] * scale, axis=0, keepdims=True)
        picked = jnp.sum(st_in[h, :, 3, :], axis=0, keepdims=True)
        valid = lax.broadcasted_iota(jnp.int32, (1, FB), 1) < TR
        total = jnp.where(valid, total, 1.0)
        lse = top + jnp.log(total)
        moment = (total_l / total - picked) / T
        factor = jnp.exp(st_own[h, :1, :] - lse) / T
        sub = lax.broadcasted_iota(jnp.int32, (FB, FB), 0)
        table = jnp.where(sub == 0, factor, jnp.where(sub == 1, moment, jnp.where(sub == 2, lse - picked, 0.0)))
        tsq[...] = table.T
        sc_all[h, pos] = tsq[:TR, :]
        for q in range(7):
            send_sc(h, q).start()

    def factors(h):
        for q in range(7):
            send_sc(h, q).wait_recv()
        for b in range(8):
            ct[h, b * TR : (b + 1) * TR, :] = jnp.broadcast_to(sc_all[h, b][:, 0:1], (TR, FB))

    def scaled_tile(h, first, col, r):
        f = ct[h]
        own_row = oh[h, :, col].astype(F32) / T
        return jnp.concatenate(
            [r[:, b * FB : (b + 1) * FB] * f - own_row[:, b * FB : (b + 1) * FB] for b in (0, 1)], axis=1
        )

    def early_part(h):
        def body(t, carry):
            r = dot(dl[h, :, :CH], e_flat[:CH, pl.ds(pl.multiple_of(t * 256, 256), 256)], NN)
            acc[h, t * 2] = r[:, :FB]
            acc[h, t * 2 + 1] = r[:, FB:]
            return carry

        lax.fori_loop(0, 8, body, 0)

    def late_tile(h):
        def tile(first, col):
            r = dot(dl[h, :, CH:], e_flat[CH:, col], NN)
            return scaled_tile(h, first, col, r + jnp.concatenate([acc[h, first], acc[h, first + 1]], axis=1))

        return tile

    def whole_tile(h):
        return lambda first, col: scaled_tile(h, first, col, dot(dl[h], e_flat[:, col], NN))

    def pre_gradient(h):
        dnormed = collect(h, core2_ss, core2_rs, mp2_ss, mp2_rs, GRAD_BOUND)
        moments = jnp.concatenate([sc_all[h, b][:, 1:2] for b in range(8)], axis=0)
        inv, act, pre = inv_s[h], act_s[h], pre_s[h]
        dact = inv * gain * dnormed - act * (inv * inv * (moments / D))
        sig = 1.0 / (1.0 + jnp.exp(-pre))
        nb[h] = (dact * sig * (1.0 + pre * (1.0 - sig))).astype(BF)
        gather_start(dpf, h, *dp_sems)

    def send_sq2(q):
        return rc(sq_sum, sq_in2.at[dp], sq2_ss.at[q], sq2_rs.at[q], at_dp(*dp_offs[q]))

    def send_squares():
        for q in range(15):
            send_sq(q).wait_recv()
        sq_sum[...] = jnp.sum(sq_in[...], axis=0)
        for q in range(7):
            send_sq2(q).start()
        sq_in2[dp] = sq_sum[...]

    def norms():
        for q in range(7):
            send_sq2(q).wait_recv()
        mean = jnp.sum(sq_in2[...], axis=0)[:1, :] / D
        inv_row = lax.rsqrt(mean + 1e-05)
        for h in (0, 1):
            for i in (0, 1):
                at = h * TH + i * FB
                inv_s[h, i * FB : (i + 1) * FB, :] = jnp.broadcast_to(inv_row[:, at : at + FB], (FB, FB)).T

    logits_chunk(0)
    logits_chunk(1)
    gather_mid(nf, 1, *nf_sems)
    combine_x(0)
    send_squares()
    gather_end(nf, 1, *nf_sems)
    logits_chunk(2)
    combine_x(1)
    second_step(0)
    logits_chunk(3)
    combine_x(2)
    second_step(1)
    combine_z(0)
    norms()
    combine_x(3)
    second_step(2)
    combine_z(1)
    rs_end(0)
    rs_end(1)
    softmax(0)
    second_step(3)
    combine_z(2)
    combine_z(3)
    forward(0)
    forward(1)
    rs_end(2)
    rs_end(3)
    softmax(1)
    forward_far(0)
    forward_far(1)
    statistics(0)
    ag_end(0)
    ag_end(1)
    forward(2)
    factors(0)
    product(0, whole_tile(0), core2_ss, core2_rs, 1)
    forward(3)
    forward_far(2)
    product(0, whole_tile(0), core2_ss, core2_rs, 0)
    forward_far(3)
    exchange(0, core2_ss, core2_rs, mp2_ss, mp2_rs, GRAD_BOUND)
    statistics(1)
    ag_end(2)
    early_part(1)
    pre_gradient(0)
    factors(1)
    ag_end(3)
    product(1, late_tile(1), core2_ss, core2_rs, 1)
    product(1, late_tile(1), core2_ss, core2_rs, 0)
    exchange(1, core2_ss, core2_rs, mp2_ss, mp2_rs, GRAD_BOUND)
    gather_mid(dpf, 0, *dp_sems)
    for h in (0, 1):
        for i in range(8):
            hid_t[i * FB : (i + 1) * FB, h * TH : (h + 1) * TH] = hid_all[h, :, i * FB : (i + 1) * FB].T
    loss = jnp.zeros((TR, 1), F32)
    for h in (0, 1):
        for b in range(8):
            loss = loss + sc_all[h, b][:, 2:3]
    loss_ref[...] = jnp.sum(loss, axis=0, keepdims=True) / T
    gather_end(dpf, 0, *dp_sems)
    pre_gradient(1)

    def grad_copy(n, col):
        return pltpu.make_async_copy(w_flat.at[:, col], grad_ref.at[:, col], out_sem.at[n])

    def grad_tile(n, core, dy):
        first = core * 8 + lax.rem(y + 4 - dy, 4) * 2
        col = pl.ds(pl.multiple_of(first * FB, 2 * FB), 2 * FB)
        r = dot(hid_t[:, :TH], dpf[0, :, col], NN) + dot(hid_t[:, TH:], dpf[1, :, col], NN)
        w_flat[:, col] = r.astype(BF)
        grad_copy(n, col).start()
        return n, col

    tiles = []
    for dy in (0, 1, 3, 2):
        for k in (dy * 2, dy * 2 + 1):
            if k:
                ag_copy(dpf, 1, dp_ss, dp_rs, k).wait_recv()
                ag_pass(dpf, 1, dpc_ss, dpc_rs, k).start()
        tiles.append(grad_tile(len(tiles), c, dy))
    for dy in (0, 1, 3, 2):
        for k in (dy * 2, dy * 2 + 1):
            ag_pass(dpf, 1, dpc_ss, dpc_rs, k).wait_recv()
        tiles.append(grad_tile(len(tiles), 1 - c, dy))
    for k in range(8):
        ag_pass(dpf, 1, dpc_ss, dpc_rs, k).wait_send()
    for k in mp_offs:
        ag_copy(dpf, 1, dp_ss, dp_rs, k).wait_send()

    for q in range(7):
        send_sq2(q).wait_send()
        for h in (0, 1):
            send_hid(q, h).wait_send()
            send_sc(h, q).wait_send()
    for q in range(15):
        send_sq(q).wait_send()
        for h in (0, 1):
            send_st(h, q).wait_send()

    def drain(g, carry):
        rx2_copy(g).wait_send()
        azz_copy(g).wait_send()
        axz_copy(g).wait_send()
        for d in range(4):
            rz_copy(g, d).wait_send()
        for d in (1, 2, 3):
            azf_copy(g, d).wait_send()
        for k in (0, 1):
            rxf_copy(g, k).wait_send()
            rxn_copy(g, k).wait_send()
            rxc_copy(g, k).wait_send()
            rzf_copy(g, k).wait_send()
            rzn_copy(g, k).wait_send()
            rzc_copy(g, k).wait_send()
            az_copy(g, k).wait_send()
            azh_copy(g, k).wait_send()
            ax_copy(g, k).wait_send()
            axh_copy(g, k).wait_send()
            axf_copy(g, k).wait_send()
            axg_copy(g, k).wait_send()
        return carry

    lax.fori_loop(0, NG, drain, 0)
    for n, col in tiles:
        grad_copy(n, col).wait()


def head(hidden, weight, gain, embed, targets):
    vm = pltpu.VMEM
    dma = pltpu.SemaphoreType.DMA
    scratch = [
        vm((V, 2048), BF), vm((1024, 2048), BF), vm((4, ROWS, 16, FB), BF), vm((2, TH, 1024), BF), vm((1024, T), BF),
        vm((2, 8, TH, FB), BF), vm((2, 16, TH, FB), F32), vm((2, 8, TH, FB), BF), vm((2, 8, TH, FB), jnp.int16),
        vm((2, 8, TH, FB), jnp.int16), vm((2, TH, 2048), BF), vm((2, TH, FB), F32), vm((2, TH, FB), F32),
        vm((2, TH, FB), F32), vm((2, TH, FB), F32), vm((2, TH, FB), BF), vm((2, TH, 2048), BF), vm((2, TH, 2048), BF),
        vm((8, T), F32), vm((16, 8, T), F32), vm((8, T), F32), vm((8, 8, T), F32), vm((2, TH, FB), F32),
        vm((NG, TH, ZW), BF), vm((NG, TH, XW), BF),
        vm((NG, 2, 2 * TR, XW), BF), vm((NG, 2, TR, XW), BF), vm((NG, 2, TR, XW), BF), vm((NG, 4, TR, ZW), BF),
        vm((NG, TR, XW), BF), vm((NG, TR, XW), BF), vm((NG, TR, ZW), BF), vm((NG, 2, TR // 2, ZW), BF),
        vm((NG, 2, TR // 2, ZW), BF), vm((NG, 2, TR // 2, ZW), BF), vm((NG, 2, TR, ZW), BF),
        vm((2, TR, V), F32), vm((FB, FB), F32), vm((2, 8, FB), F32), vm((2, 16, 8, FB), F32),
        vm((2, 8, TR, FB), F32), vm((2, TH, V), BF),
        dma((4,)), dma((8,)),
    ]
    counts = [
        (7, 2), (2, 4), (2, 8), (2, 4), (2, 8), (2, 8), (2, 8), (2, 8), (2, 8), (15,), (7,), (2, 15), (2, 7),
        (NG, 2), (NG, 2), (NG, 2), (NG, 4), (NG,), (NG, 2), (NG, 2), (NG, 2),
        (NG, 2), (NG, 2), (NG,), (NG, 3), (NG, 2), (NG, 2), (NG,), (NG, 2), (NG, 2),
    ]
    for n in counts:
        scratch += [dma(n), dma(n)]
    vspec = pl.BlockSpec(memory_space=pltpu.VMEM)
    anyspec = pl.BlockSpec(memory_space=pl.ANY)
    return pl.pallas_call(
        head_kernel,
        name="head",
        out_shape=(jax.ShapeDtypeStruct((1024, 2048), BF), jax.ShapeDtypeStruct((1, 1), F32)),
        in_specs=[vspec, anyspec, vspec, anyspec, vspec],
        out_specs=(anyspec, vspec),
        scratch_shapes=scratch,
        compiler_params=pltpu.CompilerParams(
            collective_id=0, has_side_effects=True, vmem_limit_bytes=62 << 20
        ),
    )(hidden, weight, gain, embed, targets)


def order_kernel(grad, out):
    blocks = jnp.stack([grad[:, ((j % 2) * 8 + j // 2) * FB :][:, :FB] for j in range(16)])
    out[...] = pltpu.einshape("jvl->vjl", blocks)


def in_order(grad):
    rows = 512
    return pl.pallas_call(
        order_kernel,
        name="in_order",
        grid=(1024 // rows,),
        out_shape=jax.ShapeDtypeStruct((1024, 16, FB), BF),
        in_specs=[pl.BlockSpec((rows, 2048), lambda i: (i, 0))],
        out_specs=pl.BlockSpec((rows, 16, FB), lambda i: (i, 0, 0)),
        compiler_params=pltpu.CompilerParams(vmem_limit_bytes=62 << 20),
    )(grad)


def on_device(hidden_rows, head_weight, norm_gain, vocab_embed, targets):
    grad, loss = head(
        hidden_rows,
        head_weight.reshape(1024, 16, FB),
        norm_gain.reshape(1, FB),
        vocab_embed.reshape(V, 16, FB),
        targets.reshape(1, T),
    )
    return in_order(grad).reshape(head_weight.shape), loss.reshape(())


def solution(mesh):
    return jax.shard_map(
        on_device,
        mesh=mesh,
        in_specs=(
            P("dp", "mp"),
            P("mp", None, "dp", None),
            P("mp", "dp", None),
            P("mp", None, "dp", None),
            P(),
        ),
        out_specs=(P("mp", None, "dp", None), P()),
        check_vma=False,
    )
```

```python
import jax
import jax.numpy as jnp
from jax import lax
from jax.experimental import pallas as pl
from jax.experimental.pallas import tpu as pltpu
from jax.sharding import PartitionSpec as P

MESH = pl.DeviceIdType.MESH
BF = jnp.bfloat16
F32 = jnp.float32
T, D, V, FB = 512, 16384, 4096, 128
TH = T // 2
TR = 32
CH = 2048
ZW = 768
XW = CH - ZW
NG = 4
ROWS = 256
CODE = 32000.0
PRE_BOUND = 60.0 * 0.046875 * 2048 * 1.01
GRAD_BOUND = 6.0 * 2 / T * 1.01
NT = (((1,), (1,)), ((), ()))
NN = (((1,), (0,)), ((), ()))


def dot(a, b, dims):
    return lax.dot_general(a, b, dims, preferred_element_type=F32)


def head_kernel(
    hid_ref, w_ref, gain_ref, e_ref, tgt_ref,
    grad_ref, loss_ref,
    e_flat, w_flat, stage, hid_all, hid_t, ps, acc, core_in, ps2, mp_in, oh, ct, tcol,
    pre_s, act_s, nb, nf, dpf, sq_own, sq_in, sq_sum, sq_in2, inv_s,
    lz, lx, rx, rxf, sxc, rz, sx2, rx2, szf, szn, rzf, szc, rz2, lg, tsq, st_own, st_in, sc_all, dl,
    stage_sem, out_sem,
    hid_ss, hid_rs, core_ss, core_rs, mp_ss, mp_rs, core2_ss, core2_rs, mp2_ss, mp2_rs,
    nf_ss, nf_rs, nfc_ss, nfc_rs, dp_ss, dp_rs, dpc_ss, dpc_rs,
    sq_ss, sq_rs, sq2_ss, sq2_rs, st_ss, st_rs, sc_ss, sc_rs,
    rxf_ss, rxf_rs, rxn_ss, rxn_rs, rxc_ss, rxc_rs, rz_ss, rz_rs, rx2_ss, rx2_rs,
    rzf_ss, rzf_rs, rzn_ss, rzn_rs, rzc_ss, rzc_rs,
    az_ss, az_rs, azh_ss, azh_rs, azz_ss, azz_rs, azf_ss, azf_rs, ax_ss, ax_rs, axh_ss, axh_rs,
    axz_ss, axz_rs, axf_ss, axf_rs, axg_ss, axg_rs,
):
    dp = lax.axis_index("dp")
    mp = lax.axis_index("mp")
    x, zl = lax.rem(dp, 4), dp // 4
    yz, c = mp // 2, lax.rem(mp, 2)
    y, zh = yz // 2, lax.rem(yz, 2)
    pos = x * 2 + zl

    def at_dp(dx, dz):
        return (lax.rem(zl + dz, 2) * 4 + lax.rem(x + dx, 4), mp)

    def at_mp(k, dc=0):
        return (dp, yz_of(k) * 2 + lax.rem(c + dc, 2))

    def yz_of(k):
        return lax.rem(y + k // 2, 4) * 2 + lax.rem(zh + k % 2, 2)

    def yz_from(k):
        return lax.rem(y + 4 - k // 2, 4) * 2 + lax.rem(zh + k % 2, 2)

    zpeer = at_dp(0, 1)
    sibling = at_mp(0, 1)
    dp_offs = [(k % 4, k // 4) for k in (6, 2, 5, 7, 1, 3, 4)]
    mp_offs = [5, 4, 3, 7, 2, 6, 1]
    mp15 = [(k, 1) for k in [*mp_offs, 0]] + [(k, 0) for k in mp_offs]

    def rc(src, dst, ss, rs, dev):
        return pltpu.make_async_remote_copy(
            src_ref=src, dst_ref=dst, send_sem=ss, recv_sem=rs, device_id=dev, device_id_type=MESH
        )

    def load_w(i):
        return pltpu.make_async_copy(w_ref.at[pl.ds(i * ROWS, ROWS)], stage.at[i], stage_sem.at[i])

    def load_e(i):
        slot = lax.rem(i, 4)
        return pltpu.make_async_copy(
            e_ref.at[pl.ds(i * ROWS, ROWS)], stage.at[slot], stage_sem.at[slot]
        )

    for i in range(4):
        load_w(i).start()

    barrier = pltpu.get_barrier_semaphore()
    for o in dp_offs:
        pl.semaphore_signal(barrier, inc=1, device_id=at_dp(*o), device_id_type=MESH)
    for k, dc in mp15:
        pl.semaphore_signal(barrier, inc=1, device_id=at_mp(k, dc), device_id_type=MESH)
    pl.semaphore_wait(barrier, len(dp_offs) + len(mp15))

    def tok(p):
        return pl.ds(pl.multiple_of(p * TR, TR), TR)

    def send_hid(q, h):
        return rc(
            hid_ref.at[pl.ds(h * TR, TR)], hid_all.at[h, tok(pos)],
            hid_ss.at[q, h], hid_rs.at[q, h], at_dp(*dp_offs[q]),
        )

    for h in (0, 1):
        for q in range(7):
            send_hid(q, h).start()
        hid_all[h, tok(pos), :] = hid_ref[h * TR : (h + 1) * TR, :]

    def relay(slot, out, first):
        def body(i, carry):
            r = pltpu.einshape("vjl->jvl", stage[slot, pl.ds(pl.multiple_of(i * 64, 64), 64)])
            s = pl.multiple_of(first + i * 64, 64)
            for j in range(16):
                at = ((j % 2) * 8 + j // 2) * FB
                out[pl.ds(s, 64), at : at + FB] = r[j]
            return carry

        lax.fori_loop(0, ROWS // 64, body, 0)

    def relay_e(i, carry):
        load_e(i).wait()
        relay(lax.rem(i, 4), e_flat, i * ROWS)

        @pl.when(i + 4 < V // ROWS)
        def _():
            load_e(i + 4).start()

        return carry

    for i in range(4):
        load_w(i).wait()
        relay(i, w_flat, i * ROWS)
        load_e(i).start()

    local_tgt = tgt_ref[...].astype(F32) - (mp * V).astype(F32)
    for i in range(4):
        part = jnp.broadcast_to(local_tgt[:, i * FB : (i + 1) * FB], (FB, FB)).T
        for j in (0, 1):
            block = i * 2 + j
            at = ((block % 4) * 2 + block // 4) * TR
            for h in (0, 1):
                first = j * 64 + h * TR
                tcol[h, at : at + TR, :] = part[first : first + TR, :]

    def zcol(i):
        return pl.ds(pl.multiple_of(i * CH, CH), ZW)

    def xcol(i):
        return pl.ds(pl.multiple_of(i * CH + ZW, FB), XW)

    for h in (0, 1):
        for i in (0, 1):
            ids = (lax.broadcasted_iota(jnp.int32, (TH, CH), 1) + i * CH).astype(F32)
            want = tcol[h, :, :1]
            lz[h * 2 + i] = (ids[:, :ZW] == want).astype(BF)
            lx[h * 2 + i] = (ids[:, ZW:] == want).astype(BF)

    def pick_body(n, carry):
        col = pl.ds(pl.multiple_of(n * 256, 256), 256)
        for h in (0, 1):
            r = jnp.zeros((TH, 256), F32)
            for i in (0, 1):
                r = r + dot(lz[h * 2 + i], e_flat[i * CH : i * CH + ZW, col], NN)
                r = r + dot(lx[h * 2 + i], e_flat[i * CH + ZW : (i + 1) * CH, col], NN)
            oh[h, :, col] = r.astype(BF)
        return carry

    lax.fori_loop(0, 8, relay_e, 0)

    def core_copy(h, ss, rs, t):
        two = pl.ds(t * 2, 2)
        return rc(ps.at[h, two], core_in.at[h, two], ss.at[h, t], rs.at[h, t], sibling)

    def mp_copy(h, ss, rs, k):
        return rc(ps2.at[h, yz_of(k)], mp_in.at[h, k], ss.at[h, k], rs.at[h, k], at_mp(k))

    def product(h, tile, css, crs, side):
        who = lax.rem(c + side, 2)

        def body(t, carry):
            first = who * 8 + t * 2
            r = tile(first, pl.ds(pl.multiple_of(first * FB, 2 * FB), 2 * FB))
            if side:
                ps[h, t * 2] = r[:, :FB].astype(BF)
                ps[h, t * 2 + 1] = r[:, FB:].astype(BF)
                core_copy(h, css, crs, t).start()
            else:
                acc[h, first] = r[:, :FB]
                acc[h, first + 1] = r[:, FB:]
            return carry

        lax.fori_loop(0, 4, body, 0)

    def encode(v, bound):
        root = lax.rsqrt(lax.rsqrt(jnp.abs(v) * (CODE**4 / bound)))
        code = (root + 0.5).astype(jnp.int32)
        return jnp.where(v < 0, -code, code).astype(jnp.int16)

    def decode(code, bound):
        root = code.astype(F32) * (1.0 / CODE)
        return root * jnp.abs(root) * (root * root) * bound

    def exchange(h, css, crs, mss, mrs, bound):
        for t in range(4):
            core_copy(h, css, crs, t).wait_recv()
        for k in mp_offs:
            b = yz_of(k)
            ps2[h, b] = encode(acc[h, c * 8 + b] + core_in[h, b].astype(F32), bound)
            mp_copy(h, mss, mrs, k).start()

    def collect(h, css, crs, mss, mrs, bound):
        total = acc[h, c * 8 + yz] + core_in[h, yz].astype(F32)
        for k in mp_offs:
            mp_copy(h, mss, mrs, k).wait_recv()
            total = total + decode(mp_in[h, k], bound)
        for k in mp_offs:
            mp_copy(h, mss, mrs, k).wait_send()
        for t in range(4):
            core_copy(h, css, crs, t).wait_send()
        return total

    for h in (0, 1):
        for q in range(7):
            send_hid(q, h).wait_recv()
        for side in (1, 0):
            product(h, lambda first, col, h=h: dot(hid_all[h], w_flat[:, col], NN), core_ss, core_rs, side)
        exchange(h, core_ss, core_rs, mp_ss, mp_rs, PRE_BOUND)

    lax.fori_loop(8, V // ROWS, relay_e, 0)
    lax.fori_loop(0, 2, pick_body, 0)

    gain = gain_ref[...]

    def cols(core, b):
        return pl.ds(pl.multiple_of((core * 8 + b) * FB, FB), FB)

    def ag_copy(buf, h, ss, rs, k):
        return rc(nb.at[h], buf.at[h, :, cols(c, yz)], ss.at[h, k], rs.at[h, k], at_mp(k))

    def ag_pass(buf, h, ss, rs, k):
        at = buf.at[h, :, cols(c, yz_from(k))]
        return rc(nb.at[h] if k == 0 else at, at, ss.at[h, k], rs.at[h, k], sibling)

    def gather_start(buf, h, ss, rs, css, crs):
        for k in mp_offs:
            ag_copy(buf, h, ss, rs, k).start()
        ag_pass(buf, h, css, crs, 0).start()
        buf[h, :, cols(c, yz)] = nb[h]

    def gather_mid(buf, h, ss, rs, css, crs):
        for k in reversed(mp_offs):
            ag_copy(buf, h, ss, rs, k).wait_recv()
            ag_pass(buf, h, css, crs, k).start()

    def gather_end(buf, h, ss, rs, css, crs):
        for k in range(8):
            ag_pass(buf, h, css, crs, k).wait_recv()
        for k in range(8):
            ag_pass(buf, h, css, crs, k).wait_send()
        for k in mp_offs:
            ag_copy(buf, h, ss, rs, k).wait_send()

    nf_sems = (nf_ss, nf_rs, nfc_ss, nfc_rs)
    dp_sems = (dp_ss, dp_rs, dpc_ss, dpc_rs)

    def activate(h):
        pre = collect(h, core_ss, core_rs, mp_ss, mp_rs, PRE_BOUND)
        pre_s[h] = pre
        own = hid_all[h, :, pl.ds(pl.multiple_of(dp * FB, FB), FB)].astype(F32)
        act = own + pre / (1.0 + jnp.exp(-pre))
        act_s[h] = act
        nb[h] = (act * gain).astype(BF)
        gather_start(nf, h, *nf_sems)
        squares = act * act
        for i in (0, 1):
            row = jnp.sum(squares[i * FB : (i + 1) * FB, :].T, axis=0, keepdims=True)
            at = h * TH + i * FB
            sq_own[:, at : at + FB] = jnp.broadcast_to(row, (8, FB))

    def send_sq(q):
        k, dc = mp15[q]
        return rc(sq_own, sq_in.at[mp], sq_ss.at[q], sq_rs.at[q], at_mp(k, dc))

    activate(0)
    lax.fori_loop(2, 4, pick_body, 0)
    activate(1)
    for q in range(15):
        send_sq(q).start()
    sq_in[mp] = sq_own[...]
    lax.fori_loop(4, 6, pick_body, 0)
    gather_mid(nf, 0, *nf_sems)
    lax.fori_loop(6, 8, pick_body, 0)
    gather_end(nf, 0, *nf_sems)

    def rows_of(xx, zz):
        return tok(xx * 2 + zz)

    def xd(d):
        return lax.rem(x + d, 4)

    def rz_copy(g, d):
        return rc(
            lz.at[g, rows_of(xd(d), 1 - zl)], rz.at[g, d], rz_ss.at[g, d], rz_rs.at[g, d], zpeer
        )

    def way(k):
        return at_dp(1 if k == 0 else 3, 0)

    def to(k):
        return xd(1 if k == 0 else 3)

    def source(k):
        return xd(3 if k == 0 else 1)

    def block(xx, half):
        return pl.ds(pl.multiple_of(xx * 2 * TR + half * TR, TR), TR)

    def part(half):
        return pl.ds(half * (TR // 2), TR // 2)

    def pair(ss, rs, g, k):
        return (ss.at[g, k], rs.at[g, k], way(k))

    def rxf_copy(g, k):
        return rc(lx.at[g, block(xd(2), k)], rxf.at[g, k], *pair(rxf_ss, rxf_rs, g, k))

    def rxn_copy(g, k):
        here = pl.ds((1 - k) * TR, TR)
        return rc(lx.at[g, block(to(k), 1 - k)], rx.at[g, k, here], *pair(rxn_ss, rxn_rs, g, k))

    def rxc_copy(g, k):
        return rc(sxc.at[g, k], rx.at[g, k, pl.ds(k * TR, TR)], *pair(rxc_ss, rxc_rs, g, k))

    def rx2_copy(g):
        return rc(sx2.at[g], rx2.at[g], rx2_ss.at[g], rx2_rs.at[g], zpeer)

    def rzf_copy(g, k):
        return rc(szf.at[g, part(k)], rzf.at[g, k], *pair(rzf_ss, rzf_rs, g, k))

    def rzn_copy(g, k):
        return rc(szn.at[g, k], rz2.at[g, k, part(1 - k)], *pair(rzn_ss, rzn_rs, g, k))

    def rzc_copy(g, k):
        return rc(szc.at[g, k], rz2.at[g, k, part(k)], *pair(rzc_ss, rzc_rs, g, k))

    def logits_chunk(g):
        h, i = g // 2, g % 2
        lx[g] = dot(nf[h], e_flat[i * CH + ZW : (i + 1) * CH, :], NT).astype(BF)
        for k in (0, 1):
            rxf_copy(g, k).start()
        for k in (0, 1):
            rxn_copy(g, k).start()
        lz[g] = dot(nf[h], e_flat[i * CH : i * CH + ZW, :], NT).astype(BF)
        for d in (2, 1, 3, 0):
            rz_copy(g, d).start()

    def combine_x(g):
        for k in (0, 1):
            rxf_copy(g, k).wait_recv()
            sxc[g, k] = (lx[g, block(to(k), k)].astype(F32) + rxf[g, k].astype(F32)).astype(BF)
            rxc_copy(g, k).start()

    def z_sum(g, d, rows):
        first = pl.multiple_of((xd(d) * 2 + zl) * TR + rows[0], TR // 2)
        return lz[g, pl.ds(first, rows[1])].astype(F32) + rz[g, d, rows[0] : rows[0] + rows[1]].astype(F32)

    def second_step(g):
        h, i = g // 2, g % 2
        rz_copy(g, 2).wait_recv()
        szf[g] = z_sum(g, 2, (0, TR)).astype(BF)
        for k in (0, 1):
            rzf_copy(g, k).start()
        for k in (0, 1):
            d = 1 if k == 0 else 3
            rz_copy(g, d).wait_recv()
            szn[g, k] = z_sum(g, d, ((1 - k) * (TR // 2), TR // 2)).astype(BF)
            rzn_copy(g, k).start()
        rz_copy(g, 0).wait_recv()
        lg[h, :, zcol(i)] = z_sum(g, 0, (0, TR))
        for k in (0, 1):
            rxn_copy(g, k).wait_recv()
            rxc_copy(g, k).wait_recv()
        for mine in (False, True):
            zz = zl if mine else 1 - zl
            off = pl.multiple_of(zz * TR, TR)
            s = lx[g, block(x, zz)].astype(F32)
            for k in (0, 1):
                s = s + rx[g, k, pl.ds(off, TR)].astype(F32)
            if mine:
                lg[h, :, xcol(i)] = s
            else:
                sx2[g] = s.astype(BF)
                rx2_copy(g).start()

    def combine_z(g):
        for k in (0, 1):
            rzf_copy(g, k).wait_recv()
            own = z_sum(g, 1 if k == 0 else 3, (k * (TR // 2), TR // 2))
            szc[g, k] = (own + rzf[g, k].astype(F32)).astype(BF)
            rzc_copy(g, k).start()

    def rs_end(g):
        h, i = g // 2, g % 2
        rx2_copy(g).wait_recv()
        lg[h, :, xcol(i)] = lg[h, :, xcol(i)] + rx2[g].astype(F32)
        s = lg[h, :, zcol(i)]
        for k in (0, 1):
            rzn_copy(g, k).wait_recv()
            rzc_copy(g, k).wait_recv()
            s = s + rz2[g, k].astype(F32)
        lg[h, :, zcol(i)] = s

    def dl_at(h, xx, zz, col):
        return dl.at[h, rows_of(xx, zz), col]

    def half_at(h, xx, zz, k, col):
        first = pl.multiple_of((xx * 2 + zz) * TR + k * (TR // 2), TR // 2)
        return dl.at[h, pl.ds(first, TR // 2), col]

    def az_copy(g, k):
        a = dl_at(g // 2, x, zl, zcol(g % 2))
        return rc(a, a, *pair(az_ss, az_rs, g, k))

    def azh_copy(g, k):
        a = half_at(g // 2, source(k), zl, k, zcol(g % 2))
        return rc(a, a, *pair(azh_ss, azh_rs, g, k))

    def azz_copy(g):
        a = dl_at(g // 2, x, zl, zcol(g % 2))
        return rc(a, a, azz_ss.at[g], azz_rs.at[g], zpeer)

    def azf_copy(g, d):
        a = dl_at(g // 2, xd(d), zl, zcol(g % 2))
        return rc(a, a, azf_ss.at[g, d - 1], azf_rs.at[g, d - 1], zpeer)

    def ax_copy(g, k):
        a = dl_at(g // 2, x, zl, xcol(g % 2))
        return rc(a, a, *pair(ax_ss, ax_rs, g, k))

    def axh_copy(g, k):
        a = half_at(g // 2, source(k), zl, k, xcol(g % 2))
        return rc(a, a, *pair(axh_ss, axh_rs, g, k))

    def axz_copy(g):
        a = dl_at(g // 2, x, zl, xcol(g % 2))
        return rc(a, a, axz_ss.at[g], axz_rs.at[g], zpeer)

    def axf_copy(g, k):
        a = dl_at(g // 2, x, 1 - zl, xcol(g % 2))
        return rc(a, a, *pair(axf_ss, axf_rs, g, k))

    def axg_copy(g, k):
        a = half_at(g // 2, source(k), 1 - zl, k, xcol(g % 2))
        return rc(a, a, *pair(axg_ss, axg_rs, g, k))

    lane = lax.broadcasted_iota(jnp.int32, (TR, FB), 1)

    def send_st(h, q):
        k, dc = mp15[q]
        return rc(st_own.at[h], st_in.at[h, mp], st_ss.at[h, q], st_rs.at[h, q], at_mp(k, dc))

    def softmax(h):
        inv_own = inv_s[h, tok(pos), :][:, :1]
        want = tcol[h, tok(pos), :][:, :1]
        m = jnp.full((TR, 1), -jnp.inf, F32)
        spans = [(0, ZW), (ZW, XW), (CH, ZW), (CH + ZW, XW)]
        for at, wide in spans:
            v = lg[h, :, at : at + wide] * inv_own
            lg[h, :, at : at + wide] = v
            m = jnp.maximum(m, jnp.max(v, axis=1, keepdims=True))
        s, sl, pk = (jnp.zeros((TR, 1), F32) for _ in range(3))
        for j, (at, wide) in enumerate(spans):
            ids = (lax.broadcasted_iota(jnp.int32, (TR, wide), 1) + at).astype(F32)
            v = lg[h, :, at : at + wide]
            p = jnp.exp(v - m)
            dl[h, tok(pos), at : at + wide] = p.astype(BF)
            g = h * 2 + j // 2
            if j % 2:
                axz_copy(g).start()
                for k in (0, 1):
                    ax_copy(g, k).start()
            else:
                for k in (0, 1):
                    az_copy(g, k).start()
                azz_copy(g).start()
            s = s + jnp.sum(p, axis=1, keepdims=True)
            sl = sl + jnp.sum(p * v, axis=1, keepdims=True)
            pk = pk + jnp.sum(jnp.where(ids == want, v, 0.0), axis=1, keepdims=True)
        tsq[...] = jnp.zeros((FB, FB), F32)
        tsq[:TR, :] = jnp.where(
            lane == 0, m, jnp.where(lane == 1, s, jnp.where(lane == 2, sl, jnp.where(lane == 3, pk, 0.0)))
        )
        st_own[h] = tsq[...].T[:8, :]
        for q in range(15):
            send_st(h, q).start()
        st_in[h, mp] = st_own[h]

    def forward(g):
        axz_copy(g).wait_recv()
        for k in (0, 1):
            axf_copy(g, k).start()
        for k in (0, 1):
            az_copy(g, k).wait_recv()
            azh_copy(g, k).start()
            azf_copy(g, 3 if k == 0 else 1).start()
        for k in (0, 1):
            ax_copy(g, k).wait_recv()
            axh_copy(g, k).start()

    def forward_far(g):
        for k in (0, 1):
            axf_copy(g, k).wait_recv()
            axg_copy(g, k).start()
        for k in (0, 1):
            azh_copy(g, k).wait_recv()
        azf_copy(g, 2).start()

    def ag_end(g):
        azz_copy(g).wait_recv()
        for k in (0, 1):
            axh_copy(g, k).wait_recv()
            axg_copy(g, k).wait_recv()
        for d in (1, 2, 3):
            azf_copy(g, d).wait_recv()

    def send_sc(h, q):
        a = sc_all.at[h, pos]
        return rc(a, a, sc_ss.at[h, q], sc_rs.at[h, q], at_dp(*dp_offs[q]))

    def statistics(h):
        for q in range(15):
            send_st(h, q).wait_recv()
        all_m = st_in[h, :, 0, :]
        top = jnp.max(all_m, axis=0, keepdims=True)
        scale = jnp.exp(all_m - top)
        total = jnp.sum(st_in[h, :, 1, :] * scale, axis=0, keepdims=True)
        total_l = jnp.sum(st_in[h, :, 2, :] * scale, axis=0, keepdims=True)
        picked = jnp.sum(st_in[h, :, 3, :], axis=0, keepdims=True)
        valid = lax.broadcasted_iota(jnp.int32, (1, FB), 1) < TR
        total = jnp.where(valid, total, 1.0)
        lse = top + jnp.log(total)
        moment = (total_l / total - picked) / T
        factor = jnp.exp(st_own[h, :1, :] - lse) / T
        sub = lax.broadcasted_iota(jnp.int32, (FB, FB), 0)
        table = jnp.where(sub == 0, factor, jnp.where(sub == 1, moment, jnp.where(sub == 2, lse - picked, 0.0)))
        tsq[...] = table.T
        sc_all[h, pos] = tsq[:TR, :]
        for q in range(7):
            send_sc(h, q).start()

    def factors(h):
        for q in range(7):
            send_sc(h, q).wait_recv()
        for b in range(8):
            ct[h, b * TR : (b + 1) * TR, :] = jnp.broadcast_to(sc_all[h, b][:, 0:1], (TR, FB))

    def scaled_tile(h, first, col, r):
        f = ct[h]
        own_row = oh[h, :, col].astype(F32) / T
        return jnp.concatenate(
            [r[:, b * FB : (b + 1) * FB] * f - own_row[:, b * FB : (b + 1) * FB] for b in (0, 1)], axis=1
        )

    def early_part(h):
        def body(t, carry):
            r = dot(dl[h, :, :CH], e_flat[:CH, pl.ds(pl.multiple_of(t * 256, 256), 256)], NN)
            acc[h, t * 2] = r[:, :FB]
            acc[h, t * 2 + 1] = r[:, FB:]
            return carry

        lax.fori_loop(0, 8, body, 0)

    def late_tile(h):
        def tile(first, col):
            r = dot(dl[h, :, CH:], e_flat[CH:, col], NN)
            return scaled_tile(h, first, col, r + jnp.concatenate([acc[h, first], acc[h, first + 1]], axis=1))

        return tile

    def whole_tile(h):
        return lambda first, col: scaled_tile(h, first, col, dot(dl[h], e_flat[:, col], NN))

    def pre_gradient(h):
        dnormed = collect(h, core2_ss, core2_rs, mp2_ss, mp2_rs, GRAD_BOUND)
        moments = jnp.concatenate([sc_all[h, b][:, 1:2] for b in range(8)], axis=0)
        inv, act, pre = inv_s[h], act_s[h], pre_s[h]
        dact = inv * gain * dnormed - act * (inv * inv * (moments / D))
        sig = 1.0 / (1.0 + jnp.exp(-pre))
        nb[h] = (dact * sig * (1.0 + pre * (1.0 - sig))).astype(BF)
        gather_start(dpf, h, *dp_sems)

    def send_sq2(q):
        return rc(sq_sum, sq_in2.at[dp], sq2_ss.at[q], sq2_rs.at[q], at_dp(*dp_offs[q]))

    def send_squares():
        for q in range(15):
            send_sq(q).wait_recv()
        sq_sum[...] = jnp.sum(sq_in[...], axis=0)
        for q in range(7):
            send_sq2(q).start()
        sq_in2[dp] = sq_sum[...]

    def norms():
        for q in range(7):
            send_sq2(q).wait_recv()
        mean = jnp.sum(sq_in2[...], axis=0)[:1, :] / D
        inv_row = lax.rsqrt(mean + 1e-05)
        for h in (0, 1):
            for i in (0, 1):
                at = h * TH + i * FB
                inv_s[h, i * FB : (i + 1) * FB, :] = jnp.broadcast_to(inv_row[:, at : at + FB], (FB, FB)).T

    logits_chunk(0)
    logits_chunk(1)
    gather_mid(nf, 1, *nf_sems)
    combine_x(0)
    send_squares()
    gather_end(nf, 1, *nf_sems)
    logits_chunk(2)
    combine_x(1)
    second_step(0)
    logits_chunk(3)
    combine_x(2)
    second_step(1)
    combine_z(0)
    norms()
    combine_x(3)
    second_step(2)
    combine_z(1)
    rs_end(0)
    rs_end(1)
    softmax(0)
    second_step(3)
    combine_z(2)
    combine_z(3)
    forward(0)
    forward(1)
    rs_end(2)
    rs_end(3)
    softmax(1)
    forward_far(0)
    forward_far(1)
    statistics(0)
    ag_end(0)
    ag_end(1)
    forward(2)
    factors(0)
    product(0, whole_tile(0), core2_ss, core2_rs, 1)
    forward(3)
    forward_far(2)
    product(0, whole_tile(0), core2_ss, core2_rs, 0)
    forward_far(3)
    exchange(0, core2_ss, core2_rs, mp2_ss, mp2_rs, GRAD_BOUND)
    statistics(1)
    ag_end(2)
    early_part(1)
    pre_gradient(0)
    factors(1)
    ag_end(3)
    product(1, late_tile(1), core2_ss, core2_rs, 1)
    product(1, late_tile(1), core2_ss, core2_rs, 0)
    exchange(1, core2_ss, core2_rs, mp2_ss, mp2_rs, GRAD_BOUND)
    for h in (0, 1):
        for i in range(8):
            hid_t[i * FB : (i + 1) * FB, h * TH : (h + 1) * TH] = hid_all[h, :, i * FB : (i + 1) * FB].T
    loss = jnp.zeros((TR, 1), F32)
    for h in (0, 1):
        for b in range(8):
            loss = loss + sc_all[h, b][:, 2:3]
    loss_ref[...] = jnp.sum(loss, axis=0, keepdims=True) / T
    gather_mid(dpf, 0, *dp_sems)
    pre_gradient(1)
    gather_end(dpf, 0, *dp_sems)

    def grad_copy(n, col):
        return pltpu.make_async_copy(w_flat.at[:, col], grad_ref.at[:, col], out_sem.at[n])

    def grad_tile(n, core, dy):
        first = core * 8 + lax.rem(y + 4 - dy, 4) * 2
        col = pl.ds(pl.multiple_of(first * FB, 2 * FB), 2 * FB)
        r = dot(hid_t[:, :TH], dpf[0, :, col], NN) + dot(hid_t[:, TH:], dpf[1, :, col], NN)
        w_flat[:, col] = r.astype(BF)
        grad_copy(n, col).start()
        return n, col

    tiles = []
    for dy in (0, 1, 3, 2):
        for k in (dy * 2, dy * 2 + 1):
            if k:
                ag_copy(dpf, 1, dp_ss, dp_rs, k).wait_recv()
                ag_pass(dpf, 1, dpc_ss, dpc_rs, k).start()
        tiles.append(grad_tile(len(tiles), c, dy))
    for dy in (0, 1, 3, 2):
        for k in (dy * 2, dy * 2 + 1):
            ag_pass(dpf, 1, dpc_ss, dpc_rs, k).wait_recv()
        tiles.append(grad_tile(len(tiles), 1 - c, dy))
    for k in range(8):
        ag_pass(dpf, 1, dpc_ss, dpc_rs, k).wait_send()
    for k in mp_offs:
        ag_copy(dpf, 1, dp_ss, dp_rs, k).wait_send()

    for q in range(7):
        send_sq2(q).wait_send()
        for h in (0, 1):
            send_hid(q, h).wait_send()
            send_sc(h, q).wait_send()
    for q in range(15):
        send_sq(q).wait_send()
        for h in (0, 1):
            send_st(h, q).wait_send()

    def drain(g, carry):
        rx2_copy(g).wait_send()
        azz_copy(g).wait_send()
        axz_copy(g).wait_send()
        for d in range(4):
            rz_copy(g, d).wait_send()
        for d in (1, 2, 3):
            azf_copy(g, d).wait_send()
        for k in (0, 1):
            rxf_copy(g, k).wait_send()
            rxn_copy(g, k).wait_send()
            rxc_copy(g, k).wait_send()
            rzf_copy(g, k).wait_send()
            rzn_copy(g, k).wait_send()
            rzc_copy(g, k).wait_send()
            az_copy(g, k).wait_send()
            azh_copy(g, k).wait_send()
            ax_copy(g, k).wait_send()
            axh_copy(g, k).wait_send()
            axf_copy(g, k).wait_send()
            axg_copy(g, k).wait_send()
        return carry

    lax.fori_loop(0, NG, drain, 0)
    for n, col in tiles:
        grad_copy(n, col).wait()


def head(hidden, weight, gain, embed, targets):
    vm = pltpu.VMEM
    dma = pltpu.SemaphoreType.DMA
    scratch = [
        vm((V, 2048), BF), vm((1024, 2048), BF), vm((4, ROWS, 16, FB), BF), vm((2, TH, 1024), BF), vm((1024, T), BF),
        vm((2, 8, TH, FB), BF), vm((2, 16, TH, FB), F32), vm((2, 8, TH, FB), BF), vm((2, 8, TH, FB), jnp.int16),
        vm((2, 8, TH, FB), jnp.int16), vm((2, TH, 2048), BF), vm((2, TH, FB), F32), vm((2, TH, FB), F32),
        vm((2, TH, FB), F32), vm((2, TH, FB), F32), vm((2, TH, FB), BF), vm((2, TH, 2048), BF), vm((2, TH, 2048), BF),
        vm((8, T), F32), vm((16, 8, T), F32), vm((8, T), F32), vm((8, 8, T), F32), vm((2, TH, FB), F32),
        vm((NG, TH, ZW), BF), vm((NG, TH, XW), BF),
        vm((NG, 2, 2 * TR, XW), BF), vm((NG, 2, TR, XW), BF), vm((NG, 2, TR, XW), BF), vm((NG, 4, TR, ZW), BF),
        vm((NG, TR, XW), BF), vm((NG, TR, XW), BF), vm((NG, TR, ZW), BF), vm((NG, 2, TR // 2, ZW), BF),
        vm((NG, 2, TR // 2, ZW), BF), vm((NG, 2, TR // 2, ZW), BF), vm((NG, 2, TR, ZW), BF),
        vm((2, TR, V), F32), vm((FB, FB), F32), vm((2, 8, FB), F32), vm((2, 16, 8, FB), F32),
        vm((2, 8, TR, FB), F32), vm((2, TH, V), BF),
        dma((4,)), dma((8,)),
    ]
    counts = [
        (7, 2), (2, 4), (2, 8), (2, 4), (2, 8), (2, 8), (2, 8), (2, 8), (2, 8), (15,), (7,), (2, 15), (2, 7),
        (NG, 2), (NG, 2), (NG, 2), (NG, 4), (NG,), (NG, 2), (NG, 2), (NG, 2),
        (NG, 2), (NG, 2), (NG,), (NG, 3), (NG, 2), (NG, 2), (NG,), (NG, 2), (NG, 2),
    ]
    for n in counts:
        scratch += [dma(n), dma(n)]
    vspec = pl.BlockSpec(memory_space=pltpu.VMEM)
    anyspec = pl.BlockSpec(memory_space=pl.ANY)
    return pl.pallas_call(
        head_kernel,
        name="head",
        out_shape=(jax.ShapeDtypeStruct((1024, 2048), BF), jax.ShapeDtypeStruct((1, 1), F32)),
        in_specs=[vspec, anyspec, vspec, anyspec, vspec],
        out_specs=(anyspec, vspec),
        scratch_shapes=scratch,
        compiler_params=pltpu.CompilerParams(
            collective_id=0, has_side_effects=True, vmem_limit_bytes=62 << 20
        ),
    )(hidden, weight, gain, embed, targets)


def order_kernel(grad, out):
    blocks = jnp.stack([grad[:, ((j % 2) * 8 + j // 2) * FB :][:, :FB] for j in range(16)])
    out[...] = pltpu.einshape("jvl->vjl", blocks)


def in_order(grad):
    rows = 512
    return pl.pallas_call(
        order_kernel,
        name="in_order",
        grid=(1024 // rows,),
        out_shape=jax.ShapeDtypeStruct((1024, 16, FB), BF),
        in_specs=[pl.BlockSpec((rows, 2048), lambda i: (i, 0))],
        out_specs=pl.BlockSpec((rows, 16, FB), lambda i: (i, 0, 0)),
        compiler_params=pltpu.CompilerParams(vmem_limit_bytes=62 << 20),
    )(grad)


def on_device(hidden_rows, head_weight, norm_gain, vocab_embed, targets):
    grad, loss = head(
        hidden_rows,
        head_weight.reshape(1024, 16, FB),
        norm_gain.reshape(1, FB),
        vocab_embed.reshape(V, 16, FB),
        targets.reshape(1, T),
    )
    return in_order(grad).reshape(head_weight.shape), loss.reshape(())


def solution(mesh):
    return jax.shard_map(
        on_device,
        mesh=mesh,
        in_specs=(
            P("dp", "mp"),
            P("mp", None, "dp", None),
            P("mp", "dp", None),
            P("mp", None, "dp", None),
            P(),
        ),
        out_specs=(P("mp", None, "dp", None), P()),
        check_vma=False,
    )
```
